32 devices in a mesh: group: 2 (over core), tensor: 16 (over z, y, x).
Axes of the slice: x: 2, y: 2, z: 4, core: 2. Of those that a mesh axis runs over, the one named last changes fastest.
Arguments:
- hidden_in: bfloat16 [2048, 2048], P('tensor'), may hold values from -6 to 6
- queries: bfloat16 [2048, 3072], P('tensor', 'group'), may hold values from -10 to 10
- suffix_latent: bfloat16 [2048, 576], P('tensor'), may hold values from -10 to 10
- prefix_latent: bfloat16 [2048, 576], P(('group', 'tensor')), may hold values from -6 to 6
- key_up: bfloat16 [16, 128, 512], P('group'), may hold values from -0.5 to 0.5
- value_up: bfloat16 [16, 512, 128], P('group'), may hold values from -0.25 to 0.25
- output_weight: bfloat16 [2048, 2048], P('group'), may hold values from -0.125 to 0.125
- norm_gain: bfloat16 [2048], replicated, may hold values from 0.5 to 1.5
- router: bfloat16 [2048, 16], replicated, may hold values from -0.125 to 0.125
- expert_gate: bfloat16 [16, 2048, 1408], P('tensor', None, 'group'), may hold values from -0.125 to 0.125
- expert_up: bfloat16 [16, 2048, 1408], P('tensor', None, 'group'), may hold values from -0.125 to 0.125
- expert_down: bfloat16 [16, 1408, 2048], P('tensor', 'group'), may hold values from -0.15625 to 0.15625
- next_gain: bfloat16 [2048], replicated, may hold values from 0.5 to 1.5
- next_query_weight: bfloat16 [2048, 3072], P(None, 'group'), may hold values from -0.125 to 0.125
- next_latent_weight: bfloat16 [2048, 576], P(None, 'group'), may hold values from -0.125 to 0.125
- suffix_lengths: int32 [8], replicated, may hold values from 1 to 513, 2048 in all
- request_tenant: int32 [8], replicated, may hold values from 0 to 3
- tenant_lengths: int32 [4], replicated, may hold values from 1 to 1024, 2048 in all
- page_table: int32 [256], replicated, may hold values from 0 to 255, each once
- routes: int32 [2, 1024, 6], P(None, 'tensor'), may hold values from 0 to 15, all different within a row; in each aligned block of 64 rows (0 to 63, 64 to 127, ..., all dimensions but the last counted through in order) at most 32 rows name the same one
Outputs:
- layer_out: bfloat16 [1024, 2, 2048], P('tensor', 'group')
- next_queries: bfloat16 [2048, 3072], P('tensor', 'group')
- next_latent: bfloat16 [2048, 576], P('tensor', 'group')
The draws below stay inside these ranges and needn't reach their ends.
Inputs may be any that keep to these rules, and one draw needn't show every extreme that they name: `page_table`: each stored page maps to a different logical page. In each aligned block of 64 rows of routes (in its order g, a) an expert is named by at most 32 rows, and some block reaches 32; the 6 experts of a token differ.
All inputs are finite; a program needn't handle non-finite values.
Results may differ from the reference program's by a relative error of at most 0.018.
Values may be sent and summed in bfloat16 or wider, within the bound.
No kernel may reach another device: no remote copies, remote signals or barrier semaphores. Data moves between devices by JAX's collectives and lax.ppermute only.
A program may use at most 128 MiB of HBM per device.

```python
import math
import jax
import jax.numpy as jnp
import numpy as np
from jax import lax

D = 2048
HEADS = 16
NOPE = 128
ROPE = 64
VD = 128
LAT = 512
FF_E = 1408
TOP = 6
EXPERTS = 16
TOK_T = 128
TOKENS = 2048
TOK_Q = 64
PREFIX = 2048
PAGE = 8
PAGES = 256
TENANTS = 4
REACH = 4
MAXLEN = 513
REQS = 8
CAP = 32
N_GROUP = 2
N_TENSOR = 16


def draw_queries(key, part):
    base_key = jax.random.fold_in(key, 101)
    values = jnp.clip(2.0 * jax.random.normal(base_key, (TOKENS, HEADS, NOPE + ROPE), jnp.float32), -8.0, 8.0)
    return values.reshape(TOKENS, HEADS * (NOPE + ROPE)).astype(jnp.bfloat16)


def draw_suffix_latent(key, part):
    base_key = jax.random.fold_in(key, 202)
    values = jnp.clip(jax.random.normal(base_key, (TOKENS, LAT + ROPE), jnp.float32), -6.0, 6.0)
    return values.astype(jnp.bfloat16)


def set_ends(array, rng, low, top_value):
    spot = [jax.random.randint(jax.random.fold_in(rng, axis), (), 0, length) for axis, length in enumerate(array.shape)]
    widest = array.shape.index(max(array.shape))
    next_to = spot[:widest] + [(spot[widest] + 1) % array.shape[widest]] + spot[widest + 1:]
    return array.at[tuple(spot)].set(low).at[tuple(next_to)].set(top_value)


def steps_of(key, shape, split, low, largest):
    level = 1.0
    for position, parts in split:
        heights = jax.random.uniform(jax.random.fold_in(jax.random.fold_in(key, 6), position), (parts,), jnp.float32, low / len(split), largest / len(split))
        level = level * jnp.repeat(jnp.exp(heights), shape[position] // parts).reshape((-1,) + (1,) * (len(shape) - 1 - position))
    return level


def split_up(count, total, bound, lean):
    portions = [(1 << 20) // math.isqrt(rank ** lean) + 1 for rank in range(2, count + 1)]
    surplus, counts = total - bound - (count - 1), [1] * (count - 1)
    while surplus > 0:
        free = [i for i in range(count - 1) if counts[i] < bound]
        pool, budget = sum([portions[i] for i in free]), surplus
        for i in free:
            extra = min(bound - counts[i], max(1, budget * portions[i] // pool), surplus)
            counts[i] = counts[i] + extra
            surplus = surplus - extra
    return np.array([bound] + counts)


def uneven_parts(own_key, amount, total, limit, slope):
    if amount == 2:
        one = jax.random.randint(own_key, (), max(1, total - limit), min(limit, total - 1) + 1)
        return jnp.stack([one, total - one])
    tallies = jnp.asarray(split_up(amount, total, limit, slope), jnp.int32)
    pairs = (amount - 1) // 2
    donor, receiver = tallies[1:1 + 2 * pairs:2], tallies[2:2 + 2 * pairs:2]
    slack = jnp.minimum(donor - 1, limit - receiver)
    moved = jax.random.randint(jax.random.fold_in(own_key, 1), (pairs,), 0, 1 << 20) % (slack + 1)
    tallies = tallies.at[1:1 + 2 * pairs:2].set(donor - moved).at[2:2 + 2 * pairs:2].set(receiver + moved)
    return tallies[jax.random.permutation(jax.random.fold_in(own_key, 2), amount)]


def deal_out(stream_key, own, number, rows, amount, top, reach, skew):
    order = jax.random.permutation(stream_key, amount)
    crowded, usual = shares(amount, rows * top, reach, skew, True), shares(amount, rows * top, reach, skew, False)
    places = jnp.arange(amount)

    def named(lengths, turn):
        used = int((lengths > 0).sum())
        fixed = max(1, used // 4)
        shifted = fixed + (places - fixed + turn * (used - fixed)) % max(1, amount - fixed)
        return jnp.zeros((amount,), jnp.int32).at[order[jnp.where(places < fixed, places, shifted)]].set(jnp.asarray(lengths, jnp.int32))

    lengths = jnp.where(number % 4 == 0, named(crowded, number // 4), named(usual, number - number // 4 - 1))
    mixed = jax.random.permutation(jax.random.fold_in(own, 3), amount)
    donor, receiver = mixed[0:amount // 2 * 2:2], mixed[1:amount // 2 * 2:2]
    room = jnp.minimum(lengths[donor] - 1, reach - lengths[receiver]) // 2
    room = jnp.where((donor == order[0]) | (receiver == order[0]) | (lengths[receiver] == 0), 0, jnp.maximum(room, 0))
    shifted = jax.random.randint(jax.random.fold_in(own, 4), (amount // 2,), 0, 1 << 20) % (room + 1)
    lengths = lengths.at[donor].add(-shifted).at[receiver].add(shifted)
    items = jnp.searchsorted(jnp.cumsum(lengths), jnp.arange(rows * top), side="right").astype(jnp.int32)
    listing = items.reshape(top, rows).T
    listing = listing[jax.random.permutation(jax.random.fold_in(own, 1), rows)]
    turn = jax.random.randint(jax.random.fold_in(own, 2), (rows, 1), 0, top)
    return jnp.take_along_axis(listing, (jnp.arange(top)[None, :] + turn) % top, axis=1)


def shares(amount, total, limit, skew, full):
    weights = [(1 << 20) // math.isqrt(grade ** skew) + 1 for grade in range(1, amount + 1)]
    largest = limit if full else min(limit, max(-(-total // amount), total * weights[0] // sum(weights)))
    least = 1 if total - largest >= amount - 1 else 0
    counts, spare = [largest] + [least] * (amount - 1), total - largest - least * (amount - 1)
    while spare > 0:
        movable = [i for i in range(1, amount) if counts[i] < largest] or [i for i in range(1, amount) if counts[i] < limit]
        mass, left = sum([weights[i] for i in movable]), spare
        for i in movable:
            more = min(limit - counts[i], max(1, left * weights[i] // mass), spare)
            counts[i] = counts[i] + more
            spare = spare - more
    return np.array(counts)


def normal_values(stream_key, extent, width, reach, pieces=(), kind=jnp.bfloat16):
    result = jax.random.normal(stream_key, extent, jnp.float32) * width
    if len(pieces) > 0:
        result = steps_of(stream_key, extent, pieces, -0.22, 0.18) * result
    return jnp.clip(result, min=-reach, max=reach).astype(kind)


def setup_inputs(seed: int = 0) -> dict:
    keys = jax.random.split(jax.random.key(seed), 21)
    hidden_in = normal_values(keys[0], (TOKENS, D), 1.0, 6.0, ((0, 16),))
    queries = draw_queries(jax.random.fold_in(keys[20], 71), 0)
    suffix_latent = draw_suffix_latent(jax.random.fold_in(keys[20], 71), 0)
    prefix_latent = normal_values(keys[3], (PREFIX, LAT + ROPE), 1.0, 6.0, ((0, 32),))
    key_up = normal_values(keys[4], (HEADS, NOPE, LAT), NOPE ** -0.5, 0.5, ((0, 2),))
    value_up = normal_values(keys[5], (HEADS, LAT, VD), LAT ** -0.5, 0.25, ((0, 2),))
    output_weight = normal_values(keys[6], (HEADS * VD, D), (HEADS * VD) ** -0.5, 0.125, ((0, 2),))
    norm_gain = jnp.clip(1.0 + 0.1 * jax.random.normal(keys[7], (D,), jnp.float32), 0.5, 1.5).astype(jnp.bfloat16)
    router = normal_values(keys[8], (D, EXPERTS), D ** -0.5, 0.125)
    expert_gate = normal_values(keys[9], (EXPERTS, D, FF_E), D ** -0.5, 0.125, ((0, 16), (2, 2)))
    expert_up = normal_values(keys[10], (EXPERTS, D, FF_E), D ** -0.5, 0.125, ((0, 16), (2, 2)))
    expert_down = normal_values(keys[11], (EXPERTS, FF_E, D), FF_E ** -0.5, 0.15625, ((0, 16), (1, 2)))
    next_gain = jnp.clip(1.0 + 0.1 * jax.random.normal(keys[12], (D,), jnp.float32), 0.5, 1.5).astype(jnp.bfloat16)
    next_query_weight = normal_values(keys[13], (D, HEADS * (NOPE + ROPE)), D ** -0.5, 0.125, ((1, 2),))
    next_latent_weight = normal_values(keys[14], (D, LAT + ROPE), D ** -0.5, 0.125, ((1, 2),))
    suffix_lengths = uneven_parts(keys[15], REQS, TOKENS, MAXLEN, 2).astype(jnp.int32)
    request_tenant = set_ends(jax.random.randint(keys[16], (REQS,), 0, TENANTS), jax.random.fold_in(keys[16], 1), 0, TENANTS - 1).astype(jnp.int32)
    tenant_lengths = uneven_parts(keys[17], TENANTS, PREFIX, PREFIX // 2, 1).astype(jnp.int32)
    page_table = jax.random.permutation(keys[18], PAGES).astype(jnp.int32)
    routes_keys = jax.random.split(jax.random.fold_in(keys[19], 1), N_GROUP * (TOKENS // N_GROUP) // TOK_Q)
    routes_turns = jax.random.permutation(jax.random.fold_in(keys[19], 3), N_GROUP * (TOKENS // N_GROUP) // TOK_Q)
    routes = jax.vmap(lambda own, number: deal_out(jax.random.fold_in(keys[19], 2), own, number, TOK_Q, EXPERTS, TOP, CAP, 1))(routes_keys, routes_turns).reshape((N_GROUP, TOKENS // N_GROUP, TOP))
    return {"hidden_in": hidden_in, "queries": queries, "suffix_latent": suffix_latent, "prefix_latent": prefix_latent, "key_up": key_up, "value_up": value_up, "output_weight": output_weight, "norm_gain": norm_gain, "router": router, "expert_gate": expert_gate, "expert_up": expert_up, "expert_down": expert_down, "next_gain": next_gain, "next_query_weight": next_query_weight, "next_latent_weight": next_latent_weight, "suffix_lengths": suffix_lengths, "request_tenant": request_tenant, "tenant_lengths": tenant_lengths, "page_table": page_table, "routes": routes}


VERY_NEGATIVE = -1e+30
ROUTE_SCALING = 2.446
NORM_EPSILON = 1e-06

def norm_rows(row_block, gain_vector):
    values = row_block.astype(jnp.float32)
    mean_square = lax.optimization_barrier(jnp.mean(values * values, axis=-1, keepdims=True))
    return (values * lax.rsqrt(mean_square + NORM_EPSILON) * gain_vector.astype(jnp.float32)).astype(jnp.bfloat16)

def reference(hidden_in, queries, suffix_latent, prefix_latent, key_up, value_up, output_weight, norm_gain, router, expert_gate, expert_up, expert_down, next_gain, next_query_weight, next_latent_weight, suffix_lengths, request_tenant, tenant_lengths, page_table, routes):
    token_ids = jnp.arange(TOKENS, dtype=jnp.int32)
    request_ends = jnp.cumsum(suffix_lengths).astype(jnp.int32)
    request_starts = (request_ends - suffix_lengths).astype(jnp.int32)
    request_of = lax.optimization_barrier(jnp.sum((token_ids[:, None] >= request_ends[None, :]).astype(jnp.int32), axis=1)).astype(jnp.int32)
    token_start = request_starts[request_of]
    token_tenant = request_tenant[request_of]
    tenant_ends = jnp.cumsum(tenant_lengths).astype(jnp.int32)
    tenant_starts = (tenant_ends - tenant_lengths).astype(jnp.int32)
    range_low = tenant_starts[token_tenant]
    range_high = tenant_ends[token_tenant]
    prefix_spots = jnp.arange(PREFIX, dtype=jnp.int32)
    logical = (page_table[prefix_spots // PAGE] * PAGE + prefix_spots % PAGE).astype(jnp.int32)
    padded_keys = jnp.concatenate([jnp.zeros((REACH * TOK_T, LAT + ROPE), jnp.bfloat16), suffix_latent], axis=0)
    score_scale = 1.0 / math.sqrt(NOPE + ROPE)

    def slice_attention(slice_index):
        first_token = (slice_index * TOK_T).astype(jnp.int32)
        query_block = lax.dynamic_slice_in_dim(queries, first_token, TOK_T, 0).reshape(TOK_T, HEADS, NOPE + ROPE)
        absorbed = jnp.einsum('thn,hnl->thl', query_block[:, :, :NOPE].astype(jnp.float32), key_up.astype(jnp.float32)).astype(jnp.bfloat16)
        query_full = jnp.concatenate([absorbed, query_block[:, :, NOPE:]], axis=-1)
        near_keys = lax.dynamic_slice_in_dim(padded_keys, first_token, (REACH + 1) * TOK_T, 0)
        key_rows = jnp.concatenate([prefix_latent, near_keys], axis=0)
        positions = lax.dynamic_slice_in_dim(token_ids, first_token, TOK_T, 0)
        block_start = lax.dynamic_slice_in_dim(token_start, first_token, TOK_T, 0)
        block_low = lax.dynamic_slice_in_dim(range_low, first_token, TOK_T, 0)
        block_high = lax.dynamic_slice_in_dim(range_high, first_token, TOK_T, 0)
        near_spots = first_token - REACH * TOK_T + jnp.arange((REACH + 1) * TOK_T, dtype=jnp.int32)
        near_visible = (near_spots[None, :] >= block_start[:, None]) & (near_spots[None, :] <= positions[:, None])
        far_visible = (logical[None, :] >= block_low[:, None]) & (logical[None, :] < block_high[:, None])
        visible = jnp.concatenate([far_visible, near_visible], axis=1)
        scores = jnp.einsum('thc,kc->thk', query_full.astype(jnp.float32), key_rows.astype(jnp.float32)) * score_scale
        masked = jnp.where(visible[:, None, :], scores, VERY_NEGATIVE)
        best_score = lax.optimization_barrier(jnp.max(masked, axis=-1, keepdims=True))
        weights = jnp.where(visible[:, None, :], jnp.exp(masked - best_score), 0.0)
        weight_sum = lax.optimization_barrier(jnp.sum(weights, axis=-1, keepdims=True))
        rounded = lax.optimization_barrier(weights.astype(jnp.bfloat16)).astype(jnp.float32)
        attended = jnp.einsum('thk,kl->thl', rounded, key_rows[:, :LAT].astype(jnp.float32)) / weight_sum
        latent_out = attended.astype(jnp.bfloat16)
        head_out = jnp.einsum('thl,hlv->thv', latent_out.astype(jnp.float32), value_up.astype(jnp.float32)).astype(jnp.bfloat16)
        return head_out.reshape(TOK_T, HEADS * VD)
    head_rows = lax.map(slice_attention, jnp.arange(N_TENSOR, dtype=jnp.int32)).reshape(TOKENS, HEADS * VD)
    attend_sum = jnp.dot(head_rows, output_weight, preferred_element_type=jnp.float32)
    residual = (hidden_in.astype(jnp.float32) + attend_sum).astype(jnp.bfloat16)
    normed = norm_rows(residual, norm_gain)
    route_ids = jnp.transpose(routes, (1, 0, 2)).reshape(TOKENS, TOP)
    probs = jax.nn.sigmoid(jnp.dot(normed, router, preferred_element_type=jnp.float32))
    picked = jnp.take_along_axis(probs, route_ids, axis=1)
    gate_weights = picked / lax.optimization_barrier(jnp.sum(picked, axis=1, keepdims=True)) * ROUTE_SCALING
    flat_ids = route_ids.reshape(-1)
    row_count = TOKENS * TOP
    hit_table = (flat_ids[:, None] == jnp.arange(EXPERTS, dtype=jnp.int32)[None, :]).astype(jnp.int32)
    rank_table = jnp.cumsum(hit_table, axis=0).astype(jnp.int32) - hit_table
    slot_index = lax.optimization_barrier(jnp.sum(rank_table * hit_table, axis=1)).astype(jnp.int32)
    most_rows = TOKENS // TOK_Q * CAP
    slot_rows = jnp.full((EXPERTS, most_rows), row_count, jnp.int32).at[flat_ids, slot_index].set(jnp.arange(row_count, dtype=jnp.int32))
    normed_padded = jnp.concatenate([normed, jnp.zeros((1, D), jnp.bfloat16)], axis=0)
    token_of_row = jnp.concatenate([jnp.arange(row_count, dtype=jnp.int32) // TOP, jnp.full((1,), TOKENS, jnp.int32)]).astype(jnp.int32)
    weight_of_row = jnp.concatenate([gate_weights.reshape(-1), jnp.zeros((1,), jnp.float32)])
    unit_share = FF_E // N_GROUP

    def expert_step(running, expert_index):
        rows_here = slot_rows[expert_index]
        tokens_here = token_of_row[rows_here]
        inputs = normed_padded[tokens_here]
        gate_vals = jnp.dot(inputs, expert_gate[expert_index], preferred_element_type=jnp.float32)
        up_vals = jnp.dot(inputs, expert_up[expert_index], preferred_element_type=jnp.float32)
        hidden_vals = (jax.nn.silu(gate_vals) * up_vals).astype(jnp.bfloat16)
        down_rows = expert_down[expert_index]
        combined = jnp.zeros((most_rows, D), jnp.float32)
        for quarter in range(N_GROUP):
            part_rows = jnp.dot(hidden_vals[:, quarter * unit_share:(quarter + 1) * unit_share], down_rows[quarter * unit_share:(quarter + 1) * unit_share], preferred_element_type=jnp.float32).astype(jnp.bfloat16)
            combined = combined + part_rows.astype(jnp.float32)
        running = running.at[tokens_here].add(weight_of_row[rows_here][:, None] * combined)
        return (running, None)
    moe_total, unused = lax.scan(expert_step, jnp.zeros((TOKENS + 1, D), jnp.float32), jnp.arange(EXPERTS, dtype=jnp.int32))
    layer_rows = (residual.astype(jnp.float32) + moe_total[:TOKENS]).astype(jnp.bfloat16)
    normed_next = norm_rows(layer_rows, next_gain)
    next_queries = jnp.dot(normed_next, next_query_weight, preferred_element_type=jnp.float32).astype(jnp.bfloat16)
    next_latent = jnp.dot(normed_next, next_latent_weight, preferred_element_type=jnp.float32).astype(jnp.bfloat16)
    return (layer_rows.reshape(TOKENS // N_GROUP, N_GROUP, D), next_queries, next_latent)
```

```python
import functools
import math

import jax
import jax.numpy as jnp
from jax import lax
from jax.experimental import pallas as pl
from jax.experimental.pallas import tpu as pltpu
from jax.sharding import PartitionSpec as P

NOPE = 128
ROPE = 64
LAT = 512
PAGE = 8
REACH = 4
PLANE = 4

VERY_NEGATIVE = -1e30
ROUTE_SCALING = 2.446
NORM_EPSILON = 1e-06


def ring_order(count):
    odd = list(range(1, count, 2))
    even = list(range(2, count, 2))
    return [0] + odd + even[::-1]


def send_ring(block, count):
    order = ring_order(count)
    after = {order[i]: order[(i + 1) % count] for i in range(count)}
    route = [
        (z * PLANE + p, after[z] * PLANE + p) for z in range(count) for p in range(PLANE)
    ]
    return lax.ppermute(block, "tensor", route)


def send_plane(block, distance):
    devices = range(lax.axis_size("tensor"))
    return lax.ppermute(block, "tensor", [(i, i ^ distance) for i in devices])


def send_group(block, distance):
    devices = range(lax.axis_size("group"))
    return lax.ppermute(block, "group", [(i, i ^ distance) for i in devices])


def send_later(block, distance):
    devices = range(lax.axis_size("tensor"))
    route = [(i - distance, i) for i in devices if i - distance in devices]
    return lax.ppermute(block, "tensor", route)


def norm_rows(row_block, gain_vector):
    values = row_block.astype(jnp.float32)
    mean_square = jnp.mean(values * values, axis=-1, keepdims=True)
    return (
        values * lax.rsqrt(mean_square + NORM_EPSILON) * gain_vector.astype(jnp.float32)
    ).astype(jnp.bfloat16)


def dot_t(left, right):
    return lax.dot_general(
        left, right, (((1,), (1,)), ((), ())), preferred_element_type=jnp.float32
    )


def dot_f(left, right):
    return jnp.dot(left, right, preferred_element_type=jnp.float32)


def attend_kernel(
    prefix_count,
    block_count,
    tok_quarter,
    token_ref,
    spot_ref,
    order_ref,
    query_ref,
    key_up_ref,
    value_up_ref,
    output_ref,
    *refs,
):
    key_refs = refs[:block_count]
    own_ref, other_ref, keys, bias, total = refs[block_count:]
    step = pl.program_id(0)
    tokens = query_ref.shape[0]
    pair = key_up_ref.shape[0]

    @pl.when(step == 0)
    def prepare():
        at = 0
        for ref in key_refs:
            rows = ref.shape[0]
            keys[at : at + rows, :] = ref[...]
            at += rows
        columns = token_ref[...]
        spots = spot_ref[...]
        low, high, start, here = (columns[:, i : i + 1] for i in range(4))
        far = spots[:, :prefix_count]
        near = spots[:, prefix_count:]
        bias[:, :prefix_count] = jnp.where((far >= low) & (far < high), 0.0, VERY_NEGATIVE)
        bias[:, prefix_count:] = jnp.where((near >= start) & (near <= here), 0.0, VERY_NEGATIVE)
        total[...] = jnp.zeros_like(total)

    queries = dot_f(order_ref[...], query_ref[...]).astype(jnp.bfloat16)
    size = NOPE + ROPE
    content = []
    rotated = []
    for h in range(pair):
        part = queries[:, h * size : (h + 1) * size]
        content.append(dot_f(part[:, :NOPE], key_up_ref[h]).astype(jnp.bfloat16))
        rotated.append(part[:, NOPE:])
    content = jnp.concatenate(content, axis=0)
    rotated = jnp.concatenate(rotated, axis=0)
    scores = dot_t(content, keys[:, :LAT]) + dot_t(rotated, keys[:, LAT:])
    masked = (scores.reshape(pair, tokens, -1) + bias[...][None]).reshape(pair * tokens, -1)
    best = jnp.max(masked, axis=-1, keepdims=True)
    factor = math.log2(math.e) / math.sqrt(NOPE + ROPE)
    weights = jnp.exp2((masked - best) * factor)
    weight_sum = jnp.sum(weights, axis=-1, keepdims=True)
    attended = dot_f(weights.astype(jnp.bfloat16), keys[:, :LAT]) / weight_sum
    attended = attended.astype(jnp.bfloat16)
    heads = [
        dot_f(attended[h * tokens : (h + 1) * tokens], value_up_ref[h]).astype(jnp.bfloat16)
        for h in range(pair)
    ]
    total[...] += dot_f(jnp.concatenate(heads, axis=1), output_ref[...])

    @pl.when(step == pl.num_programs(0) - 1)
    def finish():
        own_ref[...] = total[:tok_quarter, :]
        other_ref[...] = total[tok_quarter:, :].astype(jnp.bfloat16)


def attend(tokens_info, spots, order, queries, key_up, value_up, output_weight, blocks, tok_quarter):
    tokens = queries.shape[0]
    heads = key_up.shape[0]
    width = output_weight.shape[1]
    pair = 2
    key_count = sum(block.shape[0] for block in blocks)
    prefix_count = key_count - (REACH + 1) * tokens
    size = NOPE + ROPE

    def whole(array):
        return pl.BlockSpec(array.shape, lambda i: (0,) * array.ndim)

    flops = 2 * heads * tokens * key_count * (LAT + ROPE + LAT)
    return pl.pallas_call(
        functools.partial(attend_kernel, prefix_count, len(blocks), tok_quarter),
        grid=(heads // pair,),
        in_specs=[
            whole(tokens_info),
            whole(spots),
            whole(order),
            pl.BlockSpec((tokens, pair * size), lambda i: (0, i)),
            pl.BlockSpec((pair, NOPE, LAT), lambda i: (i, 0, 0)),
            pl.BlockSpec((pair, LAT, value_up.shape[2]), lambda i: (i, 0, 0)),
            pl.BlockSpec((pair * value_up.shape[2], width), lambda i: (i, 0)),
        ]
        + [whole(block) for block in blocks],
        out_specs=[
            pl.BlockSpec((tok_quarter, width), lambda i: (0, 0)),
            pl.BlockSpec((tokens - tok_quarter, width), lambda i: (0, 0)),
        ],
        out_shape=[
            jax.ShapeDtypeStruct((tok_quarter, width), jnp.float32),
            jax.ShapeDtypeStruct((tokens - tok_quarter, width), jnp.bfloat16),
        ],
        scratch_shapes=[
            pltpu.VMEM((key_count, LAT + ROPE), jnp.bfloat16),
            pltpu.VMEM((tokens, key_count), jnp.float32),
            pltpu.VMEM((tokens, width), jnp.float32),
        ],
        compiler_params=pltpu.CompilerParams(vmem_limit_bytes=40 * 1024 * 1024),
        cost_estimate=pl.CostEstimate(
            flops=flops, bytes_accessed=12_000_000, transcendentals=heads * tokens * key_count
        ),
        name="attend",
    )(tokens_info, spots, order, queries, key_up, value_up, output_weight, *blocks)


def expert_apply(rows, gate_part, up_part, down_part):
    gate_vals = dot_f(rows, gate_part)
    up_vals = dot_f(rows, up_part)
    hidden_vals = (jax.nn.silu(gate_vals) * up_vals).astype(jnp.bfloat16)
    return dot_f(hidden_vals, down_part)


def per_device(
    hidden_in,
    queries,
    suffix_latent,
    prefix_latent,
    key_up,
    value_up,
    output_weight,
    norm_gain,
    router,
    expert_gate,
    expert_up,
    expert_down,
    next_gain,
    next_query_weight,
    next_latent_weight,
    suffix_lengths,
    request_tenant,
    tenant_lengths,
    page_table,
    routes,
):
    tok_slice = hidden_in.shape[0]
    groups = lax.axis_size("group")
    ring = lax.axis_size("tensor") // PLANE
    group_index = lax.axis_index("group")
    tensor_index = lax.axis_index("tensor")
    ring_index = tensor_index // PLANE
    plane_index = tensor_index % PLANE
    tok_quarter = tok_slice // groups
    expert_count = router.shape[1]
    top_count = routes.shape[2]
    capacity = max(2, 4 * tok_quarter * top_count // (3 * expert_count))
    int32 = jnp.int32

    prefix_ring = [prefix_latent]
    routes_own = lax.dynamic_index_in_dim(routes, group_index, 0, keepdims=False)
    routes_ring = [routes_own]
    for _ in range(ring - 1):
        prefix_ring.append(send_ring(prefix_ring[-1], ring))
        routes_ring.append(send_ring(routes_ring[-1], ring))
    suffix_part = lax.dynamic_slice_in_dim(suffix_latent, group_index * tok_quarter, tok_quarter, 0)
    suffix_column = jnp.concatenate(
        [send_later(suffix_part, offset) for offset in range(1, REACH + 1)], axis=0
    )
    prefix_column = jnp.concatenate(prefix_ring, axis=0)
    prefix_plane = [prefix_column] + [send_plane(prefix_column, d) for d in range(1, PLANE)]
    blocks = []
    for j in range(groups):
        blocks += [send_group(block, j) if j else block for block in prefix_plane]
    for j in range(groups):
        blocks.append(send_group(suffix_column, j) if j else suffix_column)
    blocks.append(suffix_latent)

    order = ring_order(ring)
    place = sum(jnp.where(ring_index == z, i, 0) for i, z in enumerate(order))
    piece_rows = prefix_latent.shape[0]
    shape = (groups, PLANE, ring, piece_rows)
    j, d, k, r = (lax.broadcasted_iota(int32, shape, axis) for axis in range(4))
    turn = (place - k + ring) % ring
    source = sum(jnp.where(turn == i, z, 0) for i, z in enumerate(order))
    piece = ((group_index ^ j) * ring + source) * PLANE + (plane_index ^ d)
    spot = (piece * piece_rows + r).reshape(-1)
    page_hit = (spot // PAGE)[:, None] == jnp.arange(page_table.shape[0], dtype=int32)[None, :]
    logical = jnp.sum(jnp.where(page_hit, page_table[None, :], 0), axis=1) * PAGE + spot % PAGE
    shape = (groups, REACH, tok_quarter)
    j, o, r = (lax.broadcasted_iota(int32, shape, axis) for axis in range(3))
    earlier = (tensor_index - 1 - o) * tok_slice + (group_index ^ j) * tok_quarter + r
    first_token = tensor_index * tok_slice
    own_spots = first_token + jnp.arange(tok_slice, dtype=int32)
    spots = jnp.concatenate([logical, earlier.reshape(-1), own_spots])[None, :]

    row = jnp.arange(tok_slice, dtype=int32)
    local = (row % tok_quarter) * groups + (group_index ^ (row // tok_quarter))
    permutation = (local[:, None] == jnp.arange(tok_slice, dtype=int32)[None, :]).astype(
        jnp.bfloat16
    )
    positions = first_token + local
    requests = suffix_lengths.shape[0]
    tenants = tenant_lengths.shape[0]
    upto = jnp.arange(requests)[None, :] <= jnp.arange(requests)[:, None]
    request_ends = jnp.sum(jnp.where(upto, suffix_lengths[None, :], 0), axis=1)
    request_starts = request_ends - suffix_lengths
    inside = (positions[:, None] >= request_starts[None, :]) & (
        positions[:, None] < request_ends[None, :]
    )
    token_start = jnp.sum(jnp.where(inside, request_starts[None, :], 0), axis=1)
    token_tenant = jnp.sum(jnp.where(inside, request_tenant[None, :], 0), axis=1)
    upto = jnp.arange(tenants)[None, :] <= jnp.arange(tenants)[:, None]
    tenant_ends = jnp.sum(jnp.where(upto, tenant_lengths[None, :], 0), axis=1)
    tenant_starts = tenant_ends - tenant_lengths
    tenant_pick = token_tenant[:, None] == jnp.arange(tenants, dtype=int32)[None, :]
    range_low = jnp.sum(jnp.where(tenant_pick, tenant_starts[None, :], 0), axis=1)
    range_high = jnp.sum(jnp.where(tenant_pick, tenant_ends[None, :], 0), axis=1)
    tokens_info = jnp.stack([range_low, range_high, token_start, positions], axis=1)

    attend_own, attend_other = attend(
        tokens_info,
        spots,
        permutation,
        queries,
        key_up,
        value_up,
        output_weight,
        blocks,
        tok_quarter,
    )

    routes_all = jnp.stack(routes_ring)
    target = ring_index * PLANE + (plane_index ^ jnp.arange(PLANE, dtype=int32))
    hits = jnp.any(routes_all[:, :, :, None] == target[None, None, None, :], axis=2)
    below = (
        jnp.arange(tok_quarter)[None, :] < jnp.arange(tok_quarter)[:, None]
    ).astype(jnp.bfloat16)
    rank = jnp.einsum(
        "ij,kjd->kid", below, hits.astype(jnp.bfloat16), preferred_element_type=jnp.float32
    ).astype(int32)
    slots = jnp.arange(capacity, dtype=int32)
    taken = hits[:, :, :, None] & (rank[:, :, :, None] == slots)
    spread = taken.reshape(ring, tok_quarter, PLANE * capacity).astype(jnp.bfloat16)
    named = jnp.any(
        routes_all[:, :, :, None] == jnp.arange(expert_count, dtype=int32), axis=2
    ).astype(jnp.float32)
    aimed = (jnp.arange(expert_count, dtype=int32)[:, None] == target[None, :]).astype(jnp.float32)

    hidden_own = dot_f(permutation[:tok_quarter], hidden_in)
    attend_full = attend_own
    for j in range(1, groups):
        part = attend_other[(j - 1) * tok_quarter : j * tok_quarter]
        attend_full = attend_full + send_group(part, j).astype(jnp.float32)
    residual = (hidden_own + attend_full).astype(jnp.bfloat16)
    normed = norm_rows(residual, norm_gain)

    gate_part = expert_gate[0]
    up_part = expert_up[0]
    down_part = expert_down[0]
    rows_plane = PLANE * capacity
    block = normed
    sums = []
    for k in range(ring):
        if k:
            block = send_ring(block, ring)
        chosen = lax.dot_general(
            spread[k], block, (((0,), (0,)), ((), ())), preferred_element_type=jnp.float32
        ).astype(jnp.bfloat16)
        arrived = [
            send_plane(chosen[d * capacity : (d + 1) * capacity], d)
            if d
            else chosen[:capacity]
            for d in range(PLANE)
        ]
        rows = jnp.concatenate(arrived, axis=0)
        rows = jnp.concatenate(
            [send_group(rows, j) if j else rows for j in range(groups)], axis=0
        )
        partial = expert_apply(rows, gate_part, up_part, down_part)
        combined = partial[:rows_plane]
        for j in range(1, groups):
            part = partial[j * rows_plane : (j + 1) * rows_plane].astype(jnp.bfloat16)
            combined = combined + send_group(part, j).astype(jnp.float32)
        combined = combined.astype(jnp.bfloat16)
        returned = [
            send_plane(combined[d * capacity : (d + 1) * capacity], d)
            if d
            else combined[:capacity]
            for d in range(PLANE)
        ]
        returned = jnp.concatenate(returned, axis=0)
        probs = jax.nn.sigmoid(dot_f(block, router))
        picked = probs * named[k]
        gates = picked / jnp.sum(picked, axis=1, keepdims=True) * ROUTE_SCALING
        gates = jnp.sum(gates[:, :, None] * aimed[None, :, :], axis=1)
        scaled = spread[k].reshape(tok_quarter, PLANE, capacity) * gates[:, :, None].astype(
            jnp.bfloat16
        )
        sums.append(dot_f(scaled.reshape(tok_quarter, rows_plane), returned))
    running = None
    for k in range(1, ring):
        total = sums[k] if running is None else sums[k] + running
        running = send_ring(total.astype(jnp.bfloat16), ring).astype(jnp.float32)
    moe = sums[0] if running is None else sums[0] + running

    layer_rows = (residual.astype(jnp.float32) + moe).astype(jnp.bfloat16)
    normed_next = norm_rows(layer_rows, next_gain)
    shares = [send_group(normed_next, j) if j else normed_next for j in range(groups)]
    gathered = lax.dot_general(
        permutation,
        jnp.concatenate(shares, axis=0),
        (((0,), (0,)), ((), ())),
        preferred_element_type=jnp.float32,
    ).astype(jnp.bfloat16)
    next_queries = dot_f(gathered, next_query_weight).astype(jnp.bfloat16)
    next_latent = dot_f(gathered, next_latent_weight).astype(jnp.bfloat16)
    return (layer_rows[:, None, :], next_queries, next_latent)


def solution(mesh):
    return jax.shard_map(
        per_device,
        mesh=mesh,
        in_specs=(
            P("tensor", None),
            P("tensor", "group"),
            P("tensor", None),
            P(("group", "tensor"), None),
            P("group", None, None),
            P("group", None, None),
            P("group", None),
            P(),
            P(),
            P("tensor", None, "group"),
            P("tensor", None, "group"),
            P("tensor", "group", None),
            P(),
            P(None, "group"),
            P(None, "group"),
            P(),
            P(),
            P(),
            P(),
            P(None, "tensor", None),
        ),
        out_specs=(P("tensor", "group", None), P("tensor", "group"), P("tensor", "group")),
        check_vma=False,
    )
```

```python
import functools
import math

import jax
import jax.numpy as jnp
from jax import lax
from jax.experimental import pallas as pl
from jax.experimental.pallas import tpu as pltpu
from jax.sharding import PartitionSpec as P

NOPE = 128
ROPE = 64
LAT = 512
PAGE = 8
PLANE = 4
ROUTE_ROWS = 16

VERY_NEGATIVE = -1e30
ROUTE_SCALING = 2.446
NORM_EPSILON = 1e-06


def ring_order(count):
    odd = list(range(1, count, 2))
    even = list(range(2, count, 2))
    return [0] + odd + even[::-1]


def send_ring(block, count, steps=1):
    order = ring_order(count)
    after = {order[i]: order[(i + steps) % count] for i in range(count)}
    route = [
        (z * PLANE + p, after[z] * PLANE + p) for z in range(count) for p in range(PLANE)
    ]
    return lax.ppermute(block, "tensor", route)


def send_round(block, distance):
    count = lax.axis_size("tensor")
    return lax.ppermute(block, "tensor", [(i, (i + distance) % count) for i in range(count)])


def send_plane(block, distance):
    devices = range(lax.axis_size("tensor"))
    return lax.ppermute(block, "tensor", [(i, i ^ distance) for i in devices])


def send_group(block, distance):
    devices = range(lax.axis_size("group"))
    return lax.ppermute(block, "group", [(i, i ^ distance) for i in devices])


def norm_rows(row_block, gain_vector):
    values = row_block.astype(jnp.float32)
    mean_square = jnp.mean(values * values, axis=-1, keepdims=True)
    return (
        values * lax.rsqrt(mean_square + NORM_EPSILON) * gain_vector.astype(jnp.float32)
    ).astype(jnp.bfloat16)


def dot_t(left, right):
    return lax.dot_general(
        left, right, (((1,), (1,)), ((), ())), preferred_element_type=jnp.float32
    )


def dot_f(left, right):
    return jnp.dot(left, right, preferred_element_type=jnp.float32)


def whole(array):
    return pl.BlockSpec(array.shape, lambda *i: (0,) * len(array.shape))


def after(kernel, count):
    def inner(*refs):
        kernel(*refs[count:])

    return inner


def unread(arrays):
    return [pl.BlockSpec(memory_space=pl.ANY) for _ in arrays]


def call(kernel, name, inputs, outputs, flops, limit=12, ready=()):
    shapes = [jax.ShapeDtypeStruct(shape, dtype) for shape, dtype in outputs]
    moved = sum(a.size * a.dtype.itemsize for a in list(inputs) + shapes)
    return pl.pallas_call(
        after(kernel, len(ready)),
        grid=(1,),
        in_specs=unread(ready) + [whole(a) for a in inputs],
        out_specs=[whole(s) for s in shapes],
        out_shape=shapes,
        compiler_params=pltpu.CompilerParams(vmem_limit_bytes=limit * 1024 * 1024),
        cost_estimate=pl.CostEstimate(flops=flops, bytes_accessed=moved, transcendentals=0),
        name=name,
    )(*ready, *inputs)


def join_share(piece, suffix_columns, routes_columns, tok_quarter):
    rows = piece.shape[0]
    tokens = suffix_columns.shape[1]
    top, groups, _ = routes_columns.shape

    def kernel(piece_ref, suffix_ref, routes_ref, near_ref, full_ref, lite_ref):
        group_index = lax.axis_index("group")
        shape = (tok_quarter, tokens)
        row = lax.broadcasted_iota(jnp.int32, shape, 0)
        token = lax.broadcasted_iota(jnp.int32, shape, 1)
        select = jnp.where(token == group_index * tok_quarter + row, 1.0, 0.0)
        share = dot_t(select.astype(jnp.bfloat16), suffix_ref[...]).astype(jnp.bfloat16)
        named = jnp.zeros((top, tok_quarter), jnp.float32)
        for j in range(groups):
            part = routes_ref[:, j, :].astype(jnp.float32)
            named = jnp.where(group_index == j, part, named)
        named = jnp.concatenate(
            [named, jnp.zeros((ROUTE_ROWS - top, tok_quarter), jnp.float32)], axis=0
        )
        named = jnp.concatenate(
            [named, jnp.zeros((ROUTE_ROWS, piece_ref.shape[1] - tok_quarter), jnp.float32)], axis=1
        ).astype(jnp.bfloat16)
        piece = piece_ref[...]
        near_ref[:rows, :] = piece
        near_ref[rows:, :] = share
        full_ref[:rows, :] = piece
        full_ref[rows : rows + tok_quarter, :] = share
        full_ref[rows + tok_quarter :, :] = named
        lite_ref[:rows, :] = piece
        lite_ref[rows:, :] = named

    width = piece.shape[1]
    sizes = [rows + tok_quarter, rows + tok_quarter + ROUTE_ROWS, rows + ROUTE_ROWS]
    outputs = [((size, width), piece.dtype) for size in sizes]
    inputs = [piece, suffix_columns, routes_columns]
    return call(kernel, "join_share", inputs, outputs, 10_000_000)


def join_column(full, lites, own, rows):
    share = full.shape[0] - rows - ROUTE_ROWS

    def kernel(*refs):
        full_ref, *lite_refs, own_ref, column_ref, routes_ref = refs
        column_ref[: rows + share, :] = full_ref[: rows + share, :]
        routes_ref[0] = own_ref[rows:, :128]
        routes_ref[1] = full_ref[rows + share :, :128]
        at = rows + share
        for i, ref in enumerate(lite_refs):
            column_ref[at : at + rows, :] = ref[:rows, :]
            routes_ref[i + 2] = ref[rows:, :128]
            at += rows

    count = len(lites)
    outputs = [
        ((rows + share + count * rows, full.shape[1]), full.dtype),
        ((count + 2, ROUTE_ROWS, 128), full.dtype),
    ]
    return call(kernel, "join_column", [full, *lites, own], outputs, 0)


def join_rows(*blocks, ready=()):
    def kernel(*refs):
        out = refs[-1]
        at = 0
        for ref in refs[:-1]:
            out[at : at + ref.shape[0], :] = ref[...]
            at += ref.shape[0]

    rows = sum(block.shape[0] for block in blocks)
    shape = (rows, blocks[0].shape[1])
    return call(kernel, "join_rows", blocks, [(shape, blocks[0].dtype)], 0, ready=ready)[0]


def pass_on(blocks, ready=()):
    def kernel(*refs):
        for ref, out in zip(refs[: len(blocks)], refs[len(blocks) :]):
            out[...] = ref[...]

    outputs = [(block.shape, block.dtype) for block in blocks]
    return call(kernel, "pass_on", blocks, outputs, 0, ready=ready)


def place_keys(key_refs, spot_ref, token_ref, keys, bias):
    at = 0
    for ref in key_refs:
        rows = ref.shape[0]
        keys[at : at + rows, :] = ref[...]
        at += rows
    columns = token_ref[...]
    spots = spot_ref[...]
    low, high, start, here = (columns[:, i : i + 1] for i in range(4))
    seen = ((spots >= low) & (spots < high)) | ((spots >= start) & (spots <= here))
    bias[...] = jnp.where(seen, 0.0, VERY_NEGATIVE)


SCORE_FACTOR = math.log2(math.e) / math.sqrt(NOPE + ROPE)


def score_rows(content, rotated, keys, bias, pair):
    scores = dot_t(content, keys[:, :LAT]) + dot_t(rotated, keys[:, LAT:])
    rows, count = scores.shape
    return (scores.reshape(pair, rows // pair, count) + bias[...][None]).reshape(rows, count)


def near_kernel(
    block_count, token_ref, spot_ref, order_ref, query_ref, key_up_ref, *refs
):
    key_refs = refs[:block_count]
    content_ref, rotated_ref, best_ref, sum_ref, acc_ref, keys, bias = refs[block_count:]
    tokens = query_ref.shape[0]
    pair = key_up_ref.shape[0]

    @pl.when(pl.program_id(0) == 0)
    def prepare():
        place_keys(key_refs, spot_ref, token_ref, keys, bias)

    queries = dot_f(order_ref[...], query_ref[...]).astype(jnp.bfloat16)
    size = NOPE + ROPE
    content = []
    rotated = []
    for h in range(pair):
        part = queries[:, h * size : (h + 1) * size]
        content.append(dot_f(part[:, :NOPE], key_up_ref[h]).astype(jnp.bfloat16))
        rotated.append(part[:, NOPE:])
    content = jnp.concatenate(content, axis=0)
    rotated = jnp.concatenate(rotated, axis=0)
    content_ref[...] = content
    rotated_ref[...] = rotated
    masked = score_rows(content, rotated, keys, bias, pair)
    best = jnp.max(masked, axis=-1, keepdims=True)
    weights = jnp.exp2((masked - best) * SCORE_FACTOR)
    best_ref[...] = best
    sum_ref[...] = jnp.sum(weights, axis=-1, keepdims=True)
    acc_ref[...] = dot_f(weights.astype(jnp.bfloat16), keys[:, :LAT])


def attend_near(tokens_info, spots, order, queries, key_up, blocks, ready):
    tokens = queries.shape[0]
    heads = key_up.shape[0]
    pair = 2
    count = sum(block.shape[0] for block in blocks)
    size = NOPE + ROPE

    def per_step(columns):
        return pl.BlockSpec((pair * tokens, columns), lambda i: (i, 0))

    rows = heads * tokens
    return pl.pallas_call(
        after(functools.partial(near_kernel, len(blocks)), len(ready)),
        grid=(heads // pair,),
        in_specs=unread(ready)
        + [
            whole(tokens_info),
            whole(spots),
            whole(order),
            pl.BlockSpec((tokens, pair * size), lambda i: (0, i)),
            pl.BlockSpec((pair, NOPE, LAT), lambda i: (i, 0, 0)),
        ]
        + [whole(block) for block in blocks],
        out_specs=[per_step(LAT), per_step(ROPE), per_step(1), per_step(1), per_step(LAT)],
        out_shape=[
            jax.ShapeDtypeStruct((rows, LAT), jnp.bfloat16),
            jax.ShapeDtypeStruct((rows, ROPE), jnp.bfloat16),
            jax.ShapeDtypeStruct((rows, 1), jnp.float32),
            jax.ShapeDtypeStruct((rows, 1), jnp.float32),
            jax.ShapeDtypeStruct((rows, LAT), jnp.float32),
        ],
        scratch_shapes=[
            pltpu.VMEM((count, LAT + ROPE), jnp.bfloat16),
            pltpu.VMEM((tokens, count), jnp.float32),
        ],
        compiler_params=pltpu.CompilerParams(vmem_limit_bytes=24 * 1024 * 1024),
        cost_estimate=pl.CostEstimate(
            flops=2 * rows * count * (LAT + ROPE + LAT),
            bytes_accessed=8_000_000,
            transcendentals=rows * count,
        ),
        name="attend_near",
    )(*ready, tokens_info, spots, order, queries, key_up, *blocks)


def far_kernel(
    block_count,
    tok_quarter,
    token_ref,
    spot_ref,
    content_ref,
    rotated_ref,
    best_ref,
    sum_ref,
    acc_ref,
    value_up_ref,
    output_ref,
    *refs,
):
    key_refs = refs[:block_count]
    own_ref, other_ref, keys, bias, total = refs[block_count:]
    step = pl.program_id(0)
    pair = value_up_ref.shape[0]
    tokens = content_ref.shape[0] // pair

    @pl.when(step == 0)
    def prepare():
        place_keys(key_refs, spot_ref, token_ref, keys, bias)
        total[...] = jnp.zeros_like(total)

    masked = score_rows(content_ref[...], rotated_ref[...], keys, bias, pair)
    before = best_ref[...]
    best = jnp.maximum(before, jnp.max(masked, axis=-1, keepdims=True))
    factor = jnp.exp2((before - best) * SCORE_FACTOR)
    weights = jnp.exp2((masked - best) * SCORE_FACTOR)
    weight_sum = sum_ref[...] * factor + jnp.sum(weights, axis=-1, keepdims=True)
    attended = acc_ref[...] * factor + dot_f(weights.astype(jnp.bfloat16), keys[:, :LAT])
    attended = (attended / weight_sum).astype(jnp.bfloat16)
    heads = [
        dot_f(attended[h * tokens : (h + 1) * tokens], value_up_ref[h]).astype(jnp.bfloat16)
        for h in range(pair)
    ]
    total[...] += dot_f(jnp.concatenate(heads, axis=1), output_ref[...])

    @pl.when(step == pl.num_programs(0) - 1)
    def finish():
        own_ref[...] = total[:tok_quarter, :]
        other_ref[...] = total[tok_quarter:, :].astype(jnp.bfloat16)


def attend_far(tokens_info, spots, near, value_up, output_weight, blocks, tok_quarter):
    tokens = tokens_info.shape[0]
    heads = value_up.shape[0]
    width = output_weight.shape[1]
    pair = 2
    count = sum(block.shape[0] for block in blocks)
    rows = heads * tokens

    def per_step(columns):
        return pl.BlockSpec((pair * tokens, columns), lambda i: (i, 0))

    return pl.pallas_call(
        functools.partial(far_kernel, len(blocks), tok_quarter),
        grid=(heads // pair,),
        in_specs=[
            whole(tokens_info),
            whole(spots),
            per_step(LAT),
            per_step(ROPE),
            per_step(1),
            per_step(1),
            per_step(LAT),
            pl.BlockSpec((pair, LAT, value_up.shape[2]), lambda i: (i, 0, 0)),
            pl.BlockSpec((pair * value_up.shape[2], width), lambda i: (i, 0)),
        ]
        + [whole(block) for block in blocks],
        out_specs=[
            pl.BlockSpec((tok_quarter, width), lambda i: (0, 0)),
            pl.BlockSpec((tokens - tok_quarter, width), lambda i: (0, 0)),
        ],
        out_shape=[
            jax.ShapeDtypeStruct((tok_quarter, width), jnp.float32),
            jax.ShapeDtypeStruct((tokens - tok_quarter, width), jnp.bfloat16),
        ],
        scratch_shapes=[
            pltpu.VMEM((count, LAT + ROPE), jnp.bfloat16),
            pltpu.VMEM((tokens, count), jnp.float32),
            pltpu.VMEM((tokens, width), jnp.float32),
        ],
        compiler_params=pltpu.CompilerParams(vmem_limit_bytes=24 * 1024 * 1024),
        cost_estimate=pl.CostEstimate(
            flops=2 * rows * count * (LAT + ROPE + LAT),
            bytes_accessed=12_000_000,
            transcendentals=rows * count,
        ),
        name="attend_far",
    )(tokens_info, spots, *near, value_up, output_weight, *blocks)


def pick_rows(turn, ring, top, block, routes_ref, router_ref, scaled_ref, outs):
    tokens = block.shape[0]
    capacity = outs[0].shape[0]
    tensor_index = lax.axis_index("tensor")
    here = lax.div(tensor_index, PLANE)
    plane_index = lax.rem(tensor_index, PLANE)
    order = ring_order(ring)
    place = sum(jnp.where(here == z, i, 0) for i, z in enumerate(order))
    place = lax.rem(place - turn + ring, ring)
    source = sum(jnp.where(place == i, z, 0) for i, z in enumerate(order))
    routes = routes_ref[lax.rem(here - source + ring, ring)][:, :tokens].astype(jnp.float32)
    targets = [
        (here * PLANE + lax.bitwise_xor(plane_index, d)).astype(jnp.float32)
        for d in range(PLANE)
    ]
    hits = [
        jnp.sum(jnp.where(routes[:top] == target, 1.0, 0.0), axis=0, keepdims=True)
        for target in targets
    ]
    before = lax.broadcasted_iota(jnp.int32, (tokens, tokens), 0)
    after_it = lax.broadcasted_iota(jnp.int32, (tokens, tokens), 1)
    earlier = jnp.where(before < after_it, 1.0, 0.0).astype(jnp.bfloat16)
    ranks = dot_f(jnp.concatenate(hits, axis=0).astype(jnp.bfloat16), earlier)
    count = router_ref.shape[0]
    expert = lax.broadcasted_iota(jnp.int32, (count, tokens), 0).astype(jnp.float32)
    named = jnp.zeros((count, tokens), jnp.float32)
    for i in range(top):
        named = named + jnp.where(expert == routes[i : i + 1], 1.0, 0.0)
    picked = jax.nn.sigmoid(dot_t(router_ref[...], block)) * named
    gates = picked / jnp.sum(picked, axis=0, keepdims=True) * ROUTE_SCALING
    slot = lax.broadcasted_iota(jnp.int32, (capacity, tokens), 0).astype(jnp.float32)
    for d, out in enumerate(outs):
        taken = jnp.where(slot == ranks[d : d + 1], hits[d], 0.0)
        out[...] = dot_f(taken.astype(jnp.bfloat16), block).astype(jnp.bfloat16)
        gate = jnp.sum(jnp.where(expert == targets[d], gates, 0.0), axis=0, keepdims=True)
        scaled_ref[d * capacity : (d + 1) * capacity, :] = (taken * gate).astype(jnp.bfloat16)


def pick_outputs(block, capacity):
    tokens, width = block.shape
    pieces = [((capacity, width), jnp.bfloat16)] * PLANE
    return [((PLANE * capacity, tokens), jnp.bfloat16)] + pieces


def settle(hidden, own, others, gain, routes, router, sizes):
    ring, top, capacity = sizes

    def kernel(*refs):
        hidden_ref, own_ref = refs[:2]
        other_refs = refs[2 : 2 + len(others)]
        gain_ref, routes_ref, router_ref = refs[2 + len(others) : 5 + len(others)]
        residual_ref, normed_ref, scaled_ref, *outs = refs[5 + len(others) :]
        total = own_ref[...]
        for ref in other_refs:
            total = total + ref[...].astype(jnp.float32)
        residual = (hidden_ref[...].astype(jnp.float32) + total).astype(jnp.bfloat16)
        residual_ref[...] = residual
        normed = norm_rows(residual, gain_ref[...])
        normed_ref[...] = normed
        pick_rows(0, ring, top, normed, routes_ref, router_ref, scaled_ref, outs)

    outputs = [(hidden.shape, jnp.bfloat16)] * 2 + pick_outputs(hidden, capacity)
    inputs = [hidden, own, *others, gain, routes, router]
    residual, normed, scaled, *pieces = call(kernel, "settle", inputs, outputs, 70_000_000)
    return residual, normed, scaled, pieces


def choose(turn, block, arrived, routes, router, sizes, ready):
    ring, top, capacity = sizes

    def kernel(block_ref, routes_ref, router_ref, *refs):
        row_refs = refs[:PLANE]
        joined_ref, scaled_ref, *outs = refs[PLANE:]
        pick_rows(turn, ring, top, block_ref[...], routes_ref, router_ref, scaled_ref, outs)
        for d, ref in enumerate(row_refs):
            joined_ref[d * capacity : (d + 1) * capacity, :] = ref[...]

    joined = ((PLANE * capacity, block.shape[1]), jnp.bfloat16)
    outputs = [joined] + pick_outputs(block, capacity)
    inputs = [block, routes, router, *arrived]
    joined, scaled, *pieces = call(kernel, "choose", inputs, outputs, 70_000_000, ready=ready)
    return joined, scaled, pieces


def expert_kernel(count, kept, depth_steps, *refs):
    row_refs = refs[:count]
    gate_ref, up_ref, down_ref, own_ref, other_ref, rows, gate_sum, up_sum, hidden = refs[count:]
    step = pl.program_id(0)
    depth = gate_ref.shape[1]

    @pl.when(step == 0)
    def prepare():
        at = 0
        for ref in row_refs:
            size = ref.shape[0]
            for i in range(depth_steps):
                rows[i, at : at + size, :] = ref[:, i * depth : (i + 1) * depth]
            at += size

    @pl.when(step < depth_steps)
    def widen():
        part = rows[jnp.minimum(step, depth_steps - 1)]
        gate_part = dot_t(part, gate_ref[...])
        up_part = dot_t(part, up_ref[...])

        @pl.when(step == 0)
        def first():
            gate_sum[...] = gate_part
            up_sum[...] = up_part

        @pl.when(step > 0)
        def later():
            gate_sum[...] += gate_part
            up_sum[...] += up_part

    @pl.when(step == depth_steps - 1)
    def activate():
        hidden[...] = (jax.nn.silu(gate_sum[...]) * up_sum[...]).astype(jnp.bfloat16)

    @pl.when(step >= depth_steps)
    def narrow():
        own_ref[...] = dot_f(hidden[:kept, :], down_ref[...])
        other_ref[...] = dot_f(hidden[kept:, :], down_ref[...]).astype(jnp.bfloat16)


def expert_apply(pieces, kept, gate_part, up_part, down_part, ready):
    steps = 2
    total = sum(piece.shape[0] for piece in pieces)
    units, width = gate_part.shape
    depth = width // steps
    return pl.pallas_call(
        after(functools.partial(expert_kernel, len(pieces), kept, steps), len(ready)),
        grid=(2 * steps,),
        in_specs=unread(ready)
        + [whole(piece) for piece in pieces]
        + [
            pl.BlockSpec((units, depth), lambda i: (0, jnp.minimum(i, steps - 1))),
            pl.BlockSpec((units, depth), lambda i: (0, jnp.minimum(i, steps - 1))),
            pl.BlockSpec((units, depth), lambda i: (0, jnp.maximum(i - steps, 0))),
        ],
        out_specs=[
            pl.BlockSpec((kept, depth), lambda i: (0, jnp.maximum(i - steps, 0))),
            pl.BlockSpec((total - kept, depth), lambda i: (0, jnp.maximum(i - steps, 0))),
        ],
        out_shape=[
            jax.ShapeDtypeStruct((kept, width), jnp.float32),
            jax.ShapeDtypeStruct((total - kept, width), jnp.bfloat16),
        ],
        scratch_shapes=[
            pltpu.VMEM((steps, total, depth), jnp.bfloat16),
            pltpu.VMEM((total, units), jnp.float32),
            pltpu.VMEM((total, units), jnp.float32),
            pltpu.VMEM((total, units), jnp.bfloat16),
        ],
        compiler_params=pltpu.CompilerParams(vmem_limit_bytes=24 * 1024 * 1024),
        cost_estimate=pl.CostEstimate(
            flops=6 * total * width * units, bytes_accessed=10_000_000, transcendentals=0
        ),
        name="experts",
    )(*ready, *pieces, gate_part, up_part, down_part)


def blend(own, others, pieces, ready):
    def kernel(own_ref, *refs):
        other_refs = refs[: len(others)]
        outs = refs[len(others) :]
        total = own_ref[...]
        for ref in other_refs:
            total = total + ref[...].astype(jnp.float32)
        total = total.astype(jnp.bfloat16)
        size = outs[0].shape[0]
        for d, out in enumerate(outs):
            out[...] = total[d * size : (d + 1) * size]

    shape = (own.shape[0] // pieces, own.shape[1])
    outputs = [(shape, jnp.bfloat16)] * pieces
    return call(kernel, "blend", [own, *others], outputs, 1_000_000, ready=ready)


def scatter_sum(scaled_ref, piece_refs, running_ref):
    size = piece_refs[0].shape[0]
    returned = jnp.concatenate([ref[...] for ref in piece_refs], axis=0)
    total = lax.dot_general(
        scaled_ref[...], returned, (((0,), (0,)), ((), ())), preferred_element_type=jnp.float32
    )
    if running_ref is not None:
        total = total + running_ref[...].astype(jnp.float32)
    return total


def collect(scaled, pieces, running):
    extra = [] if running is None else [running]

    def kernel(scaled_ref, *refs):
        running_ref = refs[len(pieces)] if extra else None
        total = scatter_sum(scaled_ref, refs[: len(pieces)], running_ref)
        refs[-1][...] = total.astype(jnp.bfloat16)

    shape = (scaled.shape[1], pieces[0].shape[1])
    inputs = [scaled, *pieces, *extra]
    return call(kernel, "collect", inputs, [(shape, jnp.bfloat16)], 35_000_000)[0]


def conclude(scaled, pieces, running, residual, gain):
    extra = [] if running is None else [running]

    def kernel(residual_ref, gain_ref, scaled_ref, *refs):
        running_ref = refs[len(pieces)] if extra else None
        total = scatter_sum(scaled_ref, refs[: len(pieces)], running_ref)
        layer = (residual_ref[...].astype(jnp.float32) + total).astype(jnp.bfloat16)
        refs[-2][...] = layer
        refs[-1][...] = norm_rows(layer, gain_ref[...])

    inputs = [residual, gain, scaled, *pieces, *extra]
    return call(kernel, "conclude", inputs, [(residual.shape, jnp.bfloat16)] * 2, 35_000_000)


def per_device(
    hidden_in,
    queries,
    suffix_latent,
    prefix_latent,
    key_up,
    value_up,
    output_weight,
    norm_gain,
    router,
    expert_gate,
    expert_up,
    expert_down,
    next_gain,
    next_query_weight,
    next_latent_weight,
    suffix_lengths,
    request_tenant,
    tenant_lengths,
    page_table,
    routes,
):
    tok_slice = hidden_in.shape[0]
    groups = lax.axis_size("group")
    ring = lax.axis_size("tensor") // PLANE
    group_index = lax.axis_index("group")
    tensor_index = lax.axis_index("tensor")
    ring_index = tensor_index // PLANE
    plane_index = tensor_index % PLANE
    tok_quarter = tok_slice // groups
    expert_count = router.shape[1]
    top_count = routes.shape[2]
    capacity = max(2, 4 * tok_quarter * top_count // (3 * expert_count))
    capacity = -(-capacity // 16) * 16
    int32 = jnp.int32

    real_rows = prefix_latent.shape[0]
    piece_rows = -(-real_rows // 16) * 16
    piece = prefix_latent
    if piece_rows != real_rows:
        piece = jnp.pad(piece, ((0, piece_rows - real_rows), (0, 0)))
    routes_columns = jnp.transpose(routes, (2, 0, 1))
    both, full, lite = join_share(piece, suffix_latent.T, routes_columns, tok_quarter)
    along = [send_round(full, PLANE)] + [send_round(lite, PLANE * k) for k in range(2, ring)]
    near_plane = [send_plane(both, d) if d else both for d in range(PLANE)]
    near_blocks = [
        send_group(block, j) if j else block for j in range(groups) for block in near_plane
    ]
    column, routes_ring = join_column(along[0], along[1:], lite, piece_rows)
    far_plane = [send_plane(column, d) if d else column for d in range(PLANE)]

    later = 1 << 20
    first_token = tensor_index * tok_slice

    pages = real_rows // PAGE

    def positions_of(steps, with_suffix):
        parts = []
        for k in steps:
            from_ring = (ring_index - k + ring) % ring
            shape = (groups, PLANE, piece_rows)
            j, d, r = (lax.broadcasted_iota(int32, shape, axis) for axis in range(3))
            owner = ((group_index ^ j) * ring + from_ring) * PLANE + (plane_index ^ d)
            spot = owner * real_rows + r
            page = owner[:, :, :pages] * pages + r[:, :, :pages]
            hit = page[..., None] == jnp.arange(page_table.shape[0], dtype=int32)
            page = jnp.sum(jnp.where(hit, page_table, 0), axis=-1)
            page = jnp.repeat(page, PAGE, axis=2)
            page = jnp.pad(page, ((0, 0), (0, 0), (0, piece_rows - real_rows)))
            parts.append(jnp.where(r < real_rows, page * PAGE + spot % PAGE, -1))
            if k in with_suffix:
                shape = (groups, PLANE, tok_quarter)
                j, d, r = (lax.broadcasted_iota(int32, shape, axis) for axis in range(3))
                owner = from_ring * PLANE + (plane_index ^ d)
                token = owner * tok_slice + (group_index ^ j) * tok_quarter + r
                parts.append(token + later)
        return jnp.concatenate(parts, axis=2).reshape(1, -1)

    near_spots = positions_of([0], [0])
    far_spots = positions_of(range(1, ring), [1])

    row = jnp.arange(tok_slice, dtype=int32)
    local = (row % tok_quarter) * groups + (group_index ^ (row // tok_quarter))
    permutation = (local[:, None] == jnp.arange(tok_slice, dtype=int32)[None, :]).astype(
        jnp.bfloat16
    )
    positions = first_token + local
    requests = suffix_lengths.shape[0]
    tenants = tenant_lengths.shape[0]
    upto = jnp.arange(requests)[None, :] <= jnp.arange(requests)[:, None]
    request_ends = jnp.sum(jnp.where(upto, suffix_lengths[None, :], 0), axis=1)
    request_starts = request_ends - suffix_lengths
    inside = (positions[:, None] >= request_starts[None, :]) & (
        positions[:, None] < request_ends[None, :]
    )
    token_start = jnp.sum(jnp.where(inside, request_starts[None, :], 0), axis=1)
    token_tenant = jnp.sum(jnp.where(inside, request_tenant[None, :], 0), axis=1)
    upto = jnp.arange(tenants)[None, :] <= jnp.arange(tenants)[:, None]
    tenant_ends = jnp.sum(jnp.where(upto, tenant_lengths[None, :], 0), axis=1)
    tenant_starts = tenant_ends - tenant_lengths
    tenant_pick = token_tenant[:, None] == jnp.arange(tenants, dtype=int32)[None, :]
    range_low = jnp.sum(jnp.where(tenant_pick, tenant_starts[None, :], 0), axis=1)
    range_high = jnp.sum(jnp.where(tenant_pick, tenant_ends[None, :], 0), axis=1)
    tokens_info = jnp.stack(
        [range_low, range_high, token_start + later, positions + later], axis=1
    )

    near = attend_near(
        tokens_info, near_spots, permutation, queries, key_up, near_blocks, [column]
    )
    far_plane = pass_on(far_plane, ready=[near[4]])
    far_blocks = [
        send_group(block, j) if j else block for j in range(groups) for block in far_plane
    ]
    attend_own, attend_other = attend_far(
        tokens_info, far_spots, near, value_up, output_weight, far_blocks, tok_quarter
    )

    hidden_own = dot_f(permutation[:tok_quarter], hidden_in).astype(jnp.bfloat16)
    others = [
        send_group(attend_other[(j - 1) * tok_quarter : j * tok_quarter], j)
        for j in range(1, groups)
    ]
    sizes = (ring, top_count, capacity)
    experts_columns = router.T
    residual, block, scaled, pieces = settle(
        hidden_own,
        attend_own,
        others,
        norm_gain[None, :],
        routes_ring,
        experts_columns,
        sizes,
    )

    kept = PLANE * capacity
    gate_part = jnp.transpose(expert_gate, (0, 2, 1))[0]
    up_part = jnp.transpose(expert_up, (0, 2, 1))[0]
    down_part = expert_down[0]
    scales = [scaled]
    results = []
    for k in range(ring):
        arrived = [send_plane(piece, d) if d else piece for d, piece in enumerate(pieces)]
        ready = [result[0] for result in results[-1:]]
        if k + 1 < ring:
            block = send_ring(block, ring)
            joined, scaled, pieces = choose(
                k + 1, block, arrived, routes_ring, experts_columns, sizes, ready
            )
            scales.append(scaled)
        else:
            joined = join_rows(*arrived, ready=ready)
        rows = [send_group(joined, j) if j else joined for j in range(groups)]
        results.append(expert_apply(rows, kept, gate_part, up_part, down_part, ready))

    def give_back(k, ready):
        own, other = results[k]
        others = [send_group(other[(j - 1) * kept : j * kept], j) for j in range(1, groups)]
        pieces = blend(own, others, PLANE, ready)
        return [send_plane(piece, d) if d else piece for d, piece in enumerate(pieces)]

    running = None
    total = None
    for k in range(1, ring):
        returned = give_back(k, [])
        total = collect(scales[k], returned, running)
        running = send_ring(total, ring)
    returned = give_back(0, [] if total is None else [total])
    layer_rows, normed_next = conclude(
        scales[0], returned, running, residual, next_gain[None, :]
    )

    shares = [send_group(normed_next, j) if j else normed_next for j in range(groups)]
    gathered = lax.dot_general(
        permutation,
        jnp.concatenate(shares, axis=0),
        (((0,), (0,)), ((), ())),
        preferred_element_type=jnp.float32,
    ).astype(jnp.bfloat16)
    next_queries = dot_f(gathered, next_query_weight).astype(jnp.bfloat16)
    next_latent = dot_f(gathered, next_latent_weight).astype(jnp.bfloat16)
    return (layer_rows[:, None, :], next_queries, next_latent)


def solution(mesh):
    return jax.shard_map(
        per_device,
        mesh=mesh,
        in_specs=(
            P("tensor", None),
            P("tensor", "group"),
            P("tensor", None),
            P(("group", "tensor"), None),
            P("group", None, None),
            P("group", None, None),
            P("group", None),
            P(),
            P(),
            P("tensor", None, "group"),
            P("tensor", None, "group"),
            P("tensor", "group", None),
            P(),
            P(None, "group"),
            P(None, "group"),
            P(),
            P(),
            P(),
            P(),
            P(None, "tensor", None),
        ),
        out_specs=(P("tensor", "group", None), P("tensor", "group"), P("tensor", "group")),
        check_vma=False,
    )
```

```python
import functools
import math

import jax
import jax.numpy as jnp
import numpy as np
from jax import lax
from jax.experimental import pallas as pl
from jax.experimental.pallas import tpu as pltpu
from jax.sharding import PartitionSpec as P

NOPE = 128
ROPE = 64
LAT = 512
PAGE = 8
PLANE = 4
ROUTE_ROWS = 16
WIDE = 640

VERY_NEGATIVE = -1e30
ROUTE_SCALING = 2.446
NORM_EPSILON = 1e-06


def ring_order(count):
    odd = list(range(1, count, 2))
    even = list(range(2, count, 2))
    return [0] + odd + even[::-1]


def send_ring(block, count, steps=1):
    order = ring_order(count)
    after = {order[i]: order[(i + steps) % count] for i in range(count)}
    route = [
        (z * PLANE + p, after[z] * PLANE + p) for z in range(count) for p in range(PLANE)
    ]
    return lax.ppermute(block, "tensor", route)


def send_round(block, distance):
    count = lax.axis_size("tensor")
    return lax.ppermute(block, "tensor", [(i, (i + distance) % count) for i in range(count)])


def send_plane(block, distance):
    devices = range(lax.axis_size("tensor"))
    return lax.ppermute(block, "tensor", [(i, i ^ distance) for i in devices])


def send_group(block, distance):
    devices = range(lax.axis_size("group"))
    return lax.ppermute(block, "group", [(i, i ^ distance) for i in devices])


def norm_rows(row_block, gain_vector):
    values = row_block.astype(jnp.float32)
    mean_square = jnp.mean(values * values, axis=-1, keepdims=True)
    return (
        values * lax.rsqrt(mean_square + NORM_EPSILON) * gain_vector.astype(jnp.float32)
    ).astype(jnp.bfloat16)


def dot_t(left, right):
    return lax.dot_general(
        left, right, (((1,), (1,)), ((), ())), preferred_element_type=jnp.float32
    )


def dot_f(left, right):
    return jnp.dot(left, right, preferred_element_type=jnp.float32)


def whole(array):
    return pl.BlockSpec(array.shape, lambda *i: (0,) * len(array.shape))


def after(kernel, count):
    def inner(*refs):
        kernel(*refs[count:])

    return inner


def unread(arrays):
    return [pl.BlockSpec(memory_space=pl.ANY) for _ in arrays]


def call(kernel, name, inputs, outputs, flops, limit=12, ready=()):
    shapes = [jax.ShapeDtypeStruct(shape, dtype) for shape, dtype in outputs]
    moved = sum(a.size * a.dtype.itemsize for a in list(inputs) + shapes)
    return pl.pallas_call(
        after(kernel, len(ready)),
        grid=(1,),
        in_specs=unread(ready) + [whole(a) for a in inputs],
        out_specs=[whole(s) for s in shapes],
        out_shape=shapes,
        compiler_params=pltpu.CompilerParams(vmem_limit_bytes=limit * 1024 * 1024),
        cost_estimate=pl.CostEstimate(flops=flops, bytes_accessed=moved, transcendentals=0),
        name=name,
    )(*ready, *inputs)


def join_share(piece, suffix_columns, routes_columns, tok_quarter):
    rows = piece.shape[0]
    tokens = suffix_columns.shape[1]
    top, groups, _ = routes_columns.shape

    def kernel(piece_ref, suffix_ref, routes_ref, full_ref, lite_ref):
        group_index = lax.axis_index("group")
        shape = (tok_quarter, tokens)
        row = lax.broadcasted_iota(jnp.int32, shape, 0)
        token = lax.broadcasted_iota(jnp.int32, shape, 1)
        select = jnp.where(token == group_index * tok_quarter + row, 1.0, 0.0)
        share = dot_t(select.astype(jnp.bfloat16), suffix_ref[...]).astype(jnp.bfloat16)
        named = jnp.zeros((top, tok_quarter), jnp.float32)
        for j in range(groups):
            part = routes_ref[:, j, :].astype(jnp.float32)
            named = jnp.where(group_index == j, part, named)
        named = jnp.concatenate([named, jnp.zeros((rows - top, tok_quarter), jnp.float32)], axis=0)
        spare = WIDE - LAT - ROPE - tok_quarter
        if spare:
            named = jnp.concatenate([named, jnp.zeros((rows, spare), jnp.float32)], axis=1)
        named = named.astype(jnp.bfloat16)
        piece = piece_ref[...]
        last = jnp.concatenate([piece[:, LAT:], named], axis=1)
        for ref in (full_ref, lite_ref):
            ref[:rows, :LAT] = piece[:, :LAT]
            ref[:rows, LAT:] = last
        empty = jnp.zeros((tok_quarter, WIDE - LAT - ROPE), jnp.bfloat16)
        full_ref[rows:, :LAT] = share[:, :LAT]
        full_ref[rows:, LAT:] = jnp.concatenate([share[:, LAT:], empty], axis=1)

    outputs = [((size, WIDE), piece.dtype) for size in (rows + tok_quarter, rows)]
    inputs = [piece, suffix_columns, routes_columns]
    return call(kernel, "join_share", inputs, outputs, 10_000_000, limit=58)


def join_column(blocks, rows, share):
    count = len(blocks)

    def kernel(*refs):
        block_refs = refs[:count]
        near_ref, *far_refs, routes_ref = refs[count:]
        plane_index = lax.rem(lax.axis_index("tensor"), PLANE)
        at = 0
        for i, ref in enumerate(block_refs):
            near_ref[at : at + ref.shape[0], :] = ref[...]
            at += ref.shape[0]
            routes_ref[i] = ref[:ROUTE_ROWS, LAT:]
        here = block_refs[0][rows:, :].astype(jnp.float32)
        before = block_refs[1][rows:, :].astype(jnp.float32)
        for d, far_ref in enumerate(far_refs):
            for i, ref in enumerate(block_refs):
                far_ref[i * rows : (i + 1) * rows, :] = ref[:rows, :]
            later = plane_index < lax.bitwise_xor(plane_index, d + 1)
            part = jnp.where(later, here, before).astype(jnp.bfloat16)
            far_ref[count * rows :, :] = part

    dtype = blocks[0].dtype
    outputs = [((count * rows + 2 * share, WIDE), dtype)]
    outputs += [((count * rows + share, WIDE), dtype)] * (PLANE - 1)
    outputs.append(((count, ROUTE_ROWS, WIDE - LAT), dtype))
    near, *far, routes = call(kernel, "join_column", blocks, outputs, 0)
    return near, far, routes


def pass_on(blocks, ready):
    first = len(ready)

    def kernel(*refs):
        pass

    return pl.pallas_call(
        kernel,
        in_specs=unread(ready) + unread(blocks),
        out_specs=unread(blocks),
        out_shape=[jax.ShapeDtypeStruct(block.shape, block.dtype) for block in blocks],
        input_output_aliases={first + i: i for i in range(len(blocks))},
        compiler_params=pltpu.CompilerParams(vmem_limit_bytes=1024 * 1024),
        name="pass_on",
    )(*ready, *blocks)


LATER = 1 << 20


def key_table(groups, planes, segments):
    rows = []
    for j in range(groups):
        for d in planes:
            for k, count, real, suffix in segments:
                rows += [(j, d, k, r, suffix, r < real) for r in range(count)]
    table = np.zeros((8, len(rows)), np.int32)
    table[:6] = np.array(rows, np.int32).T
    table[6] = table[3] // PAGE
    table[7] = table[3] % PAGE
    return table


def make_plan(tables, lengths, tenants, tenant_lengths, page_table, ring, piece_rows, sizes, ready):
    tok_slice, tok_quarter, groups = sizes
    requests = lengths.shape[0]
    tenant_count = tenant_lengths.shape[0]
    pages = page_table.shape[1]
    piece_pages = piece_rows // PAGE

    def spots_of(table, page_row, group_index, ring_index, plane_index):
        j, d, k, r, suffix, real, page_at, within = (table[i : i + 1, :] for i in range(8))
        in_plane = lax.bitwise_xor(plane_index, d)
        k = jnp.where(suffix == 2, jnp.where(in_plane < plane_index, 0, 1), k)
        from_ring = ring_index - k
        from_ring = jnp.where(from_ring < 0, from_ring + ring, from_ring)
        of_group = lax.bitwise_xor(group_index, j)
        owner = (of_group * ring + from_ring) * PLANE + in_plane
        index = owner * piece_pages + page_at
        count = table.shape[1]
        page = lax.broadcasted_iota(jnp.int32, (pages, count), 0)
        hit = jnp.where(page == index, 1.0, 0.0).astype(jnp.bfloat16)
        found = dot_f(page_row, hit)[:1].astype(jnp.int32)
        logical = jnp.where(real > 0, found * PAGE + within, -1)
        token = (from_ring * PLANE + in_plane) * tok_slice + of_group * tok_quarter + r
        return jnp.where(suffix > 0, token + LATER, logical)

    def kernel(lengths_ref, tenants_ref, tenant_lengths_ref, page_ref, *refs):
        table_refs = refs[: len(tables)]
        info_ref, order_ref, *spot_refs = refs[len(tables) :]
        group_index = jnp.full((1, 1), lax.axis_index("group"), jnp.int32)
        tensor_index = lax.axis_index("tensor")
        ring_index = jnp.full((1, 1), lax.div(tensor_index, PLANE), jnp.int32)
        plane_index = jnp.full((1, 1), lax.rem(tensor_index, PLANE), jnp.int32)
        page_row = page_ref[...].astype(jnp.float32).astype(jnp.bfloat16)
        page_row = jnp.broadcast_to(page_row, (16, pages))
        for table_ref, spot_ref in zip(table_refs, spot_refs):
            spot_ref[...] = spots_of(
                table_ref[...], page_row, group_index, ring_index, plane_index
            )
        row = lax.broadcasted_iota(jnp.int32, (tok_slice, 1), 0)
        share = jnp.zeros((tok_slice, 1), jnp.int32)
        for j in range(1, groups):
            share = share + jnp.where(row >= j * tok_quarter, 1, 0)
        local = (row - share * tok_quarter) * groups + lax.bitwise_xor(group_index, share)
        column = lax.broadcasted_iota(jnp.int32, (tok_slice, tok_slice), 1)
        order_ref[...] = jnp.where(column == local, 1.0, 0.0).astype(jnp.bfloat16)
        position = local + tensor_index * tok_slice
        low = jnp.zeros((tok_slice, 1), jnp.int32)
        high = jnp.zeros((tok_slice, 1), jnp.int32)
        start = jnp.zeros((tok_slice, 1), jnp.int32)
        begin = 0
        for i in range(requests):
            end = begin + lengths_ref[i]
            inside = (position >= begin) & (position < end)
            tenant = tenants_ref[i]
            first = 0
            tenant_low = 0
            tenant_high = 0
            for t in range(tenant_count):
                last = first + tenant_lengths_ref[t]
                tenant_low = jnp.where(tenant == t, first, tenant_low)
                tenant_high = jnp.where(tenant == t, last, tenant_high)
                first = last
            start = jnp.where(inside, begin, start)
            low = jnp.where(inside, tenant_low, low)
            high = jnp.where(inside, tenant_high, high)
            begin = end
        for i, value in enumerate((low, high, start + LATER, position + LATER)):
            info_ref[:, i : i + 1] = value

    shapes = [
        jax.ShapeDtypeStruct((tok_slice, 4), jnp.int32),
        jax.ShapeDtypeStruct((tok_slice, tok_slice), jnp.bfloat16),
    ] + [jax.ShapeDtypeStruct((1, table.shape[1]), jnp.int32) for table in tables]
    scalar = pl.BlockSpec(memory_space=pltpu.SMEM)
    arrays = [page_table, *tables]
    return pl.pallas_call(
        after(kernel, len(ready)),
        grid=(1,),
        in_specs=unread(ready) + [scalar, scalar, scalar] + [whole(a) for a in arrays],
        out_specs=[whole(shape) for shape in shapes],
        out_shape=shapes,
        compiler_params=pltpu.CompilerParams(vmem_limit_bytes=58 * 1024 * 1024),
        cost_estimate=pl.CostEstimate(
            flops=4_000_000_000, bytes_accessed=1_000_000, transcendentals=0
        ),
        name="make_plan",
    )(*ready, lengths, tenants, tenant_lengths, *arrays)


def place_keys(key_refs, spot_ref, token_ref, keys, bias):
    at = 0
    for ref in key_refs:
        rows = ref.shape[0]
        keys[at : at + rows, :] = ref[...]
        at += rows
    columns = token_ref[...]
    spots = spot_ref[...]
    low, high, start, here = (columns[:, i : i + 1] for i in range(4))
    seen = ((spots >= low) & (spots < high)) | ((spots >= start) & (spots <= here))
    bias[...] = jnp.where(seen, 0.0, VERY_NEGATIVE)


SCORE_FACTOR = math.log2(math.e) / math.sqrt(NOPE + ROPE)


def score_rows(queries, keys, bias, pair):
    scores = dot_t(queries, keys[...])
    rows, count = scores.shape
    return (scores.reshape(pair, rows // pair, count) + bias[...][None]).reshape(rows, count)


def near_kernel(
    block_count, token_ref, spot_ref, order_ref, query_ref, key_up_ref, *refs
):
    key_refs = refs[:block_count]
    wide_ref, best_ref, sum_ref, acc_ref, flag_ref, keys, bias = refs[block_count:]
    flag_ref[...] = jnp.zeros_like(flag_ref)
    tokens = query_ref.shape[0]
    pair = key_up_ref.shape[0]

    @pl.when(pl.program_id(0) == 0)
    def prepare():
        place_keys(key_refs, spot_ref, token_ref, keys, bias)

    queries = dot_f(order_ref[...], query_ref[...]).astype(jnp.bfloat16)
    size = NOPE + ROPE
    wide = []
    empty = jnp.zeros((tokens, WIDE - LAT - ROPE), jnp.bfloat16)
    for h in range(pair):
        part = queries[:, h * size : (h + 1) * size]
        content = dot_f(part[:, :NOPE], key_up_ref[h]).astype(jnp.bfloat16)
        wide.append(jnp.concatenate([content, part[:, NOPE:], empty], axis=1))
    wide = jnp.concatenate(wide, axis=0)
    wide_ref[...] = wide
    masked = score_rows(wide, keys, bias, pair)
    best = jnp.max(masked, axis=-1, keepdims=True)
    weights = jnp.exp2((masked - best) * SCORE_FACTOR)
    best_ref[...] = best
    sum_ref[...] = jnp.sum(weights, axis=-1, keepdims=True)
    acc_ref[...] = dot_f(weights.astype(jnp.bfloat16), keys[:, :LAT])


def attend_near(tokens_info, spots, order, queries, key_up, blocks, ready):
    tokens = queries.shape[0]
    heads = key_up.shape[0]
    pair = min(4, heads)
    count = sum(block.shape[0] for block in blocks)
    size = NOPE + ROPE

    def per_step(columns):
        return pl.BlockSpec((pair * tokens, columns), lambda i: (i, 0))

    rows = heads * tokens
    return pl.pallas_call(
        after(functools.partial(near_kernel, len(blocks)), len(ready)),
        grid=(heads // pair,),
        in_specs=unread(ready)
        + [
            whole(tokens_info),
            whole(spots),
            whole(order),
            pl.BlockSpec((tokens, pair * size), lambda i: (0, i)),
            pl.BlockSpec((pair, NOPE, LAT), lambda i: (i, 0, 0)),
        ]
        + [whole(block) for block in blocks],
        out_specs=[per_step(WIDE), per_step(1), per_step(1), per_step(LAT)]
        + [pl.BlockSpec((8, 128), lambda i: (0, 0))],
        out_shape=[
            jax.ShapeDtypeStruct((rows, WIDE), jnp.bfloat16),
            jax.ShapeDtypeStruct((rows, 1), jnp.float32),
            jax.ShapeDtypeStruct((rows, 1), jnp.float32),
            jax.ShapeDtypeStruct((rows, LAT), jnp.float32),
            jax.ShapeDtypeStruct((8, 128), jnp.float32),
        ],
        scratch_shapes=[
            pltpu.VMEM((count, WIDE), jnp.bfloat16),
            pltpu.VMEM((tokens, count), jnp.float32),
        ],
        compiler_params=pltpu.CompilerParams(vmem_limit_bytes=58 * 1024 * 1024),
        cost_estimate=pl.CostEstimate(
            flops=2 * rows * count * (LAT + ROPE + LAT),
            bytes_accessed=8_000_000,
            transcendentals=rows * count,
        ),
        name="attend_near",
    )(*ready, tokens_info, spots, order, queries, key_up, *blocks)


def add_keys(wide_ref, best_ref, sum_ref, acc_ref, keys, bias, pair):
    masked = score_rows(wide_ref[...], keys, bias, pair)
    before = best_ref[...]
    best = jnp.maximum(before, jnp.max(masked, axis=-1, keepdims=True))
    factor = jnp.exp2((before - best) * SCORE_FACTOR)
    weights = jnp.exp2((masked - best) * SCORE_FACTOR)
    weight_sum = sum_ref[...] * factor + jnp.sum(weights, axis=-1, keepdims=True)
    attended = acc_ref[...] * factor + dot_f(weights.astype(jnp.bfloat16), keys[:, :LAT])
    return best, weight_sum, attended


def mid_kernel(block_count, pair, token_ref, spot_ref, wide_ref, best_ref, sum_ref, acc_ref, *refs):
    key_refs = refs[:block_count]
    new_best_ref, new_sum_ref, new_acc_ref, flag_ref, keys, bias = refs[block_count:]
    flag_ref[...] = jnp.zeros_like(flag_ref)

    @pl.when(pl.program_id(0) == 0)
    def prepare():
        place_keys(key_refs, spot_ref, token_ref, keys, bias)

    new_best_ref[...], new_sum_ref[...], new_acc_ref[...] = add_keys(
        wide_ref, best_ref, sum_ref, acc_ref, keys, bias, pair
    )


def attend_mid(tokens_info, spots, near, blocks):
    tokens = tokens_info.shape[0]
    rows = near[0].shape[0]
    heads = rows // tokens
    pair = min(4, heads)
    count = sum(block.shape[0] for block in blocks)

    def per_step(columns):
        return pl.BlockSpec((pair * tokens, columns), lambda i: (i, 0))

    return pl.pallas_call(
        functools.partial(mid_kernel, len(blocks), pair),
        grid=(heads // pair,),
        in_specs=[whole(tokens_info), whole(spots)]
        + [per_step(WIDE), per_step(1), per_step(1), per_step(LAT)]
        + [whole(block) for block in blocks],
        out_specs=[per_step(1), per_step(1), per_step(LAT)]
        + [pl.BlockSpec((8, 128), lambda i: (0, 0))],
        out_shape=[
            jax.ShapeDtypeStruct((rows, 1), jnp.float32),
            jax.ShapeDtypeStruct((rows, 1), jnp.float32),
            jax.ShapeDtypeStruct((rows, LAT), jnp.float32),
            jax.ShapeDtypeStruct((8, 128), jnp.float32),
        ],
        scratch_shapes=[
            pltpu.VMEM((count, WIDE), jnp.bfloat16),
            pltpu.VMEM((tokens, count), jnp.float32),
        ],
        compiler_params=pltpu.CompilerParams(vmem_limit_bytes=58 * 1024 * 1024),
        cost_estimate=pl.CostEstimate(
            flops=2 * rows * count * (LAT + ROPE + LAT),
            bytes_accessed=8_000_000,
            transcendentals=rows * count,
        ),
        name="attend_mid",
    )(tokens_info, spots, *near, *blocks)


def far_kernel(
    block_count,
    tok_quarter,
    token_ref,
    spot_ref,
    wide_ref,
    best_ref,
    sum_ref,
    acc_ref,
    value_up_ref,
    output_ref,
    *refs,
):
    key_refs = refs[:block_count]
    own_ref, other_ref, keys, bias, total = refs[block_count:]
    step = pl.program_id(0)
    pair = value_up_ref.shape[0]
    tokens = wide_ref.shape[0] // pair

    @pl.when(step == 0)
    def prepare():
        place_keys(key_refs, spot_ref, token_ref, keys, bias)
        total[...] = jnp.zeros_like(total)

    _, weight_sum, attended = add_keys(wide_ref, best_ref, sum_ref, acc_ref, keys, bias, pair)
    attended = (attended / weight_sum).astype(jnp.bfloat16)
    heads = [
        dot_f(attended[h * tokens : (h + 1) * tokens], value_up_ref[h]).astype(jnp.bfloat16)
        for h in range(pair)
    ]
    total[...] += dot_f(jnp.concatenate(heads, axis=1), output_ref[...])

    @pl.when(step == pl.num_programs(0) - 1)
    def finish():
        own_ref[...] = total[:tok_quarter, :]
        other_ref[...] = total[tok_quarter:, :].astype(jnp.bfloat16)


def attend_far(tokens_info, spots, near, value_up, output_weight, blocks, tok_quarter):
    tokens = tokens_info.shape[0]
    heads = value_up.shape[0]
    width = output_weight.shape[1]
    pair = min(4, heads)
    count = sum(block.shape[0] for block in blocks)
    rows = heads * tokens

    def per_step(columns):
        return pl.BlockSpec((pair * tokens, columns), lambda i: (i, 0))

    return pl.pallas_call(
        functools.partial(far_kernel, len(blocks), tok_quarter),
        grid=(heads // pair,),
        in_specs=[
            whole(tokens_info),
            whole(spots),
            per_step(WIDE),
            per_step(1),
            per_step(1),
            per_step(LAT),
            pl.BlockSpec((pair, LAT, value_up.shape[2]), lambda i: (i, 0, 0)),
            pl.BlockSpec((pair * value_up.shape[2], width), lambda i: (i, 0)),
        ]
        + [whole(block) for block in blocks],
        out_specs=[
            pl.BlockSpec((tok_quarter, width), lambda i: (0, 0)),
            pl.BlockSpec((tokens - tok_quarter, width), lambda i: (0, 0)),
        ],
        out_shape=[
            jax.ShapeDtypeStruct((tok_quarter, width), jnp.float32),
            jax.ShapeDtypeStruct((tokens - tok_quarter, width), jnp.bfloat16),
        ],
        scratch_shapes=[
            pltpu.VMEM((count, WIDE), jnp.bfloat16),
            pltpu.VMEM((tokens, count), jnp.float32),
            pltpu.VMEM((tokens, width), jnp.float32),
        ],
        compiler_params=pltpu.CompilerParams(vmem_limit_bytes=58 * 1024 * 1024),
        cost_estimate=pl.CostEstimate(
            flops=2 * rows * count * (LAT + ROPE + LAT),
            bytes_accessed=12_000_000,
            transcendentals=rows * count,
        ),
        name="attend_far",
    )(tokens_info, spots, *near, value_up, output_weight, *blocks)


def pick_rows(turn, ring, top, block, routes_ref, router_ref, scaled_ref, outs):
    tokens = block.shape[0]
    capacity = outs[0].shape[0]
    tensor_index = lax.axis_index("tensor")
    here = lax.div(tensor_index, PLANE)
    plane_index = lax.rem(tensor_index, PLANE)
    order = ring_order(ring)
    place = sum(jnp.where(here == z, i, 0) for i, z in enumerate(order))
    place = lax.rem(place - turn + ring, ring)
    source = sum(jnp.where(place == i, z, 0) for i, z in enumerate(order))
    routes = routes_ref[lax.rem(here - source + ring, ring)].astype(jnp.float32)
    routes = routes[:, ROPE : ROPE + tokens]
    targets = [
        (here * PLANE + lax.bitwise_xor(plane_index, d)).astype(jnp.float32)
        for d in range(PLANE)
    ]
    hits = [
        jnp.sum(jnp.where(routes[:top] == target, 1.0, 0.0), axis=0, keepdims=True)
        for target in targets
    ]
    before = lax.broadcasted_iota(jnp.int32, (tokens, tokens), 0)
    after_it = lax.broadcasted_iota(jnp.int32, (tokens, tokens), 1)
    earlier = jnp.where(before < after_it, 1.0, 0.0).astype(jnp.bfloat16)
    ranks = dot_f(jnp.concatenate(hits, axis=0).astype(jnp.bfloat16), earlier)
    count = router_ref.shape[0]
    expert = lax.broadcasted_iota(jnp.int32, (count, tokens), 0).astype(jnp.float32)
    named = jnp.zeros((count, tokens), jnp.float32)
    for i in range(top):
        named = named + jnp.where(expert == routes[i : i + 1], 1.0, 0.0)
    picked = jax.nn.sigmoid(dot_t(router_ref[...], block)) * named
    gates = picked / jnp.sum(picked, axis=0, keepdims=True) * ROUTE_SCALING
    slot = lax.broadcasted_iota(jnp.int32, (capacity, tokens), 0).astype(jnp.float32)
    for d, out in enumerate(outs):
        taken = jnp.where(slot == ranks[d : d + 1], hits[d], 0.0)
        out[...] = dot_f(taken.astype(jnp.bfloat16), block).astype(jnp.bfloat16)
        gate = jnp.sum(jnp.where(expert == targets[d], gates, 0.0), axis=0, keepdims=True)
        scaled_ref[d * capacity : (d + 1) * capacity, :] = (taken * gate).astype(jnp.bfloat16)


def pick_outputs(block, capacity):
    tokens, width = block.shape
    pieces = [((capacity, width), jnp.bfloat16)] * PLANE
    return [((PLANE * capacity, tokens), jnp.bfloat16)] + pieces


def settle(hidden, own, others, gain, routes, router, sizes):
    ring, top, capacity = sizes

    def kernel(*refs):
        hidden_ref, own_ref = refs[:2]
        other_refs = refs[2 : 2 + len(others)]
        gain_ref, routes_ref, router_ref = refs[2 + len(others) : 5 + len(others)]
        residual_ref, normed_ref, scaled_ref, *outs = refs[5 + len(others) :]
        total = own_ref[...]
        for ref in other_refs:
            total = total + ref[...].astype(jnp.float32)
        residual = (hidden_ref[...].astype(jnp.float32) + total).astype(jnp.bfloat16)
        residual_ref[...] = residual
        normed = norm_rows(residual, gain_ref[...])
        normed_ref[...] = normed
        pick_rows(0, ring, top, normed, routes_ref, router_ref, scaled_ref, outs)

    outputs = [(hidden.shape, jnp.bfloat16)] * 2 + pick_outputs(hidden, capacity)
    inputs = [hidden, own, *others, gain, routes, router]
    residual, normed, scaled, *pieces = call(kernel, "settle", inputs, outputs, 10_000_000_000)
    return residual, normed, scaled, pieces


def turn(step, block, arrived, results, routes, router, sizes, ready):
    ring, top, capacity = sizes
    inputs = []
    outputs = []
    width = arrived[0].shape[1]
    rows = 0
    if block is not None:
        inputs += [block, routes, router]
        outputs.append(((PLANE * capacity, block.shape[0]), jnp.bfloat16))
        rows += capacity
    if results is not None:
        inputs += results
        rows += capacity
    joining = step <= ring
    if joining:
        inputs += arrived
        outputs.append(((PLANE * capacity, width), jnp.bfloat16))
    count = len(inputs)
    outputs += [((rows, width), jnp.bfloat16)] * PLANE

    def kernel(*refs):
        taken = list(refs[:count])
        given = list(refs[count:])
        outs = given[-PLANE:]
        at = 0
        if block is not None:
            block_ref, routes_ref, router_ref = taken[:3]
            taken = taken[3:]
            parts = [out.at[pl.ds(0, capacity), :] for out in outs]
            values = block_ref[...]
            pick_rows(step, ring, top, values, routes_ref, router_ref, given.pop(0), parts)
            at = capacity
        if results is not None:
            total = taken[0][...]
            for ref in taken[1 : len(results)]:
                total = total + ref[...].astype(jnp.float32)
            taken = taken[len(results) :]
            total = total.astype(jnp.bfloat16)
            for d, out in enumerate(outs):
                out[at : at + capacity, :] = total[d * capacity : (d + 1) * capacity]
        if joining:
            joined_ref = given.pop(0)
            for d, ref in enumerate(taken):
                joined_ref[d * capacity : (d + 1) * capacity, :] = ref[:capacity, :]

    found = list(call(kernel, "turn", inputs, outputs, 70_000_000, ready=ready))
    scaled = found.pop(0) if block is not None else None
    joined = found.pop(0) if joining else None
    return scaled, joined, found


def expert_kernel(count, kept, depth_steps, *refs):
    row_refs = refs[:count]
    gate_ref, up_ref, down_ref, own_ref, other_ref, flag_ref, *scratch = refs[count:]
    rows, gate_sum, up_sum, hidden = scratch
    flag_ref[...] = jnp.zeros_like(flag_ref)
    step = pl.program_id(0)
    depth = gate_ref.shape[1]

    @pl.when(step == 0)
    def prepare():
        at = 0
        for ref in row_refs:
            size = ref.shape[0]
            for i in range(depth_steps):
                rows[i, at : at + size, :] = ref[:, i * depth : (i + 1) * depth]
            at += size

    @pl.when(step < depth_steps)
    def widen():
        part = rows[jnp.minimum(step, depth_steps - 1)]
        gate_part = dot_t(part, gate_ref[...])
        up_part = dot_t(part, up_ref[...])

        @pl.when(step == 0)
        def first():
            gate_sum[...] = gate_part
            up_sum[...] = up_part

        @pl.when(step > 0)
        def later():
            gate_sum[...] += gate_part
            up_sum[...] += up_part

    @pl.when(step == depth_steps - 1)
    def activate():
        hidden[...] = (jax.nn.silu(gate_sum[...]) * up_sum[...]).astype(jnp.bfloat16)

    @pl.when(step >= depth_steps)
    def narrow():
        own_ref[...] = dot_f(hidden[:kept, :], down_ref[...])
        other_ref[...] = dot_f(hidden[kept:, :], down_ref[...]).astype(jnp.bfloat16)


def expert_apply(pieces, kept, gate_part, up_part, down_part, ready):
    steps = 2
    total = sum(piece.shape[0] for piece in pieces)
    units, width = gate_part.shape
    depth = width // steps
    return pl.pallas_call(
        after(functools.partial(expert_kernel, len(pieces), kept, steps), len(ready)),
        grid=(2 * steps,),
        in_specs=unread(ready)
        + [whole(piece) for piece in pieces]
        + [
            pl.BlockSpec((units, depth), lambda i: (0, jnp.minimum(i, steps - 1))),
            pl.BlockSpec((units, depth), lambda i: (0, jnp.minimum(i, steps - 1))),
            pl.BlockSpec((units, depth), lambda i: (0, jnp.maximum(i - steps, 0))),
        ],
        out_specs=[
            pl.BlockSpec((kept, depth), lambda i: (0, jnp.maximum(i - steps, 0))),
            pl.BlockSpec((total - kept, depth), lambda i: (0, jnp.maximum(i - steps, 0))),
            pl.BlockSpec((8, 128), lambda i: (0, 0)),
        ],
        out_shape=[
            jax.ShapeDtypeStruct((kept, width), jnp.float32),
            jax.ShapeDtypeStruct((total - kept, width), jnp.bfloat16),
            jax.ShapeDtypeStruct((8, 128), jnp.float32),
        ],
        scratch_shapes=[
            pltpu.VMEM((steps, total, depth), jnp.bfloat16),
            pltpu.VMEM((total, units), jnp.float32),
            pltpu.VMEM((total, units), jnp.float32),
            pltpu.VMEM((total, units), jnp.bfloat16),
        ],
        compiler_params=pltpu.CompilerParams(vmem_limit_bytes=24 * 1024 * 1024),
        cost_estimate=pl.CostEstimate(
            flops=6 * total * width * units, bytes_accessed=10_000_000, transcendentals=0
        ),
        name="experts",
    )(*ready, *pieces, gate_part, up_part, down_part)


def scatter_sum(scaled_ref, piece_refs, running_ref):
    size = scaled_ref.shape[0] // PLANE
    parts = [ref[ref.shape[0] - size :, :] for ref in piece_refs]
    returned = jnp.concatenate(parts, axis=0)
    total = lax.dot_general(
        scaled_ref[...], returned, (((0,), (0,)), ((), ())), preferred_element_type=jnp.float32
    )
    if running_ref is not None:
        total = total + running_ref[...].astype(jnp.float32)
    return total


def collect(scaled, pieces, running):
    extra = [] if running is None else [running]

    def kernel(scaled_ref, *refs):
        running_ref = refs[len(pieces)] if extra else None
        total = scatter_sum(scaled_ref, refs[: len(pieces)], running_ref)
        refs[-1][...] = total.astype(jnp.bfloat16)

    shape = (scaled.shape[1], pieces[0].shape[1])
    inputs = [scaled, *pieces, *extra]
    return call(kernel, "collect", inputs, [(shape, jnp.bfloat16)], 35_000_000)[0]


def conclude(scaled, pieces, running, residual, gain):
    extra = [] if running is None else [running]

    def kernel(residual_ref, gain_ref, scaled_ref, *refs):
        running_ref = refs[len(pieces)] if extra else None
        total = scatter_sum(scaled_ref, refs[: len(pieces)], running_ref)
        layer = (residual_ref[...].astype(jnp.float32) + total).astype(jnp.bfloat16)
        refs[-2][...] = layer
        refs[-1][...] = norm_rows(layer, gain_ref[...])

    inputs = [residual, gain, scaled, *pieces, *extra]
    return call(kernel, "conclude", inputs, [(residual.shape, jnp.bfloat16)] * 2, 35_000_000)


def per_device(
    hidden_in,
    queries,
    suffix_latent,
    prefix_latent,
    key_up,
    value_up,
    output_weight,
    norm_gain,
    router,
    expert_gate,
    expert_up,
    expert_down,
    next_gain,
    next_query_weight,
    next_latent_weight,
    suffix_lengths,
    request_tenant,
    tenant_lengths,
    page_table,
    routes,
):
    tok_slice = hidden_in.shape[0]
    groups = lax.axis_size("group")
    ring = lax.axis_size("tensor") // PLANE
    tok_quarter = tok_slice // groups
    expert_count = router.shape[1]
    top_count = routes.shape[2]
    capacity = max(2, 4 * tok_quarter * top_count // (3 * expert_count))
    capacity = -(-capacity // 16) * 16

    real_rows = prefix_latent.shape[0]
    piece_rows = -(-real_rows // 16) * 16
    piece = prefix_latent
    if piece_rows != real_rows:
        piece = jnp.pad(piece, ((0, piece_rows - real_rows), (0, 0)))
    routes_columns = jnp.transpose(routes, (2, 0, 1))
    full, lite = join_share(piece, suffix_latent.T, routes_columns, tok_quarter)
    along = [send_round(full, PLANE)] + [send_round(lite, PLANE * k) for k in range(2, ring)]
    column, plane, routes_ring = join_column([full, *along], piece_rows, tok_quarter)
    plane = [send_plane(part, d + 1) for d, part in enumerate(plane)]
    near_blocks = [send_group(column, j) if j else column for j in range(groups)]

    near_segments = []
    far_segments = []
    for k in range(ring):
        near_segments.append((k, piece_rows, real_rows, 0))
        far_segments.append((k, piece_rows, real_rows, 0))
        if k < 2:
            near_segments.append((k, tok_quarter, 0, 1))
    far_segments.append((0, tok_quarter, 0, 2))
    sides = (
        ((0,), near_segments),
        (range(1, PLANE - 1), far_segments),
        ((PLANE - 1,), far_segments),
    )
    tables = [jnp.asarray(key_table(groups, side, parts)) for side, parts in sides]
    tokens_info, permutation, near_spots, mid_spots, far_spots = make_plan(
        tables,
        suffix_lengths,
        request_tenant,
        tenant_lengths,
        page_table[None, :],
        ring,
        real_rows,
        (tok_slice, tok_quarter, groups),
        [full],
    )

    *near, near_flag = attend_near(
        tokens_info, near_spots, permutation, queries, key_up, near_blocks, [column]
    )
    beside = pass_on(plane[:-1], [near_flag])
    mid_blocks = [send_group(block, j) if j else block for j in range(groups) for block in beside]
    *mid, mid_flag = attend_mid(tokens_info, mid_spots, near, mid_blocks)
    near = [near[0], *mid]
    across = pass_on(plane[-1:], [mid_flag])[0]
    far_blocks = [send_group(across, j) if j else across for j in range(groups)]
    attend_own, attend_other = attend_far(
        tokens_info, far_spots, near, value_up, output_weight, far_blocks, tok_quarter
    )

    hidden_own = dot_f(permutation[:tok_quarter], hidden_in).astype(jnp.bfloat16)
    others = [
        send_group(attend_other[(j - 1) * tok_quarter : j * tok_quarter], j)
        for j in range(1, groups)
    ]
    sizes = (ring, top_count, capacity)
    experts_columns = router.T
    residual, block, scaled, pieces = settle(
        hidden_own,
        attend_own,
        others,
        norm_gain[None, :],
        routes_ring,
        experts_columns,
        sizes,
    )

    kept = PLANE * capacity
    gate_part = jnp.transpose(expert_gate, (0, 2, 1))[0]
    up_part = jnp.transpose(expert_up, (0, 2, 1))[0]
    down_part = expert_down[0]
    scales = [scaled]
    results = []
    running = None
    payload = pieces
    for step in range(1, ring + 4):
        arrived = [send_plane(piece, d) if d else piece for d, piece in enumerate(payload)]
        if step <= ring - 1:
            block = send_ring(block, ring)
        if 4 <= step:
            k = step - 3
            if k < ring:
                landed = running
                total = collect(scales[k], arrived, running)
                running = send_ring(total, ring)
            else:
                break
        back = step - 2 if step - 2 < ring else 0
        given = None
        if step >= 3:
            own, other, _ = results[back]
            if back:
                along_z = [block] if step <= ring - 1 else [landed] if step > 4 else []
                other = pass_on([other], arrived[1:] + along_z)[0]
            given = [own] + [
                send_group(other[(j - 1) * kept : j * kept], j) for j in range(1, groups)
            ]
        ready = [results[step - 2][2]] if 2 <= step <= ring else []
        scaled, joined, payload = turn(
            step,
            block if step <= ring - 1 else None,
            arrived,
            given,
            routes_ring,
            experts_columns,
            sizes,
            ready if step <= ring else [total],
        )
        if scaled is not None:
            scales.append(scaled)
        if joined is not None:
            rows = [send_group(joined, j) if j else joined for j in range(groups)]
            results.append(expert_apply(rows, kept, gate_part, up_part, down_part, []))
    layer_rows, normed_next = conclude(
        scales[0], arrived, running, residual, next_gain[None, :]
    )

    shares = [send_group(normed_next, j) if j else normed_next for j in range(groups)]
    gathered = lax.dot_general(
        permutation,
        jnp.concatenate(shares, axis=0),
        (((0,), (0,)), ((), ())),
        preferred_element_type=jnp.float32,
    ).astype(jnp.bfloat16)
    next_queries = dot_f(gathered, next_query_weight).astype(jnp.bfloat16)
    next_latent = dot_f(gathered, next_latent_weight).astype(jnp.bfloat16)
    return (layer_rows[:, None, :], next_queries, next_latent)


def solution(mesh):
    return jax.shard_map(
        per_device,
        mesh=mesh,
        in_specs=(
            P("tensor", None),
            P("tensor", "group"),
            P("tensor", None),
            P(("group", "tensor"), None),
            P("group", None, None),
            P("group", None, None),
            P("group", None),
            P(),
            P(),
            P("tensor", None, "group"),
            P("tensor", None, "group"),
            P("tensor", "group", None),
            P(),
            P(None, "group"),
            P(None, "group"),
            P(),
            P(),
            P(),
            P(),
            P(None, "tensor", None),
        ),
        out_specs=(P("tensor", "group", None), P("tensor", "group"), P("tensor", "group")),
        check_vma=False,
    )
```

```python
import functools
import math

import jax
import jax.numpy as jnp
import numpy as np
from jax import lax
from jax.experimental import pallas as pl
from jax.experimental.pallas import tpu as pltpu
from jax.sharding import PartitionSpec as P

NOPE = 128
ROPE = 64
LAT = 512
PAGE = 8
PLANE = 4
ROUTE_ROWS = 16
WIDE = 640

VERY_NEGATIVE = -1e30
ROUTE_SCALING = 2.446
NORM_EPSILON = 1e-06


def ring_order(count):
    odd = list(range(1, count, 2))
    even = list(range(2, count, 2))
    return [0] + odd + even[::-1]


def send_ring(block, count, steps=1):
    order = ring_order(count)
    after = {order[i]: order[(i + steps) % count] for i in range(count)}
    route = [
        (z * PLANE + p, after[z] * PLANE + p) for z in range(count) for p in range(PLANE)
    ]
    return lax.ppermute(block, "tensor", route)


def send_round(block, distance):
    count = lax.axis_size("tensor")
    return lax.ppermute(block, "tensor", [(i, (i + distance) % count) for i in range(count)])


def send_plane(block, distance):
    devices = range(lax.axis_size("tensor"))
    return lax.ppermute(block, "tensor", [(i, i ^ distance) for i in devices])


def send_pieces(pieces):
    sent = {d: send_plane(pieces[d], d) for d in reversed(range(1, PLANE))}
    return [pieces[0]] + [sent[d] for d in range(1, PLANE)]


def send_group(block, distance):
    devices = range(lax.axis_size("group"))
    return lax.ppermute(block, "group", [(i, i ^ distance) for i in devices])


def norm_rows(row_block, gain_vector):
    values = row_block.astype(jnp.float32)
    mean_square = jnp.mean(values * values, axis=-1, keepdims=True)
    return (
        values * lax.rsqrt(mean_square + NORM_EPSILON) * gain_vector.astype(jnp.float32)
    ).astype(jnp.bfloat16)


def dot_t(left, right):
    return lax.dot_general(
        left, right, (((1,), (1,)), ((), ())), preferred_element_type=jnp.float32
    )


def dot_f(left, right):
    return jnp.dot(left, right, preferred_element_type=jnp.float32)


def whole(array):
    return pl.BlockSpec(array.shape, lambda *i: (0,) * len(array.shape))


def after(kernel, count):
    def inner(*refs):
        kernel(*refs[count:])

    return inner


def resident(arrays):
    return [pl.BlockSpec(memory_space=pltpu.VMEM) for _ in arrays]


def unread(arrays):
    return [pl.BlockSpec(memory_space=pl.ANY) for _ in arrays]


def call(kernel, name, inputs, outputs, flops, limit=12, ready=(), streamed=False):
    shapes = [jax.ShapeDtypeStruct(shape, dtype) for shape, dtype in outputs]
    moved = sum(a.size * a.dtype.itemsize for a in list(inputs) + shapes)
    if streamed:
        places = {
            "grid": (1,),
            "in_specs": unread(ready) + [whole(a) for a in inputs],
            "out_specs": [whole(shape) for shape in shapes],
        }
    else:
        places = {
            "in_specs": unread(ready) + resident(inputs),
            "out_specs": resident(shapes),
        }
    return pl.pallas_call(
        after(kernel, len(ready)),
        **places,
        out_shape=shapes,
        compiler_params=pltpu.CompilerParams(vmem_limit_bytes=limit * 1024 * 1024),
        cost_estimate=pl.CostEstimate(flops=flops, bytes_accessed=moved, transcendentals=0),
        name=name,
    )(*ready, *inputs)


def join_share(piece, suffix_columns, routes_columns, tok_quarter):
    rows = piece.shape[0]
    tokens = suffix_columns.shape[1]
    top, groups, _ = routes_columns.shape

    def kernel(piece_ref, suffix_ref, routes_ref, full_ref, lite_ref):
        group_index = lax.axis_index("group")
        shape = (tok_quarter, tokens)
        row = lax.broadcasted_iota(jnp.int32, shape, 0)
        token = lax.broadcasted_iota(jnp.int32, shape, 1)
        select = jnp.where(token == group_index * tok_quarter + row, 1.0, 0.0)
        share = dot_t(select.astype(jnp.bfloat16), suffix_ref[...]).astype(jnp.bfloat16)
        named = jnp.zeros((top, tok_quarter), jnp.float32)
        for j in range(groups):
            part = routes_ref[:, j, :].astype(jnp.float32)
            named = jnp.where(group_index == j, part, named)
        named = jnp.concatenate([named, jnp.zeros((rows - top, tok_quarter), jnp.float32)], axis=0)
        spare = WIDE - LAT - ROPE - tok_quarter
        if spare:
            named = jnp.concatenate([named, jnp.zeros((rows, spare), jnp.float32)], axis=1)
        named = named.astype(jnp.bfloat16)
        piece = piece_ref[...]
        last = jnp.concatenate([piece[:, LAT:], named], axis=1)
        for ref in (full_ref, lite_ref):
            ref[:rows, :LAT] = piece[:, :LAT]
            ref[:rows, LAT:] = last
        empty = jnp.zeros((tok_quarter, WIDE - LAT - ROPE), jnp.bfloat16)
        full_ref[rows:, :LAT] = share[:, :LAT]
        full_ref[rows:, LAT:] = jnp.concatenate([share[:, LAT:], empty], axis=1)

    outputs = [((size, WIDE), piece.dtype) for size in (rows + tok_quarter, rows)]
    inputs = [piece, suffix_columns, routes_columns]
    return call(kernel, "join_share", inputs, outputs, 10_000_000, limit=58, streamed=True)


def join_column(blocks, rows, share, ready):
    count = len(blocks)

    def kernel(*refs):
        block_refs = refs[:count]
        near_ref, *far_refs, routes_ref = refs[count:]
        plane_index = lax.rem(lax.axis_index("tensor"), PLANE)
        at = 0
        for i, ref in enumerate(block_refs):
            near_ref[at : at + ref.shape[0], :] = ref[...]
            at += ref.shape[0]
            routes_ref[i] = ref[:ROUTE_ROWS, LAT:]
        here = block_refs[0][rows:, :].astype(jnp.float32)
        before = block_refs[1][rows:, :].astype(jnp.float32)
        for d, far_ref in enumerate(far_refs):
            if d < PLANE - 2:
                for i, ref in enumerate(block_refs):
                    far_ref[i * rows : (i + 1) * rows, :] = ref[:rows, :]
            later = plane_index < lax.bitwise_xor(plane_index, d + 1)
            part = jnp.where(later, here, before).astype(jnp.bfloat16)
            far_ref[far_ref.shape[0] - share :, :] = part

    dtype = blocks[0].dtype
    outputs = [((count * rows + 2 * share, WIDE), dtype)]
    outputs += [((count * rows + share, WIDE), dtype)] * (PLANE - 2)
    outputs.append(((share, WIDE), dtype))
    outputs.append(((count, ROUTE_ROWS, WIDE - LAT), dtype))
    near, *far, routes = call(kernel, "join_column", blocks, outputs, 0, ready=ready)
    return near, far, routes


def halves(by_y, by_x, rows):
    def kernel(by_y_ref, by_x_ref, first_ref, second_ref):
        first_ref[...] = by_y_ref[:rows, :]
        second_ref[...] = by_x_ref[rows : 2 * rows, :]

    outputs = [((rows, WIDE), by_y.dtype)] * 2
    return call(kernel, "halves", [by_y, by_x], outputs, 0)


def pass_on(blocks, ready):
    first = len(ready)

    def kernel(*refs):
        pass

    return pl.pallas_call(
        kernel,
        in_specs=unread(ready) + unread(blocks),
        out_specs=unread(blocks),
        out_shape=[jax.ShapeDtypeStruct(block.shape, block.dtype) for block in blocks],
        input_output_aliases={first + i: i for i in range(len(blocks))},
        compiler_params=pltpu.CompilerParams(vmem_limit_bytes=1024 * 1024),
        name="pass_on",
    )(*ready, *blocks)


LATER = 1 << 20


def key_table(groups, sides):
    rows = []
    for j in range(groups):
        for d, segments in sides:
            for k, count, real, suffix in segments:
                rows += [(j, d, k, r, suffix, r < real) for r in range(count)]
    table = np.zeros((8, len(rows)), np.int32)
    table[:6] = np.array(rows, np.int32).T
    table[6] = table[3] // PAGE
    table[7] = table[3] % PAGE
    return table


def make_plan(tables, lengths, tenants, tenant_lengths, page_table, ring, piece_rows, sizes, ready):
    tok_slice, tok_quarter, groups = sizes
    requests = lengths.shape[0]
    tenant_count = tenant_lengths.shape[0]
    pages = page_table.shape[1]
    piece_pages = piece_rows // PAGE

    def spots_of(table, page_row, group_index, ring_index, plane_index):
        j, d, k, r, suffix, real, page_at, within = (table[i : i + 1, :] for i in range(8))
        in_plane = lax.bitwise_xor(plane_index, d)
        k = jnp.where(suffix == 2, jnp.where(in_plane < plane_index, 0, 1), k)
        from_ring = ring_index - k
        from_ring = jnp.where(from_ring < 0, from_ring + ring, from_ring)
        of_group = lax.bitwise_xor(group_index, j)
        owner = (of_group * ring + from_ring) * PLANE + in_plane
        index = owner * piece_pages + page_at
        count = table.shape[1]
        page = lax.broadcasted_iota(jnp.int32, (pages, count), 0)
        hit = jnp.where(page == index, 1.0, 0.0).astype(jnp.bfloat16)
        found = dot_f(page_row, hit)[:1].astype(jnp.int32)
        logical = jnp.where(real > 0, found * PAGE + within, -1)
        token = (from_ring * PLANE + in_plane) * tok_slice + of_group * tok_quarter + r
        return jnp.where(suffix > 0, token + LATER, logical)

    def kernel(lengths_ref, tenants_ref, tenant_lengths_ref, page_ref, *refs):
        table_refs = refs[: len(tables)]
        info_ref, order_ref, *spot_refs = refs[len(tables) :]
        group_index = jnp.full((1, 1), lax.axis_index("group"), jnp.int32)
        tensor_index = lax.axis_index("tensor")
        ring_index = jnp.full((1, 1), lax.div(tensor_index, PLANE), jnp.int32)
        plane_index = jnp.full((1, 1), lax.rem(tensor_index, PLANE), jnp.int32)
        page_row = page_ref[...].astype(jnp.float32).astype(jnp.bfloat16)
        page_row = jnp.broadcast_to(page_row, (16, pages))
        for table_ref, spot_ref in zip(table_refs, spot_refs):
            spot_ref[...] = spots_of(
                table_ref[...], page_row, group_index, ring_index, plane_index
            )
        row = lax.broadcasted_iota(jnp.int32, (tok_slice, 1), 0)
        share = jnp.zeros((tok_slice, 1), jnp.int32)
        for j in range(1, groups):
            share = share + jnp.where(row >= j * tok_quarter, 1, 0)
        local = (row - share * tok_quarter) * groups + lax.bitwise_xor(group_index, share)
        column = lax.broadcasted_iota(jnp.int32, (tok_slice, tok_slice), 1)
        order_ref[...] = jnp.where(column == local, 1.0, 0.0).astype(jnp.bfloat16)
        position = local + tensor_index * tok_slice
        low = jnp.zeros((tok_slice, 1), jnp.int32)
        high = jnp.zeros((tok_slice, 1), jnp.int32)
        start = jnp.zeros((tok_slice, 1), jnp.int32)
        begin = 0
        for i in range(requests):
            end = begin + lengths_ref[i]
            inside = (position >= begin) & (position < end)
            tenant = tenants_ref[i]
            first = 0
            tenant_low = 0
            tenant_high = 0
            for t in range(tenant_count):
                last = first + tenant_lengths_ref[t]
                tenant_low = jnp.where(tenant == t, first, tenant_low)
                tenant_high = jnp.where(tenant == t, last, tenant_high)
                first = last
            start = jnp.where(inside, begin, start)
            low = jnp.where(inside, tenant_low, low)
            high = jnp.where(inside, tenant_high, high)
            begin = end
        for i, value in enumerate((low, high, start + LATER, position + LATER)):
            info_ref[:, i : i + 1] = value

    shapes = [
        jax.ShapeDtypeStruct((tok_slice, 4), jnp.int32),
        jax.ShapeDtypeStruct((tok_slice, tok_slice), jnp.bfloat16),
    ] + [jax.ShapeDtypeStruct((1, table.shape[1]), jnp.int32) for table in tables]
    scalar = pl.BlockSpec(memory_space=pltpu.SMEM)
    arrays = [page_table, *tables]
    return pl.pallas_call(
        after(kernel, len(ready)),
        grid=(1,),
        in_specs=unread(ready) + [scalar, scalar, scalar] + [whole(a) for a in arrays],
        out_specs=[whole(shape) for shape in shapes],
        out_shape=shapes,
        compiler_params=pltpu.CompilerParams(vmem_limit_bytes=58 * 1024 * 1024),
        cost_estimate=pl.CostEstimate(
            flops=4_000_000_000, bytes_accessed=1_000_000, transcendentals=0
        ),
        name="make_plan",
    )(*ready, lengths, tenants, tenant_lengths, *arrays)


def place_keys(key_refs, spot_ref, token_ref, keys, bias):
    at = 0
    for ref in key_refs:
        rows = ref.shape[0]
        keys[at : at + rows, :] = ref[...]
        at += rows
    columns = token_ref[...]
    spots = spot_ref[...]
    low, high, start, here = (columns[:, i : i + 1] for i in range(4))
    seen = ((spots >= low) & (spots < high)) | ((spots >= start) & (spots <= here))
    bias[...] = jnp.where(seen, 0.0, VERY_NEGATIVE)


SCORE_FACTOR = math.log2(math.e) / math.sqrt(NOPE + ROPE)


def score_rows(queries, keys, bias, pair):
    scores = dot_t(queries, keys[...])
    rows, count = scores.shape
    return (scores.reshape(pair, rows // pair, count) + bias[...][None]).reshape(rows, count)


def near_kernel(block_count, pair, token_ref, spot_ref, order_ref, query_ref, key_up_ref, *refs):
    key_refs = refs[:block_count]
    wide_ref, best_ref, sum_ref, acc_ref, flag_ref, keys, bias = refs[block_count:]
    flag_ref[...] = jnp.zeros_like(flag_ref)
    tokens = query_ref.shape[0]
    place_keys(key_refs, spot_ref, token_ref, keys, bias)
    queries = dot_f(order_ref[...], query_ref[...]).astype(jnp.bfloat16)
    size = NOPE + ROPE
    empty = jnp.zeros((tokens, WIDE - LAT - ROPE), jnp.bfloat16)
    for first in range(0, key_up_ref.shape[0], pair):
        wide = []
        for h in range(first, first + pair):
            part = queries[:, h * size : (h + 1) * size]
            content = dot_f(part[:, :NOPE], key_up_ref[h]).astype(jnp.bfloat16)
            wide.append(jnp.concatenate([content, part[:, NOPE:], empty], axis=1))
        wide = jnp.concatenate(wide, axis=0)
        here = pl.ds(first * tokens, pair * tokens)
        wide_ref[here, :] = wide
        masked = score_rows(wide, keys, bias, pair)
        best = jnp.max(masked, axis=-1, keepdims=True)
        weights = jnp.exp2((masked - best) * SCORE_FACTOR)
        best_ref[here, :] = best
        sum_ref[here, :] = jnp.sum(weights, axis=-1, keepdims=True)
        acc_ref[here, :] = dot_f(weights.astype(jnp.bfloat16), keys[:, :LAT])


def attend_call(kernel, name, inputs, outputs, scratch, work, limit=24):
    shapes = [jax.ShapeDtypeStruct(shape, dtype) for shape, dtype in outputs]
    return pl.pallas_call(
        kernel,
        in_specs=resident(inputs),
        out_specs=resident(shapes),
        out_shape=shapes,
        scratch_shapes=scratch,
        compiler_params=pltpu.CompilerParams(vmem_limit_bytes=limit * 1024 * 1024),
        cost_estimate=pl.CostEstimate(
            flops=work, bytes_accessed=8_000_000, transcendentals=work // 2176
        ),
        name=name,
    )(*inputs)


def key_scratch(tokens, blocks):
    count = sum(block.shape[0] for block in blocks)
    return [pltpu.VMEM((count, WIDE), jnp.bfloat16), pltpu.VMEM((tokens, count), jnp.float32)]


def attend_near(tokens_info, spots, order, queries, key_up, blocks):
    tokens = queries.shape[0]
    heads = key_up.shape[0]
    rows = heads * tokens
    outputs = [
        ((rows, WIDE), jnp.bfloat16),
        ((rows, 1), jnp.float32),
        ((rows, 1), jnp.float32),
        ((rows, LAT), jnp.float32),
        ((8, 128), jnp.float32),
    ]
    return attend_call(
        functools.partial(near_kernel, len(blocks), min(4, heads)),
        "attend_near",
        [tokens_info, spots, order, queries, key_up, *blocks],
        outputs,
        key_scratch(tokens, blocks),
        2 * rows * spots.shape[1] * (LAT + ROPE + LAT),
    )


def add_keys(here, wide_ref, best_ref, sum_ref, acc_ref, keys, bias, pair):
    masked = score_rows(wide_ref[here, :], keys, bias, pair)
    before = best_ref[here, :]
    best = jnp.maximum(before, jnp.max(masked, axis=-1, keepdims=True))
    factor = jnp.exp2((before - best) * SCORE_FACTOR)
    weights = jnp.exp2((masked - best) * SCORE_FACTOR)
    weight_sum = sum_ref[here, :] * factor + jnp.sum(weights, axis=-1, keepdims=True)
    attended = acc_ref[here, :] * factor + dot_f(weights.astype(jnp.bfloat16), keys[:, :LAT])
    return best, weight_sum, attended


def mid_kernel(block_count, pair, token_ref, spot_ref, wide_ref, best_ref, sum_ref, acc_ref, *refs):
    key_refs = refs[:block_count]
    new_best_ref, new_sum_ref, new_acc_ref, flag_ref, keys, bias = refs[block_count:]
    flag_ref[...] = jnp.zeros_like(flag_ref)
    place_keys(key_refs, spot_ref, token_ref, keys, bias)
    rows = pair * token_ref.shape[0]
    for first in range(0, wide_ref.shape[0], rows):
        here = pl.ds(first, rows)
        new_best_ref[here, :], new_sum_ref[here, :], new_acc_ref[here, :] = add_keys(
            here, wide_ref, best_ref, sum_ref, acc_ref, keys, bias, pair
        )


def attend_mid(tokens_info, spots, near, blocks):
    tokens = tokens_info.shape[0]
    rows = near[0].shape[0]
    outputs = [
        ((rows, 1), jnp.float32),
        ((rows, 1), jnp.float32),
        ((rows, LAT), jnp.float32),
        ((8, 128), jnp.float32),
    ]
    return attend_call(
        functools.partial(mid_kernel, len(blocks), min(4, rows // tokens)),
        "attend_mid",
        [tokens_info, spots, *near, *blocks],
        outputs,
        key_scratch(tokens, blocks),
        2 * rows * spots.shape[1] * (LAT + ROPE + LAT),
    )


def far_kernel(
    block_count,
    pair,
    token_ref,
    spot_ref,
    wide_ref,
    best_ref,
    sum_ref,
    acc_ref,
    value_up_ref,
    output_ref,
    *refs,
):
    key_refs = refs[:block_count]
    own_ref, other_ref, keys, bias = refs[block_count:]
    tokens = token_ref.shape[0]
    rows = pair * tokens
    place_keys(key_refs, spot_ref, token_ref, keys, bias)
    heads = []
    for first in range(0, wide_ref.shape[0], rows):
        _, weight_sum, attended = add_keys(
            pl.ds(first, rows), wide_ref, best_ref, sum_ref, acc_ref, keys, bias, pair
        )
        attended = (attended / weight_sum).astype(jnp.bfloat16)
        for h in range(pair):
            part = attended[h * tokens : (h + 1) * tokens]
            value = value_up_ref[first // tokens + h]
            heads.append(dot_f(part, value).astype(jnp.bfloat16))
    total = dot_f(jnp.concatenate(heads, axis=1), output_ref[...])
    mine = own_ref.shape[0]
    own_ref[...] = total[:mine]
    other_ref[...] = total[mine:].astype(jnp.bfloat16)


def attend_far(tokens_info, spots, near, value_up, output_weight, blocks, tok_quarter):
    tokens = tokens_info.shape[0]
    heads = value_up.shape[0]
    width = output_weight.shape[1]
    outputs = [
        ((tok_quarter, width), jnp.float32),
        ((tokens - tok_quarter, width), jnp.bfloat16),
    ]
    return attend_call(
        functools.partial(far_kernel, len(blocks), min(4, heads)),
        "attend_far",
        [tokens_info, spots, *near, value_up, output_weight, *blocks],
        outputs,
        key_scratch(tokens, blocks),
        2 * heads * tokens * spots.shape[1] * (LAT + ROPE + LAT),
    )


def pick_rows(turn, ring, top, block, routes_ref, router_ref, scaled_ref, outs):
    tokens = block.shape[0]
    capacity = outs[0].shape[0]
    tensor_index = lax.axis_index("tensor")
    here = lax.div(tensor_index, PLANE)
    plane_index = lax.rem(tensor_index, PLANE)
    order = ring_order(ring)
    place = sum(jnp.where(here == z, i, 0) for i, z in enumerate(order))
    place = lax.rem(place - turn + ring, ring)
    source = sum(jnp.where(place == i, z, 0) for i, z in enumerate(order))
    routes = routes_ref[lax.rem(here - source + ring, ring)].astype(jnp.float32)
    routes = routes[:, ROPE : ROPE + tokens]
    targets = [
        (here * PLANE + lax.bitwise_xor(plane_index, d)).astype(jnp.float32)
        for d in range(PLANE)
    ]
    hits = [
        jnp.sum(jnp.where(routes[:top] == target, 1.0, 0.0), axis=0, keepdims=True)
        for target in targets
    ]
    before = lax.broadcasted_iota(jnp.int32, (tokens, tokens), 0)
    after_it = lax.broadcasted_iota(jnp.int32, (tokens, tokens), 1)
    earlier = jnp.where(before < after_it, 1.0, 0.0).astype(jnp.bfloat16)
    ranks = dot_f(jnp.concatenate(hits, axis=0).astype(jnp.bfloat16), earlier)
    count = router_ref.shape[0]
    expert = lax.broadcasted_iota(jnp.int32, (count, tokens), 0).astype(jnp.float32)
    named = jnp.zeros((count, tokens), jnp.float32)
    for i in range(top):
        named = named + jnp.where(expert == routes[i : i + 1], 1.0, 0.0)
    picked = jax.nn.sigmoid(dot_t(router_ref[...], block)) * named
    gates = picked / jnp.sum(picked, axis=0, keepdims=True) * ROUTE_SCALING
    slot = lax.broadcasted_iota(jnp.int32, (capacity, tokens), 0).astype(jnp.float32)
    for d, out in enumerate(outs):
        taken = jnp.where(slot == ranks[d : d + 1], hits[d], 0.0)
        out[...] = dot_f(taken.astype(jnp.bfloat16), block).astype(jnp.bfloat16)
        gate = jnp.sum(jnp.where(expert == targets[d], gates, 0.0), axis=0, keepdims=True)
        scaled_ref[d * capacity : (d + 1) * capacity, :] = (taken * gate).astype(jnp.bfloat16)


def pick_outputs(block, capacity):
    tokens, width = block.shape
    pieces = [((capacity, width), jnp.bfloat16)] * PLANE
    return [((PLANE * capacity, tokens), jnp.bfloat16)] + pieces


def settle(hidden, own, others, gain, routes, router, sizes):
    ring, top, capacity = sizes

    def kernel(*refs):
        hidden_ref, own_ref = refs[:2]
        other_refs = refs[2 : 2 + len(others)]
        gain_ref, routes_ref, router_ref = refs[2 + len(others) : 5 + len(others)]
        residual_ref, normed_ref, scaled_ref, *outs = refs[5 + len(others) :]
        total = own_ref[...]
        for ref in other_refs:
            total = total + ref[...].astype(jnp.float32)
        residual = (hidden_ref[...].astype(jnp.float32) + total).astype(jnp.bfloat16)
        residual_ref[...] = residual
        normed = norm_rows(residual, gain_ref[...])
        normed_ref[...] = normed
        pick_rows(0, ring, top, normed, routes_ref, router_ref, scaled_ref, outs)

    outputs = [(hidden.shape, jnp.bfloat16)] * 2 + pick_outputs(hidden, capacity)
    inputs = [hidden, own, *others, gain, routes, router]
    residual, normed, scaled, *pieces = call(kernel, "settle", inputs, outputs, 10_000_000_000)
    return residual, normed, scaled, pieces


def turn(step, block, arrived, results, routes, router, sizes, ready):
    ring, top, capacity = sizes
    inputs = []
    outputs = []
    width = arrived[0].shape[1]
    rows = 0
    if block is not None:
        inputs += [block, routes, router]
        outputs.append(((PLANE * capacity, block.shape[0]), jnp.bfloat16))
        rows += capacity
    if results is not None:
        inputs += results
        rows += capacity
    joining = step <= ring
    if joining:
        inputs += arrived
        outputs.append(((PLANE * capacity, width), jnp.bfloat16))
    count = len(inputs)
    outputs += [((rows, width), jnp.bfloat16)] * PLANE

    def kernel(*refs):
        taken = list(refs[:count])
        given = list(refs[count:])
        outs = given[-PLANE:]
        at = 0
        if block is not None:
            block_ref, routes_ref, router_ref = taken[:3]
            taken = taken[3:]
            parts = [out.at[pl.ds(0, capacity), :] for out in outs]
            values = block_ref[...]
            pick_rows(step, ring, top, values, routes_ref, router_ref, given.pop(0), parts)
            at = capacity
        if results is not None:
            total = taken[0][...]
            for ref in taken[1 : len(results)]:
                total = total + ref[...].astype(jnp.float32)
            taken = taken[len(results) :]
            total = total.astype(jnp.bfloat16)
            for d, out in enumerate(outs):
                out[at : at + capacity, :] = total[d * capacity : (d + 1) * capacity]
        if joining:
            joined_ref = given.pop(0)
            for d, ref in enumerate(taken):
                joined_ref[d * capacity : (d + 1) * capacity, :] = ref[:capacity, :]

    found = list(call(kernel, "turn", inputs, outputs, 70_000_000, ready=ready))
    scaled = found.pop(0) if block is not None else None
    joined = found.pop(0) if joining else None
    return scaled, joined, found


def expert_apply(pieces, kept, gate_part, up_part, down_part):
    total = sum(piece.shape[0] for piece in pieces)
    units, width = gate_part.shape

    def kernel(*refs):
        row_refs = refs[: len(pieces)]
        gate_ref, up_ref, down_ref, own_ref, other_ref, flag_ref = refs[len(pieces) :]
        flag_ref[...] = jnp.zeros_like(flag_ref)
        rows = jnp.concatenate([ref[...] for ref in row_refs], axis=0)
        gate_vals = dot_t(rows, gate_ref[...])
        up_vals = dot_t(rows, up_ref[...])
        hidden = (jax.nn.silu(gate_vals) * up_vals).astype(jnp.bfloat16)
        partial = dot_f(hidden, down_ref[...])
        own_ref[...] = partial[:kept]
        other_ref[...] = partial[kept:].astype(jnp.bfloat16)

    outputs = [
        ((kept, width), jnp.float32),
        ((total - kept, width), jnp.bfloat16),
        ((8, 128), jnp.float32),
    ]
    inputs = [*pieces, gate_part, up_part, down_part]
    return call(kernel, "experts", inputs, outputs, 6 * total * width * units, limit=20)


def scatter_sum(scaled_ref, piece_refs, running_ref):
    size = scaled_ref.shape[0] // PLANE
    parts = [ref[ref.shape[0] - size :, :] for ref in piece_refs]
    returned = jnp.concatenate(parts, axis=0)
    total = lax.dot_general(
        scaled_ref[...], returned, (((0,), (0,)), ((), ())), preferred_element_type=jnp.float32
    )
    if running_ref is not None:
        total = total + running_ref[...].astype(jnp.float32)
    return total


def collect(scaled, pieces, running):
    extra = [] if running is None else [running]

    def kernel(scaled_ref, *refs):
        running_ref = refs[len(pieces)] if extra else None
        total = scatter_sum(scaled_ref, refs[: len(pieces)], running_ref)
        refs[-1][...] = total.astype(jnp.bfloat16)

    shape = (scaled.shape[1], pieces[0].shape[1])
    inputs = [scaled, *pieces, *extra]
    return call(kernel, "collect", inputs, [(shape, jnp.bfloat16)], 35_000_000)[0]


def conclude(scaled, pieces, running, residual, gain):
    extra = [] if running is None else [running]

    def kernel(residual_ref, gain_ref, scaled_ref, *refs):
        running_ref = refs[len(pieces)] if extra else None
        total = scatter_sum(scaled_ref, refs[: len(pieces)], running_ref)
        layer = (residual_ref[...].astype(jnp.float32) + total).astype(jnp.bfloat16)
        refs[-2][...] = layer
        refs[-1][...] = norm_rows(layer, gain_ref[...])

    inputs = [residual, gain, scaled, *pieces, *extra]
    return call(kernel, "conclude", inputs, [(residual.shape, jnp.bfloat16)] * 2, 35_000_000)


def project(shares, order, query_weight, latent_rows):
    def kernel(order_ref, query_ref, latent_ref, *refs):
        share_refs = refs[: len(shares)]
        queries_ref, latents_ref = refs[len(shares) :]
        rows = jnp.concatenate([ref[...] for ref in share_refs], axis=0)
        rows = lax.dot_general(
            order_ref[...], rows, (((0,), (0,)), ((), ())), preferred_element_type=jnp.float32
        ).astype(jnp.bfloat16)
        latents_ref[...] = dot_t(latent_ref[...], rows).astype(jnp.bfloat16)
        queries_ref[...] = dot_f(rows, query_ref[...]).astype(jnp.bfloat16)

    tokens = order.shape[0]
    outputs = [
        ((tokens, query_weight.shape[1]), jnp.bfloat16),
        ((latent_rows.shape[0], tokens), jnp.bfloat16),
    ]
    inputs = [order, query_weight, latent_rows, *shares]
    return call(kernel, "project", inputs, outputs, 1_000_000_000, limit=16)


def per_device(
    hidden_in,
    queries,
    suffix_latent,
    prefix_latent,
    key_up,
    value_up,
    output_weight,
    norm_gain,
    router,
    expert_gate,
    expert_up,
    expert_down,
    next_gain,
    next_query_weight,
    next_latent_weight,
    suffix_lengths,
    request_tenant,
    tenant_lengths,
    page_table,
    routes,
):
    tok_slice = hidden_in.shape[0]
    groups = lax.axis_size("group")
    ring = lax.axis_size("tensor") // PLANE
    tok_quarter = tok_slice // groups
    expert_count = router.shape[1]
    top_count = routes.shape[2]
    capacity = max(2, 4 * tok_quarter * top_count // (3 * expert_count))
    capacity = -(-capacity // 16) * 16

    real_rows = prefix_latent.shape[0]
    piece_rows = -(-real_rows // 16) * 16
    piece = prefix_latent
    if piece_rows != real_rows:
        piece = jnp.pad(piece, ((0, piece_rows - real_rows), (0, 0)))
    routes_columns = jnp.transpose(routes, (2, 0, 1))
    full, lite = join_share(piece, suffix_latent.T, routes_columns, tok_quarter)
    along = [send_round(full, PLANE)] + [send_round(lite, PLANE * k) for k in range(2, ring)]
    near_segments = []
    far_segments = []
    for k in range(ring):
        near_segments.append((k, piece_rows, real_rows, 0))
        far_segments.append((k, piece_rows, real_rows, 0))
        if k < 2:
            near_segments.append((k, tok_quarter, 0, 1))
    far_segments.append((0, tok_quarter, 0, 2))
    sides = (
        [(0, near_segments)],
        [(1, far_segments), (2, far_segments)],
        [(3, far_segments)],
    )
    tables = [jnp.asarray(key_table(groups, side)) for side in sides]
    tokens_info, permutation, near_spots, mid_spots, far_spots = make_plan(
        tables,
        suffix_lengths,
        request_tenant,
        tenant_lengths,
        page_table[None, :],
        ring,
        real_rows,
        (tok_slice, tok_quarter, groups),
        [full],
    )

    column, plane, routes_ring = join_column(
        [full, *along], piece_rows, tok_quarter, [near_spots]
    )
    plane = send_pieces([column, *plane])[1:]
    near_blocks = [send_group(column, j) if j else column for j in range(groups)]

    *near, near_flag = attend_near(
        tokens_info, near_spots, permutation, queries, key_up, near_blocks
    )
    beside = pass_on(plane[:2], [near_flag])
    first, second = halves(beside[1], beside[0], ring * piece_rows // 2)
    across = [send_plane(first, 1), send_plane(second, 2)]
    mid_blocks = [send_group(block, j) if j else block for j in range(groups) for block in beside]
    *mid, mid_flag = attend_mid(tokens_info, mid_spots, near, mid_blocks)
    near = [near[0], *mid]
    across = pass_on([*across, plane[2]], [mid_flag])
    far_blocks = [send_group(block, j) if j else block for j in range(groups) for block in across]
    attend_own, attend_other = attend_far(
        tokens_info, far_spots, near, value_up, output_weight, far_blocks, tok_quarter
    )

    hidden_own = dot_f(permutation[:tok_quarter], hidden_in).astype(jnp.bfloat16)
    others = [
        send_group(attend_other[(j - 1) * tok_quarter : j * tok_quarter], j)
        for j in range(1, groups)
    ]
    sizes = (ring, top_count, capacity)
    experts_columns = router.T
    residual, block, scaled, pieces = settle(
        hidden_own,
        attend_own,
        others,
        norm_gain[None, :],
        routes_ring,
        experts_columns,
        sizes,
    )

    kept = PLANE * capacity
    gate_part = jnp.transpose(expert_gate, (0, 2, 1))[0]
    up_part = jnp.transpose(expert_up, (0, 2, 1))[0]
    down_part = expert_down[0]
    scales = [scaled]
    results = []
    running = None
    payload = pieces
    for step in range(1, ring + 4):
        if step <= ring - 1:
            block = send_ring(block, ring)
        arrived = send_pieces(payload)
        if 4 <= step:
            k = step - 3
            if k < ring:
                landed = running
                total = collect(scales[k], arrived, running)
                running = send_ring(total, ring)
            else:
                break
        back = step - 2 if step - 2 < ring else 0
        given = None
        if step >= 3:
            own, other, _ = results[back]
            if back:
                along_z = [block] if step <= ring - 1 else [landed] if step > 4 else []
                other = pass_on([other], arrived[1:] + along_z)[0]
            given = [own] + [
                send_group(other[(j - 1) * kept : j * kept], j) for j in range(1, groups)
            ]
        ready = [results[step - 2][2]] if 2 <= step <= ring else []
        scaled, joined, payload = turn(
            step,
            block if step <= ring - 1 else None,
            arrived,
            given,
            routes_ring,
            experts_columns,
            sizes,
            ready if step <= ring else [total],
        )
        if scaled is not None:
            scales.append(scaled)
        if joined is not None:
            rows = [send_group(joined, j) if j else joined for j in range(groups)]
            results.append(expert_apply(rows, kept, gate_part, up_part, down_part))
    layer_rows, normed_next = conclude(
        scales[0], arrived, running, residual, next_gain[None, :]
    )

    shares = [send_group(normed_next, j) if j else normed_next for j in range(groups)]
    next_queries, next_latent = project(
        shares, permutation, next_query_weight, next_latent_weight.T
    )
    return (layer_rows[:, None, :], next_queries, next_latent.T)


def solution(mesh):
    return jax.shard_map(
        per_device,
        mesh=mesh,
        in_specs=(
            P("tensor", None),
            P("tensor", "group"),
            P("tensor", None),
            P(("group", "tensor"), None),
            P("group", None, None),
            P("group", None, None),
            P("group", None),
            P(),
            P(),
            P("tensor", None, "group"),
            P("tensor", None, "group"),
            P("tensor", "group", None),
            P(),
            P(None, "group"),
            P(None, "group"),
            P(),
            P(),
            P(),
            P(),
            P(None, "tensor", None),
        ),
        out_specs=(P("tensor", "group", None), P("tensor", "group"), P("tensor", "group")),
        check_vma=False,
    )
```

```python
import functools
import math

import jax
import jax.numpy as jnp
import numpy as np
from jax import lax
from jax.experimental import pallas as pl
from jax.experimental.pallas import tpu as pltpu
from jax.sharding import PartitionSpec as P

NOPE = 128
ROPE = 64
LAT = 512
PAGE = 8
PLANE = 4
ROUTE_ROWS = 16
WIDE = 640

VERY_NEGATIVE = -1e30
ROUTE_SCALING = 2.446
NORM_EPSILON = 1e-06


def ring_order(count):
    odd = list(range(1, count, 2))
    even = list(range(2, count, 2))
    return [0] + odd + even[::-1]


def send_ring(block, count, steps=1):
    order = ring_order(count)
    after = {order[i]: order[(i + steps) % count] for i in range(count)}
    route = [
        (z * PLANE + p, after[z] * PLANE + p) for z in range(count) for p in range(PLANE)
    ]
    return lax.ppermute(block, "tensor", route)


def send_round(block, distance):
    count = lax.axis_size("tensor")
    return lax.ppermute(block, "tensor", [(i, (i + distance) % count) for i in range(count)])


def send_plane(block, distance):
    devices = range(lax.axis_size("tensor"))
    return lax.ppermute(block, "tensor", [(i, i ^ distance) for i in devices])


def send_pieces(pieces):
    sent = {d: send_plane(pieces[d], d) for d in reversed(range(1, PLANE))}
    return [pieces[0]] + [sent[d] for d in range(1, PLANE)]


def send_group(block, distance):
    devices = range(lax.axis_size("group"))
    return lax.ppermute(block, "group", [(i, i ^ distance) for i in devices])


def norm_rows(row_block, gain_vector):
    values = row_block.astype(jnp.float32)
    mean_square = jnp.mean(values * values, axis=-1, keepdims=True)
    return (
        values * lax.rsqrt(mean_square + NORM_EPSILON) * gain_vector.astype(jnp.float32)
    ).astype(jnp.bfloat16)


def dot_t(left, right):
    return lax.dot_general(
        left, right, (((1,), (1,)), ((), ())), preferred_element_type=jnp.float32
    )


def dot_f(left, right):
    return jnp.dot(left, right, preferred_element_type=jnp.float32)


def whole(array):
    return pl.BlockSpec(array.shape, lambda *i: (0,) * len(array.shape))


def after(kernel, count):
    def inner(*refs):
        kernel(*refs[count:])

    return inner


def resident(arrays):
    return [pl.BlockSpec(memory_space=pltpu.VMEM) for _ in arrays]


def unread(arrays):
    return [pl.BlockSpec(memory_space=pl.ANY) for _ in arrays]


def call(kernel, name, inputs, outputs, flops, limit=12, ready=(), streamed=False):
    shapes = [jax.ShapeDtypeStruct(shape, dtype) for shape, dtype in outputs]
    moved = sum(a.size * a.dtype.itemsize for a in list(inputs) + shapes)
    if streamed:
        places = {
            "grid": (1,),
            "in_specs": unread(ready) + [whole(a) for a in inputs],
            "out_specs": [whole(shape) for shape in shapes],
        }
    else:
        places = {
            "in_specs": unread(ready) + resident(inputs),
            "out_specs": resident(shapes),
        }
    return pl.pallas_call(
        after(kernel, len(ready)),
        **places,
        out_shape=shapes,
        compiler_params=pltpu.CompilerParams(vmem_limit_bytes=limit * 1024 * 1024),
        cost_estimate=pl.CostEstimate(flops=flops, bytes_accessed=moved, transcendentals=0),
        name=name,
    )(*ready, *inputs)


def join_share(piece, suffix_columns, routes_columns, tok_quarter):
    rows = piece.shape[0]
    tokens = suffix_columns.shape[1]
    top, groups, _ = routes_columns.shape

    def kernel(piece_ref, suffix_ref, routes_ref, full_ref, lite_ref):
        group_index = lax.axis_index("group")
        shape = (tok_quarter, tokens)
        row = lax.broadcasted_iota(jnp.int32, shape, 0)
        token = lax.broadcasted_iota(jnp.int32, shape, 1)
        select = jnp.where(token == group_index * tok_quarter + row, 1.0, 0.0)
        share = dot_t(select.astype(jnp.bfloat16), suffix_ref[...]).astype(jnp.bfloat16)
        named = jnp.zeros((top, tok_quarter), jnp.float32)
        for j in range(groups):
            part = routes_ref[:, j, :].astype(jnp.float32)
            named = jnp.where(group_index == j, part, named)
        named = jnp.concatenate([named, jnp.zeros((rows - top, tok_quarter), jnp.float32)], axis=0)
        spare = WIDE - LAT - ROPE - tok_quarter
        if spare:
            named = jnp.concatenate([named, jnp.zeros((rows, spare), jnp.float32)], axis=1)
        named = named.astype(jnp.bfloat16)
        piece = piece_ref[...]
        last = jnp.concatenate([piece[:, LAT:], named], axis=1)
        for ref in (full_ref, lite_ref):
            ref[:rows, :LAT] = piece[:, :LAT]
            ref[:rows, LAT:] = last
        empty = jnp.zeros((tok_quarter, WIDE - LAT - ROPE), jnp.bfloat16)
        full_ref[rows:, :LAT] = share[:, :LAT]
        full_ref[rows:, LAT:] = jnp.concatenate([share[:, LAT:], empty], axis=1)

    outputs = [((size, WIDE), piece.dtype) for size in (rows + tok_quarter, rows)]
    inputs = [piece, suffix_columns, routes_columns]
    return call(kernel, "join_share", inputs, outputs, 10_000_000, limit=58, streamed=True)


def join_column(blocks, rows, share, ready):
    count = len(blocks)

    def kernel(*refs):
        block_refs = refs[:count]
        near_ref, *far_refs, routes_ref = refs[count:]
        plane_index = lax.rem(lax.axis_index("tensor"), PLANE)
        at = 0
        for i, ref in enumerate(block_refs):
            near_ref[at : at + ref.shape[0], :] = ref[...]
            at += ref.shape[0]
            routes_ref[i] = ref[:ROUTE_ROWS, LAT:]
        here = block_refs[0][rows:, :].astype(jnp.float32)
        before = block_refs[1][rows:, :].astype(jnp.float32)
        for d, far_ref in enumerate(far_refs):
            for i, ref in enumerate(block_refs):
                far_ref[i * rows : (i + 1) * rows, :] = ref[:rows, :]
            later = plane_index < lax.bitwise_xor(plane_index, d + 1)
            part = jnp.where(later, here, before).astype(jnp.bfloat16)
            far_ref[far_ref.shape[0] - share :, :] = part

    dtype = blocks[0].dtype
    outputs = [((count * rows + 2 * share, WIDE), dtype)]
    outputs += [((count * rows + share, WIDE), dtype)] * (PLANE - 2)
    outputs.append(((count, ROUTE_ROWS, WIDE - LAT), dtype))
    near, *far, routes = call(kernel, "join_column", blocks, outputs, 0, ready=ready)
    return near, far, routes


def halves(by_y, by_x, first, prefix):
    share = by_y.shape[0] - prefix

    def kernel(by_y_ref, by_x_ref, first_ref, second_ref):
        first_ref[:first, :] = by_y_ref[:first, :]
        first_ref[first:, :] = by_y_ref[prefix:, :]
        second_ref[...] = by_x_ref[first:prefix, :]

    outputs = [((first + share, WIDE), by_y.dtype), ((prefix - first, WIDE), by_y.dtype)]
    return call(kernel, "halves", [by_y, by_x], outputs, 0)


def pass_on(blocks, ready):
    first = len(ready)

    def kernel(*refs):
        pass

    return pl.pallas_call(
        kernel,
        in_specs=unread(ready) + unread(blocks),
        out_specs=unread(blocks),
        out_shape=[jax.ShapeDtypeStruct(block.shape, block.dtype) for block in blocks],
        input_output_aliases={first + i: i for i in range(len(blocks))},
        compiler_params=pltpu.CompilerParams(vmem_limit_bytes=1024 * 1024),
        name="pass_on",
    )(*ready, *blocks)


LATER = 1 << 20


def segment_rows(d, segments):
    return [(d, k, r, s, r < real) for k, count, real, s in segments for r in range(count)]


def key_table(groups, side):
    rows = [(j, *row) for j in range(groups) for row in side]
    table = np.zeros((8, len(rows)), np.int32)
    table[:6] = np.array(rows, np.int32).T
    table[6] = table[3] // PAGE
    table[7] = table[3] % PAGE
    return table


def make_plan(table, counts, lengths, tenants, tenant_lengths, page_table, ring, piece_rows, sizes, ready):
    tok_slice, tok_quarter, groups = sizes
    requests = lengths.shape[0]
    tenant_count = tenant_lengths.shape[0]
    pages = page_table.shape[1]
    piece_pages = piece_rows // PAGE

    def spots_of(part, page_row, group_index, ring_index, plane_index):
        j, d, k, r, suffix, real, page_at, within = (part[i : i + 1, :] for i in range(8))
        in_plane = lax.bitwise_xor(plane_index, d)
        k = jnp.where(suffix == 2, jnp.where(in_plane < plane_index, 0, 1), k)
        from_ring = ring_index - k
        from_ring = jnp.where(from_ring < 0, from_ring + ring, from_ring)
        of_group = lax.bitwise_xor(group_index, j)
        owner = (of_group * ring + from_ring) * PLANE + in_plane
        index = owner * piece_pages + page_at
        count = part.shape[1]
        page = lax.broadcasted_iota(jnp.int32, (pages, count), 0)
        hit = jnp.where(page == index, 1.0, 0.0).astype(jnp.bfloat16)
        found = dot_f(page_row, hit)[:1].astype(jnp.int32)
        logical = jnp.where(real > 0, found * PAGE + within, -1)
        token = (from_ring * PLANE + in_plane) * tok_slice + of_group * tok_quarter + r
        return jnp.where(suffix > 0, token + LATER, logical)

    def kernel(lengths_ref, tenants_ref, tenant_lengths_ref, page_ref, table_ref, *refs):
        info_ref, order_ref, *spot_refs = refs
        group_index = jnp.full((1, 1), lax.axis_index("group"), jnp.int32)
        tensor_index = lax.axis_index("tensor")
        ring_index = jnp.full((1, 1), lax.div(tensor_index, PLANE), jnp.int32)
        plane_index = jnp.full((1, 1), lax.rem(tensor_index, PLANE), jnp.int32)
        page_row = page_ref[...].astype(jnp.float32).astype(jnp.bfloat16)
        page_row = jnp.broadcast_to(page_row, (16, pages))
        at = 0
        for count, spot_ref in zip(counts, spot_refs):
            part = table_ref[:, at : at + count]
            spot_ref[...] = spots_of(part, page_row, group_index, ring_index, plane_index)
            at += count
        row = lax.broadcasted_iota(jnp.int32, (tok_slice, 1), 0)
        share = jnp.zeros((tok_slice, 1), jnp.int32)
        for j in range(1, groups):
            share = share + jnp.where(row >= j * tok_quarter, 1, 0)
        local = (row - share * tok_quarter) * groups + lax.bitwise_xor(group_index, share)
        column = lax.broadcasted_iota(jnp.int32, (tok_slice, tok_slice), 1)
        order_ref[...] = jnp.where(column == local, 1.0, 0.0).astype(jnp.bfloat16)
        position = local + tensor_index * tok_slice
        low = jnp.zeros((tok_slice, 1), jnp.int32)
        high = jnp.zeros((tok_slice, 1), jnp.int32)
        start = jnp.zeros((tok_slice, 1), jnp.int32)
        begin = 0
        for i in range(requests):
            end = begin + lengths_ref[i]
            inside = (position >= begin) & (position < end)
            tenant = tenants_ref[i]
            first = 0
            tenant_low = 0
            tenant_high = 0
            for t in range(tenant_count):
                last = first + tenant_lengths_ref[t]
                tenant_low = jnp.where(tenant == t, first, tenant_low)
                tenant_high = jnp.where(tenant == t, last, tenant_high)
                first = last
            start = jnp.where(inside, begin, start)
            low = jnp.where(inside, tenant_low, low)
            high = jnp.where(inside, tenant_high, high)
            begin = end
        for i, value in enumerate((low, high, start + LATER, position + LATER)):
            info_ref[:, i : i + 1] = value

    shapes = [
        jax.ShapeDtypeStruct((tok_slice, 4), jnp.int32),
        jax.ShapeDtypeStruct((tok_slice, tok_slice), jnp.bfloat16),
    ] + [jax.ShapeDtypeStruct((1, count), jnp.int32) for count in counts]
    scalar = pl.BlockSpec(memory_space=pltpu.SMEM)
    arrays = [page_table, table]
    return pl.pallas_call(
        after(kernel, len(ready)),
        in_specs=unread(ready) + [scalar, scalar, scalar] + resident(arrays),
        out_specs=resident(shapes),
        out_shape=shapes,
        compiler_params=pltpu.CompilerParams(vmem_limit_bytes=20 * 1024 * 1024),
        cost_estimate=pl.CostEstimate(
            flops=4_000_000_000, bytes_accessed=1_000_000, transcendentals=0
        ),
        name="make_plan",
    )(*ready, lengths, tenants, tenant_lengths, *arrays)


def place_keys(key_refs, spot_ref, token_ref, keys, bias):
    at = 0
    for ref in key_refs:
        rows = ref.shape[0]
        keys[at : at + rows, :] = ref[...]
        at += rows
    columns = token_ref[...]
    spots = spot_ref[...]
    low, high, start, here = (columns[:, i : i + 1] for i in range(4))
    seen = ((spots >= low) & (spots < high)) | ((spots >= start) & (spots <= here))
    bias[...] = jnp.where(seen, 0.0, VERY_NEGATIVE)


SCORE_FACTOR = math.log2(math.e) / math.sqrt(NOPE + ROPE)


def score_rows(queries, keys, bias, pair):
    scores = dot_t(queries, keys[...])
    rows, count = scores.shape
    return (scores.reshape(pair, rows // pair, count) + bias[...][None]).reshape(rows, count)


def near_kernel(block_count, pair, token_ref, spot_ref, order_ref, query_ref, key_up_ref, *refs):
    key_refs = refs[:block_count]
    wide_ref, best_ref, sum_ref, acc_ref, flag_ref, keys, bias = refs[block_count:]
    flag_ref[...] = jnp.zeros_like(flag_ref)
    tokens = query_ref.shape[0]
    place_keys(key_refs, spot_ref, token_ref, keys, bias)
    queries = dot_f(order_ref[...], query_ref[...]).astype(jnp.bfloat16)
    size = NOPE + ROPE
    empty = jnp.zeros((tokens, WIDE - LAT - ROPE), jnp.bfloat16)
    for first in range(0, key_up_ref.shape[0], pair):
        wide = []
        for h in range(first, first + pair):
            part = queries[:, h * size : (h + 1) * size]
            content = dot_f(part[:, :NOPE], key_up_ref[h]).astype(jnp.bfloat16)
            wide.append(jnp.concatenate([content, part[:, NOPE:], empty], axis=1))
        wide = jnp.concatenate(wide, axis=0)
        here = pl.ds(first * tokens, pair * tokens)
        wide_ref[here, :] = wide
        masked = score_rows(wide, keys, bias, pair)
        best = jnp.max(masked, axis=-1, keepdims=True)
        weights = jnp.exp2((masked - best) * SCORE_FACTOR)
        best_ref[here, :] = best
        sum_ref[here, :] = jnp.sum(weights, axis=-1, keepdims=True)
        acc_ref[here, :] = dot_f(weights.astype(jnp.bfloat16), keys[:, :LAT])


def attend_call(kernel, name, inputs, outputs, scratch, work, limit=24):
    shapes = [jax.ShapeDtypeStruct(shape, dtype) for shape, dtype in outputs]
    return pl.pallas_call(
        kernel,
        in_specs=resident(inputs),
        out_specs=resident(shapes),
        out_shape=shapes,
        scratch_shapes=scratch,
        compiler_params=pltpu.CompilerParams(vmem_limit_bytes=limit * 1024 * 1024),
        cost_estimate=pl.CostEstimate(
            flops=work, bytes_accessed=8_000_000, transcendentals=work // 2176
        ),
        name=name,
    )(*inputs)


def key_scratch(tokens, blocks):
    count = sum(block.shape[0] for block in blocks)
    return [pltpu.VMEM((count, WIDE), jnp.bfloat16), pltpu.VMEM((tokens, count), jnp.float32)]


def attend_near(tokens_info, spots, order, queries, key_up, blocks):
    tokens = queries.shape[0]
    heads = key_up.shape[0]
    rows = heads * tokens
    outputs = [
        ((rows, WIDE), jnp.bfloat16),
        ((rows, 1), jnp.float32),
        ((rows, 1), jnp.float32),
        ((rows, LAT), jnp.float32),
        ((8, 128), jnp.float32),
    ]
    return attend_call(
        functools.partial(near_kernel, len(blocks), min(4, heads)),
        "attend_near",
        [tokens_info, spots, order, queries, key_up, *blocks],
        outputs,
        key_scratch(tokens, blocks),
        2 * rows * spots.shape[1] * (LAT + ROPE + LAT),
    )


def add_keys(here, wide_ref, best_ref, sum_ref, acc_ref, keys, bias, pair):
    masked = score_rows(wide_ref[here, :], keys, bias, pair)
    before = best_ref[here, :]
    best = jnp.maximum(before, jnp.max(masked, axis=-1, keepdims=True))
    factor = jnp.exp2((before - best) * SCORE_FACTOR)
    weights = jnp.exp2((masked - best) * SCORE_FACTOR)
    weight_sum = sum_ref[here, :] * factor + jnp.sum(weights, axis=-1, keepdims=True)
    attended = acc_ref[here, :] * factor + dot_f(weights.astype(jnp.bfloat16), keys[:, :LAT])
    return best, weight_sum, attended


def mid_kernel(block_count, pair, token_ref, spot_ref, wide_ref, best_ref, sum_ref, acc_ref, *refs):
    key_refs = refs[:block_count]
    new_best_ref, new_sum_ref, new_acc_ref, flag_ref, keys, bias = refs[block_count:]
    flag_ref[...] = jnp.zeros_like(flag_ref)
    place_keys(key_refs, spot_ref, token_ref, keys, bias)
    rows = pair * token_ref.shape[0]
    for first in range(0, wide_ref.shape[0], rows):
        here = pl.ds(first, rows)
        new_best_ref[here, :], new_sum_ref[here, :], new_acc_ref[here, :] = add_keys(
            here, wide_ref, best_ref, sum_ref, acc_ref, keys, bias, pair
        )


def attend_mid(tokens_info, spots, near, blocks):
    tokens = tokens_info.shape[0]
    rows = near[0].shape[0]
    outputs = [
        ((rows, 1), jnp.float32),
        ((rows, 1), jnp.float32),
        ((rows, LAT), jnp.float32),
        ((8, 128), jnp.float32),
    ]
    return attend_call(
        functools.partial(mid_kernel, len(blocks), min(4, rows // tokens)),
        "attend_mid",
        [tokens_info, spots, *near, *blocks],
        outputs,
        key_scratch(tokens, blocks),
        2 * rows * spots.shape[1] * (LAT + ROPE + LAT),
    )


def far_kernel(
    block_count,
    pair,
    token_ref,
    spot_ref,
    wide_ref,
    best_ref,
    sum_ref,
    acc_ref,
    value_up_ref,
    output_ref,
    *refs,
):
    key_refs = refs[:block_count]
    own_ref, other_ref, keys, bias = refs[block_count:]
    tokens = token_ref.shape[0]
    rows = pair * tokens
    place_keys(key_refs, spot_ref, token_ref, keys, bias)
    heads = []
    for first in range(0, wide_ref.shape[0], rows):
        _, weight_sum, attended = add_keys(
            pl.ds(first, rows), wide_ref, best_ref, sum_ref, acc_ref, keys, bias, pair
        )
        attended = (attended / weight_sum).astype(jnp.bfloat16)
        for h in range(pair):
            part = attended[h * tokens : (h + 1) * tokens]
            value = value_up_ref[first // tokens + h]
            heads.append(dot_f(part, value).astype(jnp.bfloat16))
    total = dot_f(jnp.concatenate(heads, axis=1), output_ref[...])
    mine = own_ref.shape[0]
    own_ref[...] = total[:mine]
    other_ref[...] = total[mine:].astype(jnp.bfloat16)


def attend_far(tokens_info, spots, near, value_up, output_weight, blocks, tok_quarter):
    tokens = tokens_info.shape[0]
    heads = value_up.shape[0]
    width = output_weight.shape[1]
    outputs = [
        ((tok_quarter, width), jnp.float32),
        ((tokens - tok_quarter, width), jnp.bfloat16),
    ]
    return attend_call(
        functools.partial(far_kernel, len(blocks), min(4, heads)),
        "attend_far",
        [tokens_info, spots, *near, value_up, output_weight, *blocks],
        outputs,
        key_scratch(tokens, blocks),
        2 * heads * tokens * spots.shape[1] * (LAT + ROPE + LAT),
    )


def pick_rows(turn, ring, top, block, routes_ref, router_ref, scaled_ref, outs):
    tokens = block.shape[0]
    capacity = outs[0].shape[0]
    tensor_index = lax.axis_index("tensor")
    here = lax.div(tensor_index, PLANE)
    plane_index = lax.rem(tensor_index, PLANE)
    order = ring_order(ring)
    place = sum(jnp.where(here == z, i, 0) for i, z in enumerate(order))
    place = lax.rem(place - turn + ring, ring)
    source = sum(jnp.where(place == i, z, 0) for i, z in enumerate(order))
    routes = routes_ref[lax.rem(here - source + ring, ring)].astype(jnp.float32)
    routes = routes[:, ROPE : ROPE + tokens]
    targets = [
        (here * PLANE + lax.bitwise_xor(plane_index, d)).astype(jnp.float32)
        for d in range(PLANE)
    ]
    hits = [
        jnp.sum(jnp.where(routes[:top] == target, 1.0, 0.0), axis=0, keepdims=True)
        for target in targets
    ]
    before = lax.broadcasted_iota(jnp.int32, (tokens, tokens), 0)
    after_it = lax.broadcasted_iota(jnp.int32, (tokens, tokens), 1)
    earlier = jnp.where(before < after_it, 1.0, 0.0).astype(jnp.bfloat16)
    ranks = dot_f(jnp.concatenate(hits, axis=0).astype(jnp.bfloat16), earlier)
    count = router_ref.shape[0]
    expert = lax.broadcasted_iota(jnp.int32, (count, tokens), 0).astype(jnp.float32)
    named = jnp.zeros((count, tokens), jnp.float32)
    for i in range(top):
        named = named + jnp.where(expert == routes[i : i + 1], 1.0, 0.0)
    picked = jax.nn.sigmoid(dot_t(router_ref[...], block)) * named
    gates = picked / jnp.sum(picked, axis=0, keepdims=True) * ROUTE_SCALING
    slot = lax.broadcasted_iota(jnp.int32, (capacity, tokens), 0).astype(jnp.float32)
    for d, out in enumerate(outs):
        taken = jnp.where(slot == ranks[d : d + 1], hits[d], 0.0)
        out[...] = dot_f(taken.astype(jnp.bfloat16), block).astype(jnp.bfloat16)
        gate = jnp.sum(jnp.where(expert == targets[d], gates, 0.0), axis=0, keepdims=True)
        scaled_ref[d * capacity : (d + 1) * capacity, :] = (taken * gate).astype(jnp.bfloat16)


def pick_outputs(block, capacity):
    tokens, width = block.shape
    pieces = [((capacity, width), jnp.bfloat16)] * PLANE
    return [((PLANE * capacity, tokens), jnp.bfloat16)] + pieces


def settle(hidden, own, others, gain, routes, router, sizes):
    ring, top, capacity = sizes

    def kernel(*refs):
        hidden_ref, own_ref = refs[:2]
        other_refs = refs[2 : 2 + len(others)]
        gain_ref, routes_ref, router_ref = refs[2 + len(others) : 5 + len(others)]
        residual_ref, normed_ref, scaled_ref, *outs = refs[5 + len(others) :]
        total = own_ref[...]
        for ref in other_refs:
            total = total + ref[...].astype(jnp.float32)
        residual = (hidden_ref[...].astype(jnp.float32) + total).astype(jnp.bfloat16)
        residual_ref[...] = residual
        normed = norm_rows(residual, gain_ref[...])
        normed_ref[...] = normed
        pick_rows(0, ring, top, normed, routes_ref, router_ref, scaled_ref, outs)

    outputs = [(hidden.shape, jnp.bfloat16)] * 2 + pick_outputs(hidden, capacity)
    inputs = [hidden, own, *others, gain, routes, router]
    residual, normed, scaled, *pieces = call(kernel, "settle", inputs, outputs, 10_000_000_000)
    return residual, normed, scaled, pieces


def turn(step, block, arrived, routes, router, sizes, ready):
    ring, top, capacity = sizes
    width = arrived[0].shape[1]
    inputs = [*arrived]
    outputs = [((PLANE * capacity, width), jnp.bfloat16)]
    if block is not None:
        inputs += [block, routes, router]
        outputs.append(((PLANE * capacity, block.shape[0]), jnp.bfloat16))
        outputs += [((capacity, width), jnp.bfloat16)] * PLANE

    def kernel(*refs):
        row_refs = refs[:PLANE]
        joined_ref = refs[len(inputs)]
        for d, ref in enumerate(row_refs):
            joined_ref[d * capacity : (d + 1) * capacity, :] = ref[:capacity, :]
        if block is not None:
            block_ref, routes_ref, router_ref = refs[PLANE : len(inputs)]
            scaled_ref, *outs = refs[len(inputs) + 1 :]
            pick_rows(
                step, ring, top, block_ref[...], routes_ref, router_ref, scaled_ref, outs
            )

    joined, *found = call(kernel, "turn", inputs, outputs, 70_000_000, ready=ready)
    if block is None:
        return joined, None, []
    return joined, found[0], found[1:]


def blend(own, others, pieces, ready):
    capacity = own.shape[0] // PLANE
    first = pieces[0].shape[0] if pieces else 0
    inputs = [own, *others, *pieces]

    def kernel(*refs):
        outs = refs[len(inputs) :]
        total = refs[0][...]
        for ref in refs[1 : 1 + len(others)]:
            total = total + ref[...].astype(jnp.float32)
        total = total.astype(jnp.bfloat16)
        for d, out in enumerate(outs):
            if pieces:
                out[:first, :] = refs[1 + len(others) + d][...]
            out[first:, :] = total[d * capacity : (d + 1) * capacity]

    outputs = [((first + capacity, own.shape[1]), jnp.bfloat16)] * PLANE
    return call(kernel, "blend", inputs, outputs, 1_000_000, ready=ready)


def expert_apply(pieces, kept, gate_part, up_part, down_part):
    total = sum(piece.shape[0] for piece in pieces)
    units, width = gate_part.shape

    def kernel(*refs):
        row_refs = refs[: len(pieces)]
        gate_ref, up_ref, down_ref, own_ref, other_ref, flag_ref = refs[len(pieces) :]
        flag_ref[...] = jnp.zeros_like(flag_ref)
        rows = jnp.concatenate([ref[...] for ref in row_refs], axis=0)
        gate_vals = dot_t(rows, gate_ref[...])
        up_vals = dot_t(rows, up_ref[...])
        hidden = (jax.nn.silu(gate_vals) * up_vals).astype(jnp.bfloat16)
        partial = dot_f(hidden, down_ref[...])
        own_ref[...] = partial[:kept]
        other_ref[...] = partial[kept:].astype(jnp.bfloat16)

    outputs = [
        ((kept, width), jnp.float32),
        ((total - kept, width), jnp.bfloat16),
        ((8, 128), jnp.float32),
    ]
    inputs = [*pieces, gate_part, up_part, down_part]
    return call(kernel, "experts", inputs, outputs, 6 * total * width * units, limit=20)


def scatter_sum(scaled_ref, piece_refs, running_ref):
    size = scaled_ref.shape[0] // PLANE
    parts = [ref[ref.shape[0] - size :, :] for ref in piece_refs]
    returned = jnp.concatenate(parts, axis=0)
    total = lax.dot_general(
        scaled_ref[...], returned, (((0,), (0,)), ((), ())), preferred_element_type=jnp.float32
    )
    if running_ref is not None:
        total = total + running_ref[...].astype(jnp.float32)
    return total


def collect(scaled, pieces, running):
    extra = [] if running is None else [running]

    def kernel(scaled_ref, *refs):
        running_ref = refs[len(pieces)] if extra else None
        total = scatter_sum(scaled_ref, refs[: len(pieces)], running_ref)
        refs[-1][...] = total.astype(jnp.bfloat16)

    shape = (scaled.shape[1], pieces[0].shape[1])
    inputs = [scaled, *pieces, *extra]
    return call(kernel, "collect", inputs, [(shape, jnp.bfloat16)], 35_000_000)[0]


def conclude(scaled, pieces, running, residual, gain):
    extra = [] if running is None else [running]

    def kernel(residual_ref, gain_ref, scaled_ref, *refs):
        running_ref = refs[len(pieces)] if extra else None
        total = scatter_sum(scaled_ref, refs[: len(pieces)], running_ref)
        layer = (residual_ref[...].astype(jnp.float32) + total).astype(jnp.bfloat16)
        refs[-2][...] = layer
        refs[-1][...] = norm_rows(layer, gain_ref[...])

    inputs = [residual, gain, scaled, *pieces, *extra]
    return call(kernel, "conclude", inputs, [(residual.shape, jnp.bfloat16)] * 2, 35_000_000)


def project(shares, order, query_weight, latent_rows):
    def kernel(order_ref, query_ref, latent_ref, *refs):
        share_refs = refs[: len(shares)]
        queries_ref, latents_ref = refs[len(shares) :]
        rows = jnp.concatenate([ref[...] for ref in share_refs], axis=0)
        rows = lax.dot_general(
            order_ref[...], rows, (((0,), (0,)), ((), ())), preferred_element_type=jnp.float32
        ).astype(jnp.bfloat16)
        latents_ref[...] = dot_t(latent_ref[...], rows).astype(jnp.bfloat16)
        queries_ref[...] = dot_f(rows, query_ref[...]).astype(jnp.bfloat16)

    tokens = order.shape[0]
    outputs = [
        ((tokens, query_weight.shape[1]), jnp.bfloat16),
        ((latent_rows.shape[0], tokens), jnp.bfloat16),
    ]
    inputs = [order, query_weight, latent_rows, *shares]
    return call(kernel, "project", inputs, outputs, 1_000_000_000, limit=16)


def per_device(
    hidden_in,
    queries,
    suffix_latent,
    prefix_latent,
    key_up,
    value_up,
    output_weight,
    norm_gain,
    router,
    expert_gate,
    expert_up,
    expert_down,
    next_gain,
    next_query_weight,
    next_latent_weight,
    suffix_lengths,
    request_tenant,
    tenant_lengths,
    page_table,
    routes,
):
    tok_slice = hidden_in.shape[0]
    groups = lax.axis_size("group")
    ring = lax.axis_size("tensor") // PLANE
    tok_quarter = tok_slice // groups
    expert_count = router.shape[1]
    top_count = routes.shape[2]
    capacity = max(2, 4 * tok_quarter * top_count // (3 * expert_count))
    capacity = -(-capacity // 16) * 16

    real_rows = prefix_latent.shape[0]
    piece_rows = -(-real_rows // 16) * 16
    piece = prefix_latent
    if piece_rows != real_rows:
        piece = jnp.pad(piece, ((0, piece_rows - real_rows), (0, 0)))
    routes_columns = jnp.transpose(routes, (2, 0, 1))
    full, lite = join_share(piece, suffix_latent.T, routes_columns, tok_quarter)
    along = [send_round(full, PLANE)] + [send_round(lite, PLANE * k) for k in range(2, ring)]
    near_segments = []
    far_segments = []
    for k in range(ring):
        near_segments.append((k, piece_rows, real_rows, 0))
        far_segments.append((k, piece_rows, real_rows, 0))
        if k < 2:
            near_segments.append((k, tok_quarter, 0, 1))
    far_segments.append((0, tok_quarter, 0, 2))
    prefix_rows = ring * piece_rows
    first_rows = (prefix_rows - tok_quarter) // 2
    diagonal = segment_rows(3, far_segments)
    sides = (
        segment_rows(0, near_segments),
        segment_rows(1, far_segments) + segment_rows(2, far_segments),
        diagonal[:first_rows] + diagonal[prefix_rows:] + diagonal[first_rows:prefix_rows],
    )
    tables = [key_table(groups, side) for side in sides]
    tokens_info, permutation, near_spots, mid_spots, far_spots = make_plan(
        jnp.asarray(np.concatenate(tables, axis=1)),
        [part.shape[1] for part in tables],
        suffix_lengths,
        request_tenant,
        tenant_lengths,
        page_table[None, :],
        ring,
        real_rows,
        (tok_slice, tok_quarter, groups),
        [full],
    )

    column, plane, routes_ring = join_column(
        [full, *along], piece_rows, tok_quarter, [near_spots]
    )
    plane = [send_plane(part, d + 1) for d, part in enumerate(plane)]
    near_blocks = [send_group(column, j) if j else column for j in range(groups)]

    *near, near_flag = attend_near(
        tokens_info, near_spots, permutation, queries, key_up, near_blocks
    )
    beside = pass_on(plane, [near_flag])
    first, second = halves(beside[1], beside[0], first_rows, prefix_rows)
    across = [send_plane(first, 1), send_plane(second, 2)]
    mid_blocks = [send_group(block, j) if j else block for j in range(groups) for block in beside]
    *mid, mid_flag = attend_mid(tokens_info, mid_spots, near, mid_blocks)
    near = [near[0], *mid]
    across = pass_on(across, [mid_flag])
    far_blocks = [send_group(block, j) if j else block for j in range(groups) for block in across]
    attend_own, attend_other = attend_far(
        tokens_info, far_spots, near, value_up, output_weight, far_blocks, tok_quarter
    )

    hidden_own = dot_f(permutation[:tok_quarter], hidden_in).astype(jnp.bfloat16)
    others = [
        send_group(attend_other[(j - 1) * tok_quarter : j * tok_quarter], j)
        for j in range(1, groups)
    ]
    sizes = (ring, top_count, capacity)
    experts_columns = router.T
    residual, block, scaled, pieces = settle(
        hidden_own,
        attend_own,
        others,
        norm_gain[None, :],
        routes_ring,
        experts_columns,
        sizes,
    )

    kept = PLANE * capacity
    gate_part = jnp.transpose(expert_gate, (0, 2, 1))[0]
    up_part = jnp.transpose(expert_up, (0, 2, 1))[0]
    down_part = expert_down[0]
    scales = [scaled]
    results = []
    running = None
    payload = pieces
    for step in range(1, ring + 4):
        if step <= ring - 1:
            block = send_ring(block, ring)
        arrived = send_pieces(payload)
        if 4 <= step:
            k = step - 3
            if k < ring:
                landed = running
                total = collect(scales[k], arrived, running)
                running = send_ring(total, ring)
            else:
                break
        payload = []
        back = step - 2 if step - 2 < ring else 0
        if step >= 3:
            own, other, _ = results[back]
            if back:
                along_z = [block] if step <= ring - 1 else [landed] if step > 4 else []
                other = pass_on([other], arrived[1:] + along_z)[0]
            others = [
                send_group(other[(j - 1) * kept : j * kept], j) for j in range(1, groups)
            ]
        if step <= ring:
            joined, scaled, payload = turn(
                step,
                block if step <= ring - 1 else None,
                arrived,
                routes_ring,
                experts_columns,
                sizes,
                [results[step - 2][2]] if step >= 2 else [],
            )
            scales.append(scaled)
            rows = [send_group(joined, j) if j else joined for j in range(groups)]
            results.append(expert_apply(rows, kept, gate_part, up_part, down_part))
        if step >= 3:
            payload = blend(own, others, payload, [] if back else [total])
    layer_rows, normed_next = conclude(
        scales[0], arrived, running, residual, next_gain[None, :]
    )

    shares = [send_group(normed_next, j) if j else normed_next for j in range(groups)]
    next_queries, next_latent = project(
        shares, permutation, next_query_weight, next_latent_weight.T
    )
    return (layer_rows[:, None, :], next_queries, next_latent.T)


def solution(mesh):
    return jax.shard_map(
        per_device,
        mesh=mesh,
        in_specs=(
            P("tensor", None),
            P("tensor", "group"),
            P("tensor", None),
            P(("group", "tensor"), None),
            P("group", None, None),
            P("group", None, None),
            P("group", None),
            P(),
            P(),
            P("tensor", None, "group"),
            P("tensor", None, "group"),
            P("tensor", "group", None),
            P(),
            P(None, "group"),
            P(None, "group"),
            P(),
            P(),
            P(),
            P(),
            P(None, "tensor", None),
        ),
        out_specs=(P("tensor", "group", None), P("tensor", "group"), P("tensor", "group")),
        check_vma=False,
    )
```

```python
import functools
import math

import jax
import jax.numpy as jnp
import numpy as np
from jax import lax
from jax.experimental import pallas as pl
from jax.experimental.pallas import tpu as pltpu
from jax.sharding import PartitionSpec as P

NOPE = 128
ROPE = 64
LAT = 512
PAGE = 8
PLANE = 4
ROUTE_ROWS = 16
WIDE = 640

VERY_NEGATIVE = -1e30
ROUTE_SCALING = 2.446
NORM_EPSILON = 1e-06


def ring_order(count):
    odd = list(range(1, count, 2))
    even = list(range(2, count, 2))
    return [0] + odd + even[::-1]


def send_ring(block, count, steps=1):
    order = ring_order(count)
    after = {order[i]: order[(i + steps) % count] for i in range(count)}
    route = [
        (z * PLANE + p, after[z] * PLANE + p) for z in range(count) for p in range(PLANE)
    ]
    return lax.ppermute(block, "tensor", route)


def send_round(block, distance):
    count = lax.axis_size("tensor")
    return lax.ppermute(block, "tensor", [(i, (i + distance) % count) for i in range(count)])


def send_plane(block, distance):
    devices = range(lax.axis_size("tensor"))
    return lax.ppermute(block, "tensor", [(i, i ^ distance) for i in devices])


def send_pieces(pieces):
    sent = {d: send_plane(pieces[d], d) for d in reversed(range(1, PLANE))}
    return [pieces[0]] + [sent[d] for d in range(1, PLANE)]


def send_group(block, distance):
    devices = range(lax.axis_size("group"))
    return lax.ppermute(block, "group", [(i, i ^ distance) for i in devices])


def norm_rows(row_block, gain_vector):
    values = row_block.astype(jnp.float32)
    mean_square = jnp.mean(values * values, axis=-1, keepdims=True)
    return (
        values * lax.rsqrt(mean_square + NORM_EPSILON) * gain_vector.astype(jnp.float32)
    ).astype(jnp.bfloat16)


def dot_t(left, right):
    return lax.dot_general(
        left, right, (((1,), (1,)), ((), ())), preferred_element_type=jnp.float32
    )


def dot_f(left, right):
    return jnp.dot(left, right, preferred_element_type=jnp.float32)


def whole(array):
    return pl.BlockSpec(array.shape, lambda *i: (0,) * len(array.shape))


def after(kernel, count):
    def inner(*refs):
        kernel(*refs[count:])

    return inner


def resident(arrays):
    return [pl.BlockSpec(memory_space=pltpu.VMEM) for _ in arrays]


def unread(arrays):
    return [pl.BlockSpec(memory_space=pl.ANY) for _ in arrays]


def call(kernel, name, inputs, outputs, flops, limit=12, ready=(), streamed=False):
    shapes = [jax.ShapeDtypeStruct(shape, dtype) for shape, dtype in outputs]
    moved = sum(a.size * a.dtype.itemsize for a in list(inputs) + shapes)
    if streamed:
        places = {
            "grid": (1,),
            "in_specs": unread(ready) + [whole(a) for a in inputs],
            "out_specs": [whole(shape) for shape in shapes],
        }
    else:
        places = {
            "in_specs": unread(ready) + resident(inputs),
            "out_specs": resident(shapes),
        }
    return pl.pallas_call(
        after(kernel, len(ready)),
        **places,
        out_shape=shapes,
        compiler_params=pltpu.CompilerParams(vmem_limit_bytes=limit * 1024 * 1024),
        cost_estimate=pl.CostEstimate(flops=flops, bytes_accessed=moved, transcendentals=0),
        name=name,
    )(*ready, *inputs)


def join_share(piece, suffix_columns, routes_columns, tok_quarter):
    rows = piece.shape[0]
    tokens = suffix_columns.shape[1]
    top, groups, _ = routes_columns.shape

    def kernel(piece_ref, suffix_ref, routes_ref, full_ref, lite_ref):
        group_index = lax.axis_index("group")
        shape = (tok_quarter, tokens)
        row = lax.broadcasted_iota(jnp.int32, shape, 0)
        token = lax.broadcasted_iota(jnp.int32, shape, 1)
        select = jnp.where(token == group_index * tok_quarter + row, 1.0, 0.0)
        share = dot_t(select.astype(jnp.bfloat16), suffix_ref[...]).astype(jnp.bfloat16)
        named = jnp.zeros((top, tok_quarter), jnp.float32)
        for j in range(groups):
            part = routes_ref[:, j, :].astype(jnp.float32)
            named = jnp.where(group_index == j, part, named)
        named = jnp.concatenate([named, jnp.zeros((rows - top, tok_quarter), jnp.float32)], axis=0)
        spare = WIDE - LAT - ROPE - tok_quarter
        if spare:
            named = jnp.concatenate([named, jnp.zeros((rows, spare), jnp.float32)], axis=1)
        named = named.astype(jnp.bfloat16)
        piece = piece_ref[...]
        last = jnp.concatenate([piece[:, LAT:], named], axis=1)
        for ref in (full_ref, lite_ref):
            ref[:rows, :LAT] = piece[:, :LAT]
            ref[:rows, LAT:] = last
        empty = jnp.zeros((tok_quarter, WIDE - LAT - ROPE), jnp.bfloat16)
        full_ref[rows:, :LAT] = share[:, :LAT]
        full_ref[rows:, LAT:] = jnp.concatenate([share[:, LAT:], empty], axis=1)

    outputs = [((size, WIDE), piece.dtype) for size in (rows + tok_quarter, rows)]
    inputs = [piece, suffix_columns, routes_columns]
    return call(kernel, "join_share", inputs, outputs, 10_000_000, limit=58, streamed=True)


def join_column(blocks, rows, share, ready):
    count = len(blocks)

    def kernel(*refs):
        block_refs = refs[:count]
        near_ref, *far_refs, routes_ref = refs[count:]
        plane_index = lax.rem(lax.axis_index("tensor"), PLANE)
        at = 0
        for i, ref in enumerate(block_refs):
            near_ref[at : at + ref.shape[0], :] = ref[...]
            at += ref.shape[0]
            routes_ref[i] = ref[:ROUTE_ROWS, LAT:]
        here = block_refs[0][rows:, :].astype(jnp.float32)
        before = block_refs[1][rows:, :].astype(jnp.float32)
        for d, far_ref in enumerate(far_refs):
            for i, ref in enumerate(block_refs):
                far_ref[i * rows : (i + 1) * rows, :] = ref[:rows, :]
            later = plane_index < lax.bitwise_xor(plane_index, d + 1)
            part = jnp.where(later, here, before).astype(jnp.bfloat16)
            far_ref[far_ref.shape[0] - share :, :] = part

    dtype = blocks[0].dtype
    outputs = [((count * rows + 2 * share, WIDE), dtype)]
    outputs += [((count * rows + share, WIDE), dtype)] * (PLANE - 2)
    outputs.append(((count, ROUTE_ROWS, WIDE - LAT), dtype))
    near, *far, routes = call(kernel, "join_column", blocks, outputs, 0, ready=ready)
    return near, far, routes


def halves(by_y, by_x, first, prefix):
    share = by_y.shape[0] - prefix

    def kernel(by_y_ref, by_x_ref, first_ref, second_ref):
        first_ref[:first, :] = by_y_ref[:first, :]
        first_ref[first:, :] = by_y_ref[prefix:, :]
        second_ref[...] = by_x_ref[first:prefix, :]

    outputs = [((first + share, WIDE), by_y.dtype), ((prefix - first, WIDE), by_y.dtype)]
    return call(kernel, "halves", [by_y, by_x], outputs, 0)


def pass_on(blocks, ready):
    first = len(ready)

    def kernel(*refs):
        pass

    return pl.pallas_call(
        kernel,
        in_specs=unread(ready) + unread(blocks),
        out_specs=unread(blocks),
        out_shape=[jax.ShapeDtypeStruct(block.shape, block.dtype) for block in blocks],
        input_output_aliases={first + i: i for i in range(len(blocks))},
        compiler_params=pltpu.CompilerParams(vmem_limit_bytes=1024 * 1024),
        name="pass_on",
    )(*ready, *blocks)


LATER = 1 << 20


def segment_rows(d, segments):
    return [(d, k, r, s, r < real) for k, count, real, s in segments for r in range(count)]


def key_table(groups, side):
    rows = [(j, *row) for j in range(groups) for row in side]
    table = np.zeros((8, len(rows)), np.int32)
    table[:6] = np.array(rows, np.int32).T
    table[6] = table[3] // PAGE
    table[7] = table[3] % PAGE
    return table


def make_plan(table, counts, lengths, tenants, tenant_lengths, page_table, ring, piece_rows, sizes, ready):
    tok_slice, tok_quarter, groups = sizes
    requests = lengths.shape[0]
    tenant_count = tenant_lengths.shape[0]
    pages = page_table.shape[1]
    piece_pages = piece_rows // PAGE

    def spots_of(part, page_row, group_index, ring_index, plane_index):
        j, d, k, r, suffix, real, page_at, within = (part[i : i + 1, :] for i in range(8))
        in_plane = lax.bitwise_xor(plane_index, d)
        k = jnp.where(suffix == 2, jnp.where(in_plane < plane_index, 0, 1), k)
        from_ring = ring_index - k
        from_ring = jnp.where(from_ring < 0, from_ring + ring, from_ring)
        of_group = lax.bitwise_xor(group_index, j)
        owner = (of_group * ring + from_ring) * PLANE + in_plane
        index = owner * piece_pages + page_at
        count = part.shape[1]
        page = lax.broadcasted_iota(jnp.int32, (pages, count), 0)
        hit = jnp.where(page == index, 1.0, 0.0).astype(jnp.bfloat16)
        found = dot_f(page_row, hit)[:1].astype(jnp.int32)
        logical = jnp.where(real > 0, found * PAGE + within, -1)
        token = (from_ring * PLANE + in_plane) * tok_slice + of_group * tok_quarter + r
        return jnp.where(suffix > 0, token + LATER, logical)

    def kernel(lengths_ref, tenants_ref, tenant_lengths_ref, page_ref, table_ref, *refs):
        info_ref, order_ref, *spot_refs = refs
        group_index = jnp.full((1, 1), lax.axis_index("group"), jnp.int32)
        tensor_index = lax.axis_index("tensor")
        ring_index = jnp.full((1, 1), lax.div(tensor_index, PLANE), jnp.int32)
        plane_index = jnp.full((1, 1), lax.rem(tensor_index, PLANE), jnp.int32)
        page_row = page_ref[...].astype(jnp.float32).astype(jnp.bfloat16)
        page_row = jnp.broadcast_to(page_row, (16, pages))
        at = 0
        for count, spot_ref in zip(counts, spot_refs):
            part = table_ref[:, at : at + count]
            spot_ref[...] = spots_of(part, page_row, group_index, ring_index, plane_index)
            at += count
        row = lax.broadcasted_iota(jnp.int32, (tok_slice, 1), 0)
        share = jnp.zeros((tok_slice, 1), jnp.int32)
        for j in range(1, groups):
            share = share + jnp.where(row >= j * tok_quarter, 1, 0)
        local = (row - share * tok_quarter) * groups + lax.bitwise_xor(group_index, share)
        column = lax.broadcasted_iota(jnp.int32, (tok_slice, tok_slice), 1)
        order_ref[...] = jnp.where(column == local, 1.0, 0.0).astype(jnp.bfloat16)
        position = local + tensor_index * tok_slice
        low = jnp.zeros((tok_slice, 1), jnp.int32)
        high = jnp.zeros((tok_slice, 1), jnp.int32)
        start = jnp.zeros((tok_slice, 1), jnp.int32)
        begin = 0
        for i in range(requests):
            end = begin + lengths_ref[i]
            inside = (position >= begin) & (position < end)
            tenant = tenants_ref[i]
            first = 0
            tenant_low = 0
            tenant_high = 0
            for t in range(tenant_count):
                last = first + tenant_lengths_ref[t]
                tenant_low = jnp.where(tenant == t, first, tenant_low)
                tenant_high = jnp.where(tenant == t, last, tenant_high)
                first = last
            start = jnp.where(inside, begin, start)
            low = jnp.where(inside, tenant_low, low)
            high = jnp.where(inside, tenant_high, high)
            begin = end
        for i, value in enumerate((low, high, start + LATER, position + LATER)):
            info_ref[:, i : i + 1] = value

    shapes = [
        jax.ShapeDtypeStruct((tok_slice, 4), jnp.int32),
        jax.ShapeDtypeStruct((tok_slice, tok_slice), jnp.bfloat16),
    ] + [jax.ShapeDtypeStruct((1, count), jnp.int32) for count in counts]
    scalar = pl.BlockSpec(memory_space=pltpu.SMEM)
    arrays = [page_table, table]
    return pl.pallas_call(
        after(kernel, len(ready)),
        in_specs=unread(ready) + [scalar, scalar, scalar] + resident(arrays),
        out_specs=resident(shapes),
        out_shape=shapes,
        compiler_params=pltpu.CompilerParams(vmem_limit_bytes=20 * 1024 * 1024),
        cost_estimate=pl.CostEstimate(
            flops=4_000_000_000, bytes_accessed=1_000_000, transcendentals=0
        ),
        name="make_plan",
    )(*ready, lengths, tenants, tenant_lengths, *arrays)


def place_keys(key_refs, spot_ref, token_ref, keys, bias):
    at = 0
    for ref in key_refs:
        rows = ref.shape[0]
        keys[at : at + rows, :] = ref[...]
        at += rows
    columns = token_ref[...]
    spots = spot_ref[...]
    low, high, start, here = (columns[:, i : i + 1] for i in range(4))
    seen = ((spots >= low) & (spots < high)) | ((spots >= start) & (spots <= here))
    bias[...] = jnp.where(seen, 0.0, VERY_NEGATIVE)


SCORE_FACTOR = math.log2(math.e) / math.sqrt(NOPE + ROPE)


def score_rows(queries, keys, bias, pair):
    scores = dot_t(queries, keys[...])
    rows, count = scores.shape
    return (scores.reshape(pair, rows // pair, count) + bias[...][None]).reshape(rows, count)


def near_kernel(block_count, pair, token_ref, spot_ref, order_ref, query_ref, key_up_ref, *refs):
    key_refs = refs[:block_count]
    wide_ref, best_ref, sum_ref, acc_ref, flag_ref, keys, bias = refs[block_count:]
    flag_ref[...] = jnp.zeros_like(flag_ref)
    tokens = query_ref.shape[0]
    place_keys(key_refs, spot_ref, token_ref, keys, bias)
    queries = dot_f(order_ref[...], query_ref[...]).astype(jnp.bfloat16)
    size = NOPE + ROPE
    empty = jnp.zeros((tokens, WIDE - LAT - ROPE), jnp.bfloat16)
    for first in range(0, key_up_ref.shape[0], pair):
        wide = []
        for h in range(first, first + pair):
            part = queries[:, h * size : (h + 1) * size]
            content = dot_f(part[:, :NOPE], key_up_ref[h]).astype(jnp.bfloat16)
            wide.append(jnp.concatenate([content, part[:, NOPE:], empty], axis=1))
        wide = jnp.concatenate(wide, axis=0)
        here = pl.ds(first * tokens, pair * tokens)
        wide_ref[here, :] = wide
        masked = score_rows(wide, keys, bias, pair)
        best = jnp.max(masked, axis=-1, keepdims=True)
        weights = jnp.exp2((masked - best) * SCORE_FACTOR)
        best_ref[here, :] = best
        sum_ref[here, :] = jnp.sum(weights, axis=-1, keepdims=True)
        acc_ref[here, :] = dot_f(weights.astype(jnp.bfloat16), keys[:, :LAT])


def attend_call(kernel, name, inputs, outputs, scratch, work, limit=24):
    shapes = [jax.ShapeDtypeStruct(shape, dtype) for shape, dtype in outputs]
    return pl.pallas_call(
        kernel,
        in_specs=resident(inputs),
        out_specs=resident(shapes),
        out_shape=shapes,
        scratch_shapes=scratch,
        compiler_params=pltpu.CompilerParams(vmem_limit_bytes=limit * 1024 * 1024),
        cost_estimate=pl.CostEstimate(
            flops=work, bytes_accessed=8_000_000, transcendentals=work // 2176
        ),
        name=name,
    )(*inputs)


def key_scratch(tokens, blocks):
    count = sum(block.shape[0] for block in blocks)
    return [pltpu.VMEM((count, WIDE), jnp.bfloat16), pltpu.VMEM((tokens, count), jnp.float32)]


def attend_near(tokens_info, spots, order, queries, key_up, blocks):
    tokens = queries.shape[0]
    heads = key_up.shape[0]
    rows = heads * tokens
    outputs = [
        ((rows, WIDE), jnp.bfloat16),
        ((rows, 1), jnp.float32),
        ((rows, 1), jnp.float32),
        ((rows, LAT), jnp.float32),
        ((8, 128), jnp.float32),
    ]
    return attend_call(
        functools.partial(near_kernel, len(blocks), min(4, heads)),
        "attend_near",
        [tokens_info, spots, order, queries, key_up, *blocks],
        outputs,
        key_scratch(tokens, blocks),
        2 * rows * spots.shape[1] * (LAT + ROPE + LAT),
    )


def add_keys(here, wide_ref, best_ref, sum_ref, acc_ref, keys, bias, pair):
    masked = score_rows(wide_ref[here, :], keys, bias, pair)
    before = best_ref[here, :]
    best = jnp.maximum(before, jnp.max(masked, axis=-1, keepdims=True))
    factor = jnp.exp2((before - best) * SCORE_FACTOR)
    weights = jnp.exp2((masked - best) * SCORE_FACTOR)
    weight_sum = sum_ref[here, :] * factor + jnp.sum(weights, axis=-1, keepdims=True)
    attended = acc_ref[here, :] * factor + dot_f(weights.astype(jnp.bfloat16), keys[:, :LAT])
    return best, weight_sum, attended


def mid_kernel(block_count, pair, token_ref, spot_ref, wide_ref, best_ref, sum_ref, acc_ref, *refs):
    key_refs = refs[:block_count]
    new_best_ref, new_sum_ref, new_acc_ref, flag_ref, keys, bias = refs[block_count:]
    flag_ref[...] = jnp.zeros_like(flag_ref)
    place_keys(key_refs, spot_ref, token_ref, keys, bias)
    rows = pair * token_ref.shape[0]
    for first in range(0, wide_ref.shape[0], rows):
        here = pl.ds(first, rows)
        new_best_ref[here, :], new_sum_ref[here, :], new_acc_ref[here, :] = add_keys(
            here, wide_ref, best_ref, sum_ref, acc_ref, keys, bias, pair
        )


def attend_mid(tokens_info, spots, near, blocks):
    tokens = tokens_info.shape[0]
    rows = near[0].shape[0]
    outputs = [
        ((rows, 1), jnp.float32),
        ((rows, 1), jnp.float32),
        ((rows, LAT), jnp.float32),
        ((8, 128), jnp.float32),
    ]
    return attend_call(
        functools.partial(mid_kernel, len(blocks), min(4, rows // tokens)),
        "attend_mid",
        [tokens_info, spots, *near, *blocks],
        outputs,
        key_scratch(tokens, blocks),
        2 * rows * spots.shape[1] * (LAT + ROPE + LAT),
    )


def far_kernel(
    block_count,
    pair,
    token_ref,
    spot_ref,
    wide_ref,
    best_ref,
    sum_ref,
    acc_ref,
    value_up_ref,
    output_ref,
    *refs,
):
    key_refs = refs[:block_count]
    own_ref, other_ref, keys, bias = refs[block_count:]
    tokens = token_ref.shape[0]
    rows = pair * tokens
    place_keys(key_refs, spot_ref, token_ref, keys, bias)
    heads = []
    for first in range(0, wide_ref.shape[0], rows):
        _, weight_sum, attended = add_keys(
            pl.ds(first, rows), wide_ref, best_ref, sum_ref, acc_ref, keys, bias, pair
        )
        attended = (attended / weight_sum).astype(jnp.bfloat16)
        for h in range(pair):
            part = attended[h * tokens : (h + 1) * tokens]
            value = value_up_ref[first // tokens + h]
            heads.append(dot_f(part, value).astype(jnp.bfloat16))
    total = dot_f(jnp.concatenate(heads, axis=1), output_ref[...])
    mine = own_ref.shape[0]
    own_ref[...] = total[:mine]
    other_ref[...] = total[mine:].astype(jnp.bfloat16)


def attend_far(tokens_info, spots, near, value_up, output_weight, blocks, tok_quarter):
    tokens = tokens_info.shape[0]
    heads = value_up.shape[0]
    width = output_weight.shape[1]
    outputs = [
        ((tok_quarter, width), jnp.float32),
        ((tokens - tok_quarter, width), jnp.bfloat16),
    ]
    return attend_call(
        functools.partial(far_kernel, len(blocks), min(4, heads)),
        "attend_far",
        [tokens_info, spots, *near, value_up, output_weight, *blocks],
        outputs,
        key_scratch(tokens, blocks),
        2 * heads * tokens * spots.shape[1] * (LAT + ROPE + LAT),
    )


def pick_rows(turn, ring, top, block, routes_ref, router_ref, scaled_ref, outs):
    tokens = block.shape[0]
    capacity = outs[0].shape[0]
    tensor_index = lax.axis_index("tensor")
    here = lax.div(tensor_index, PLANE)
    plane_index = lax.rem(tensor_index, PLANE)
    order = ring_order(ring)
    place = sum(jnp.where(here == z, i, 0) for i, z in enumerate(order))
    place = lax.rem(place - turn + ring, ring)
    source = sum(jnp.where(place == i, z, 0) for i, z in enumerate(order))
    routes = routes_ref[lax.rem(here - source + ring, ring)].astype(jnp.float32)
    routes = routes[:, ROPE : ROPE + tokens]
    targets = [
        (here * PLANE + lax.bitwise_xor(plane_index, d)).astype(jnp.float32)
        for d in range(PLANE)
    ]
    hits = [
        jnp.sum(jnp.where(routes[:top] == target, 1.0, 0.0), axis=0, keepdims=True)
        for target in targets
    ]
    before = lax.broadcasted_iota(jnp.int32, (tokens, tokens), 0)
    after_it = lax.broadcasted_iota(jnp.int32, (tokens, tokens), 1)
    earlier = jnp.where(before < after_it, 1.0, 0.0).astype(jnp.bfloat16)
    ranks = dot_f(jnp.concatenate(hits, axis=0).astype(jnp.bfloat16), earlier)
    count = router_ref.shape[0]
    expert = lax.broadcasted_iota(jnp.int32, (count, tokens), 0).astype(jnp.float32)
    named = jnp.zeros((count, tokens), jnp.float32)
    for i in range(top):
        named = named + jnp.where(expert == routes[i : i + 1], 1.0, 0.0)
    picked = jax.nn.sigmoid(dot_t(router_ref[...], block)) * named
    gates = picked / jnp.sum(picked, axis=0, keepdims=True) * ROUTE_SCALING
    slot = lax.broadcasted_iota(jnp.int32, (capacity, tokens), 0).astype(jnp.float32)
    for d, out in enumerate(outs):
        taken = jnp.where(slot == ranks[d : d + 1], hits[d], 0.0)
        out[...] = dot_f(taken.astype(jnp.bfloat16), block).astype(jnp.bfloat16)
        gate = jnp.sum(jnp.where(expert == targets[d], gates, 0.0), axis=0, keepdims=True)
        scaled_ref[d * capacity : (d + 1) * capacity, :] = (taken * gate).astype(jnp.bfloat16)


def pick_outputs(block, capacity):
    tokens, width = block.shape
    pieces = [((capacity, width), jnp.bfloat16)] * PLANE
    return [((PLANE * capacity, tokens), jnp.bfloat16)] + pieces


def settle(hidden, own, others, gain, routes, router, sizes):
    ring, top, capacity = sizes

    def kernel(*refs):
        hidden_ref, own_ref = refs[:2]
        other_refs = refs[2 : 2 + len(others)]
        gain_ref, routes_ref, router_ref = refs[2 + len(others) : 5 + len(others)]
        residual_ref, normed_ref, scaled_ref, *outs = refs[5 + len(others) :]
        total = own_ref[...]
        for ref in other_refs:
            total = total + ref[...].astype(jnp.float32)
        residual = (hidden_ref[...].astype(jnp.float32) + total).astype(jnp.bfloat16)
        residual_ref[...] = residual
        normed = norm_rows(residual, gain_ref[...])
        normed_ref[...] = normed
        pick_rows(0, ring, top, normed, routes_ref, router_ref, scaled_ref, outs)

    outputs = [(hidden.shape, jnp.bfloat16)] * 2 + pick_outputs(hidden, capacity)
    inputs = [hidden, own, *others, gain, routes, router]
    residual, normed, scaled, *pieces = call(kernel, "settle", inputs, outputs, 10_000_000_000)
    return residual, normed, scaled, pieces


def choose(step, block, routes, router, sizes, ready):
    ring, top, capacity = sizes
    width = block.shape[1]

    def kernel(block_ref, routes_ref, router_ref, scaled_ref, *outs):
        pick_rows(step, ring, top, block_ref[...], routes_ref, router_ref, scaled_ref, outs)

    outputs = [((PLANE * capacity, block.shape[0]), jnp.bfloat16)]
    outputs += [((capacity, width), jnp.bfloat16)] * PLANE
    inputs = [block, routes, router]
    scaled, *pieces = call(kernel, "choose", inputs, outputs, 70_000_000, ready=ready)
    return scaled, pieces


def join_arrived(arrived, capacity, ready):
    def kernel(*refs):
        joined_ref = refs[PLANE]
        for d, ref in enumerate(refs[:PLANE]):
            joined_ref[d * capacity : (d + 1) * capacity, :] = ref[:capacity, :]

    outputs = [((PLANE * capacity, arrived[0].shape[1]), jnp.bfloat16)]
    return call(kernel, "join_arrived", arrived, outputs, 0, ready=ready)[0]


def blend(own, others, pieces, ready):
    capacity = own.shape[0] // PLANE
    first = pieces[0].shape[0] if pieces else 0
    inputs = [own, *others, *pieces]

    def kernel(*refs):
        outs = refs[len(inputs) :]
        total = refs[0][...]
        for ref in refs[1 : 1 + len(others)]:
            total = total + ref[...].astype(jnp.float32)
        total = total.astype(jnp.bfloat16)
        for d, out in enumerate(outs):
            if pieces:
                out[:first, :] = refs[1 + len(others) + d][...]
            out[first:, :] = total[d * capacity : (d + 1) * capacity]

    outputs = [((first + capacity, own.shape[1]), jnp.bfloat16)] * PLANE
    return call(kernel, "blend", inputs, outputs, 1_000_000, ready=ready)


def expert_apply(pieces, kept, gate_part, up_part, down_part):
    total = sum(piece.shape[0] for piece in pieces)
    units, width = gate_part.shape

    def kernel(*refs):
        row_refs = refs[: len(pieces)]
        gate_ref, up_ref, down_ref, own_ref, other_ref, flag_ref = refs[len(pieces) :]
        flag_ref[...] = jnp.zeros_like(flag_ref)
        rows = jnp.concatenate([ref[...] for ref in row_refs], axis=0)
        gate_vals = dot_t(rows, gate_ref[...])
        up_vals = dot_t(rows, up_ref[...])
        hidden = (jax.nn.silu(gate_vals) * up_vals).astype(jnp.bfloat16)
        partial = dot_f(hidden, down_ref[...])
        own_ref[...] = partial[:kept]
        other_ref[...] = partial[kept:].astype(jnp.bfloat16)

    outputs = [
        ((kept, width), jnp.float32),
        ((total - kept, width), jnp.bfloat16),
        ((8, 128), jnp.float32),
    ]
    inputs = [*pieces, gate_part, up_part, down_part]
    return call(kernel, "experts", inputs, outputs, 6 * total * width * units, limit=20)


def scatter_sum(scaled_ref, piece_refs, running_ref):
    size = scaled_ref.shape[0] // PLANE
    parts = [ref[ref.shape[0] - size :, :] for ref in piece_refs]
    returned = jnp.concatenate(parts, axis=0)
    total = lax.dot_general(
        scaled_ref[...], returned, (((0,), (0,)), ((), ())), preferred_element_type=jnp.float32
    )
    if running_ref is not None:
        total = total + running_ref[...].astype(jnp.float32)
    return total


def collect(scaled, pieces, running):
    extra = [] if running is None else [running]

    def kernel(scaled_ref, *refs):
        running_ref = refs[len(pieces)] if extra else None
        total = scatter_sum(scaled_ref, refs[: len(pieces)], running_ref)
        refs[-1][...] = total.astype(jnp.bfloat16)

    shape = (scaled.shape[1], pieces[0].shape[1])
    inputs = [scaled, *pieces, *extra]
    return call(kernel, "collect", inputs, [(shape, jnp.bfloat16)], 35_000_000)[0]


def conclude(scaled, pieces, running, residual, gain):
    extra = [] if running is None else [running]

    def kernel(residual_ref, gain_ref, scaled_ref, *refs):
        running_ref = refs[len(pieces)] if extra else None
        total = scatter_sum(scaled_ref, refs[: len(pieces)], running_ref)
        layer = (residual_ref[...].astype(jnp.float32) + total).astype(jnp.bfloat16)
        refs[-2][...] = layer
        refs[-1][...] = norm_rows(layer, gain_ref[...])

    inputs = [residual, gain, scaled, *pieces, *extra]
    return call(kernel, "conclude", inputs, [(residual.shape, jnp.bfloat16)] * 2, 35_000_000)


def project(shares, order, query_weight, latent_rows, layer_rows):
    def kernel(order_ref, query_ref, latent_ref, layer_ref, *refs):
        share_refs = refs[: len(shares)]
        queries_ref, latents_ref, copy_ref = refs[len(shares) :]
        copy_ref[...] = layer_ref[...]
        rows = jnp.concatenate([ref[...] for ref in share_refs], axis=0)
        rows = lax.dot_general(
            order_ref[...], rows, (((0,), (0,)), ((), ())), preferred_element_type=jnp.float32
        ).astype(jnp.bfloat16)
        latents_ref[...] = dot_t(latent_ref[...], rows).astype(jnp.bfloat16)
        queries_ref[...] = dot_f(rows, query_ref[...]).astype(jnp.bfloat16)

    tokens = order.shape[0]
    outputs = [
        ((tokens, query_weight.shape[1]), jnp.bfloat16),
        ((latent_rows.shape[0], tokens), jnp.bfloat16),
        (layer_rows.shape, jnp.bfloat16),
    ]
    inputs = [order, query_weight, latent_rows, layer_rows, *shares]
    return call(kernel, "project", inputs, outputs, 1_000_000_000, limit=16)


def per_device(
    hidden_in,
    queries,
    suffix_latent,
    prefix_latent,
    key_up,
    value_up,
    output_weight,
    norm_gain,
    router,
    expert_gate,
    expert_up,
    expert_down,
    next_gain,
    next_query_weight,
    next_latent_weight,
    suffix_lengths,
    request_tenant,
    tenant_lengths,
    page_table,
    routes,
):
    tok_slice = hidden_in.shape[0]
    groups = lax.axis_size("group")
    ring = lax.axis_size("tensor") // PLANE
    tok_quarter = tok_slice // groups
    expert_count = router.shape[1]
    top_count = routes.shape[2]
    capacity = max(2, 4 * tok_quarter * top_count // (3 * expert_count))
    capacity = -(-capacity // 16) * 16

    real_rows = prefix_latent.shape[0]
    piece_rows = -(-real_rows // 16) * 16
    piece = prefix_latent
    if piece_rows != real_rows:
        piece = jnp.pad(piece, ((0, piece_rows - real_rows), (0, 0)))
    routes_columns = jnp.transpose(routes, (2, 0, 1))
    full, lite = join_share(piece, suffix_latent.T, routes_columns, tok_quarter)
    along = [send_round(full, PLANE)] + [send_round(lite, PLANE * k) for k in range(2, ring)]
    near_segments = []
    far_segments = []
    for k in range(ring):
        near_segments.append((k, piece_rows, real_rows, 0))
        far_segments.append((k, piece_rows, real_rows, 0))
        if k < 2:
            near_segments.append((k, tok_quarter, 0, 1))
    far_segments.append((0, tok_quarter, 0, 2))
    prefix_rows = ring * piece_rows
    first_rows = (prefix_rows - tok_quarter) // 2
    diagonal = segment_rows(3, far_segments)
    sides = (
        segment_rows(0, near_segments),
        segment_rows(1, far_segments) + segment_rows(2, far_segments),
        diagonal[:first_rows] + diagonal[prefix_rows:] + diagonal[first_rows:prefix_rows],
    )
    tables = [key_table(groups, side) for side in sides]
    tokens_info, permutation, near_spots, mid_spots, far_spots = make_plan(
        jnp.asarray(np.concatenate(tables, axis=1)),
        [part.shape[1] for part in tables],
        suffix_lengths,
        request_tenant,
        tenant_lengths,
        page_table[None, :],
        ring,
        real_rows,
        (tok_slice, tok_quarter, groups),
        [full],
    )

    column, plane, routes_ring = join_column(
        [full, *along], piece_rows, tok_quarter, [near_spots]
    )
    plane = [send_plane(part, d + 1) for d, part in enumerate(plane)]
    near_blocks = [send_group(column, j) if j else column for j in range(groups)]

    *near, near_flag = attend_near(
        tokens_info, near_spots, permutation, queries, key_up, near_blocks
    )
    beside = pass_on(plane, [near_flag])
    first, second = halves(beside[1], beside[0], first_rows, prefix_rows)
    across = [send_plane(first, 1), send_plane(second, 2)]
    mid_blocks = [send_group(block, j) if j else block for j in range(groups) for block in beside]
    *mid, mid_flag = attend_mid(tokens_info, mid_spots, near, mid_blocks)
    near = [near[0], *mid]
    across = pass_on(across, [mid_flag])
    far_blocks = [send_group(block, j) if j else block for j in range(groups) for block in across]
    attend_own, attend_other = attend_far(
        tokens_info, far_spots, near, value_up, output_weight, far_blocks, tok_quarter
    )

    hidden_own = dot_f(permutation[:tok_quarter], hidden_in).astype(jnp.bfloat16)
    others = [
        send_group(attend_other[(j - 1) * tok_quarter : j * tok_quarter], j)
        for j in range(1, groups)
    ]
    sizes = (ring, top_count, capacity)
    experts_columns = router.T
    residual, block, scaled, pieces = settle(
        hidden_own,
        attend_own,
        others,
        norm_gain[None, :],
        routes_ring,
        experts_columns,
        sizes,
    )

    kept = PLANE * capacity
    gate_part = jnp.transpose(expert_gate, (0, 2, 1))[0]
    up_part = jnp.transpose(expert_up, (0, 2, 1))[0]
    down_part = expert_down[0]
    scales = [scaled]
    results = []
    running = None
    payload = pieces
    for step in range(1, ring + 4):
        if step <= ring - 1:
            block = send_ring(block, ring)
        arrived = send_pieces(payload)
        if 4 <= step:
            k = step - 3
            if k < ring:
                landed = running
                total = collect(scales[k], arrived, running)
                running = send_ring(total, ring)
            else:
                break
        payload = []
        back = step - 2 if step - 2 < ring else 0
        if step >= 3:
            own, other, _ = results[back]
            if back:
                along_z = [block] if step <= ring - 1 else [landed] if step > 4 else []
                other = pass_on([other], arrived[1:] + along_z)[0]
            others = [
                send_group(other[(j - 1) * kept : j * kept], j) for j in range(1, groups)
            ]
        if step <= ring:
            ready = [results[step - 2][2]] if step >= 2 else []
            if step <= ring - 1:
                scaled, payload = choose(
                    step, block, routes_ring, experts_columns, sizes, ready
                )
                scales.append(scaled)
                ready = [scaled]
            joined = join_arrived(arrived, capacity, ready)
            rows = [send_group(joined, j) if j else joined for j in range(groups)]
            results.append(expert_apply(rows, kept, gate_part, up_part, down_part))
        if step >= 3:
            payload = blend(own, others, payload, [] if back else [total])
    layer_rows, normed_next = conclude(
        scales[0], arrived, running, residual, next_gain[None, :]
    )

    shares = [send_group(normed_next, j) if j else normed_next for j in range(groups)]
    next_queries, next_latent, layer_rows = project(
        shares, permutation, next_query_weight, next_latent_weight.T, layer_rows
    )
    return (layer_rows[:, None, :], next_queries, next_latent.T)


def solution(mesh):
    return jax.shard_map(
        per_device,
        mesh=mesh,
        in_specs=(
            P("tensor", None),
            P("tensor", "group"),
            P("tensor", None),
            P(("group", "tensor"), None),
            P("group", None, None),
            P("group", None, None),
            P("group", None),
            P(),
            P(),
            P("tensor", None, "group"),
            P("tensor", None, "group"),
            P("tensor", "group", None),
            P(),
            P(None, "group"),
            P(None, "group"),
            P(),
            P(),
            P(),
            P(),
            P(None, "tensor", None),
        ),
        out_specs=(P("tensor", "group", None), P("tensor", "group"), P("tensor", "group")),
        check_vma=False,
    )
```

```python
import functools
import math

import jax
import jax.numpy as jnp
import numpy as np
from jax import lax
from jax.experimental import pallas as pl
from jax.experimental.pallas import tpu as pltpu
from jax.sharding import PartitionSpec as P

NOPE = 128
ROPE = 64
LAT = 512
PAGE = 8
PLANE = 4
ROUTE_ROWS = 16
WIDE = 640

VERY_NEGATIVE = -1e30
ROUTE_SCALING = 2.446
NORM_EPSILON = 1e-06


def ring_order(count):
    odd = list(range(1, count, 2))
    even = list(range(2, count, 2))
    return [0] + odd + even[::-1]


def send_ring(block, count, steps=1):
    order = ring_order(count)
    after = {order[i]: order[(i + steps) % count] for i in range(count)}
    route = [
        (z * PLANE + p, after[z] * PLANE + p) for z in range(count) for p in range(PLANE)
    ]
    return lax.ppermute(block, "tensor", route)


def send_round(block, distance):
    count = lax.axis_size("tensor")
    return lax.ppermute(block, "tensor", [(i, (i + distance) % count) for i in range(count)])


def send_plane(block, distance):
    devices = range(lax.axis_size("tensor"))
    return lax.ppermute(block, "tensor", [(i, i ^ distance) for i in devices])


def send_pieces(pieces):
    sent = {d: send_plane(pieces[d], d) for d in reversed(range(1, PLANE))}
    return [pieces[0]] + [sent[d] for d in range(1, PLANE)]


def send_group(block, distance):
    devices = range(lax.axis_size("group"))
    return lax.ppermute(block, "group", [(i, i ^ distance) for i in devices])


def norm_rows(row_block, gain_vector):
    values = row_block.astype(jnp.float32)
    mean_square = jnp.mean(values * values, axis=-1, keepdims=True)
    return (
        values * lax.rsqrt(mean_square + NORM_EPSILON) * gain_vector.astype(jnp.float32)
    ).astype(jnp.bfloat16)


def dot_t(left, right):
    return lax.dot_general(
        left, right, (((1,), (1,)), ((), ())), preferred_element_type=jnp.float32
    )


def dot_f(left, right):
    return jnp.dot(left, right, preferred_element_type=jnp.float32)


def whole(array):
    return pl.BlockSpec(array.shape, lambda *i: (0,) * len(array.shape))


def after(kernel, count):
    def inner(*refs):
        kernel(*refs[count:])

    return inner


def resident(arrays):
    return [pl.BlockSpec(memory_space=pltpu.VMEM) for _ in arrays]


def unread(arrays):
    return [pl.BlockSpec(memory_space=pl.ANY) for _ in arrays]


def call(kernel, name, inputs, outputs, flops, limit=12, ready=(), streamed=False):
    shapes = [jax.ShapeDtypeStruct(shape, dtype) for shape, dtype in outputs]
    moved = sum(a.size * a.dtype.itemsize for a in list(inputs) + shapes)
    if streamed:
        places = {
            "grid": (1,),
            "in_specs": unread(ready) + [whole(a) for a in inputs],
            "out_specs": [whole(shape) for shape in shapes],
        }
    else:
        places = {
            "in_specs": unread(ready) + resident(inputs),
            "out_specs": resident(shapes),
        }
    return pl.pallas_call(
        after(kernel, len(ready)),
        **places,
        out_shape=shapes,
        compiler_params=pltpu.CompilerParams(vmem_limit_bytes=limit * 1024 * 1024),
        cost_estimate=pl.CostEstimate(flops=flops, bytes_accessed=moved, transcendentals=0),
        name=name,
    )(*ready, *inputs)


def join_share(piece, suffix_columns, routes_columns, tok_quarter):
    rows = piece.shape[0]
    tokens = suffix_columns.shape[1]
    top, groups, _ = routes_columns.shape

    def kernel(piece_ref, suffix_ref, routes_ref, full_ref, lite_ref):
        group_index = lax.axis_index("group")
        shape = (tok_quarter, tokens)
        row = lax.broadcasted_iota(jnp.int32, shape, 0)
        token = lax.broadcasted_iota(jnp.int32, shape, 1)
        select = jnp.where(token == group_index * tok_quarter + row, 1.0, 0.0)
        share = dot_t(select.astype(jnp.bfloat16), suffix_ref[...]).astype(jnp.bfloat16)
        named = jnp.zeros((top, tok_quarter), jnp.float32)
        for j in range(groups):
            part = routes_ref[:, j, :].astype(jnp.float32)
            named = jnp.where(group_index == j, part, named)
        named = jnp.concatenate([named, jnp.zeros((rows - top, tok_quarter), jnp.float32)], axis=0)
        spare = WIDE - LAT - ROPE - tok_quarter
        if spare:
            named = jnp.concatenate([named, jnp.zeros((rows, spare), jnp.float32)], axis=1)
        named = named.astype(jnp.bfloat16)
        piece = piece_ref[...]
        last = jnp.concatenate([piece[:, LAT:], named], axis=1)
        for ref in (full_ref, lite_ref):
            ref[:rows, :LAT] = piece[:, :LAT]
            ref[:rows, LAT:] = last
        empty = jnp.zeros((tok_quarter, WIDE - LAT - ROPE), jnp.bfloat16)
        full_ref[rows:, :LAT] = share[:, :LAT]
        full_ref[rows:, LAT:] = jnp.concatenate([share[:, LAT:], empty], axis=1)

    outputs = [((size, WIDE), piece.dtype) for size in (rows + tok_quarter, rows)]
    inputs = [piece, suffix_columns, routes_columns]
    return call(kernel, "join_share", inputs, outputs, 10_000_000, limit=58, streamed=True)


def join_column(blocks, rows, share, ready):
    count = len(blocks)

    def kernel(*refs):
        block_refs = refs[:count]
        near_ref, *far_refs, routes_ref = refs[count:]
        plane_index = lax.rem(lax.axis_index("tensor"), PLANE)
        at = 0
        for i, ref in enumerate(block_refs):
            near_ref[at : at + ref.shape[0], :] = ref[...]
            at += ref.shape[0]
            routes_ref[i] = ref[:ROUTE_ROWS, LAT:]
        here = block_refs[0][rows:, :].astype(jnp.float32)
        before = block_refs[1][rows:, :].astype(jnp.float32)
        for d, far_ref in enumerate(far_refs):
            for i, ref in enumerate(block_refs):
                far_ref[i * rows : (i + 1) * rows, :] = ref[:rows, :]
            later = plane_index < lax.bitwise_xor(plane_index, d + 1)
            part = jnp.where(later, here, before).astype(jnp.bfloat16)
            far_ref[far_ref.shape[0] - share :, :] = part

    dtype = blocks[0].dtype
    outputs = [((count * rows + 2 * share, WIDE), dtype)]
    outputs += [((count * rows + share, WIDE), dtype)] * (PLANE - 2)
    outputs.append(((count, ROUTE_ROWS, WIDE - LAT), dtype))
    near, *far, routes = call(kernel, "join_column", blocks, outputs, 0, ready=ready)
    return near, far, routes


def halves(by_y, by_x, first, prefix):
    share = by_y.shape[0] - prefix

    def kernel(by_y_ref, by_x_ref, first_ref, second_ref):
        first_ref[:first, :] = by_y_ref[:first, :]
        first_ref[first:, :] = by_y_ref[prefix:, :]
        second_ref[...] = by_x_ref[first:prefix, :]

    outputs = [((first + share, WIDE), by_y.dtype), ((prefix - first, WIDE), by_y.dtype)]
    return call(kernel, "halves", [by_y, by_x], outputs, 0)


def pass_on(blocks, ready):
    first = len(ready)

    def kernel(*refs):
        pass

    return pl.pallas_call(
        kernel,
        in_specs=unread(ready) + unread(blocks),
        out_specs=unread(blocks),
        out_shape=[jax.ShapeDtypeStruct(block.shape, block.dtype) for block in blocks],
        input_output_aliases={first + i: i for i in range(len(blocks))},
        compiler_params=pltpu.CompilerParams(vmem_limit_bytes=1024 * 1024),
        name="pass_on",
    )(*ready, *blocks)


LATER = 1 << 20


def segment_rows(d, segments):
    return [(d, k, r, s, r < real) for k, count, real, s in segments for r in range(count)]


def key_table(groups, side):
    rows = [(j, *row) for j in range(groups) for row in side]
    table = np.zeros((8, len(rows)), np.int32)
    table[:6] = np.array(rows, np.int32).T
    table[6] = table[3] // PAGE
    table[7] = table[3] % PAGE
    return table


def make_plan(table, counts, lengths, tenants, tenant_lengths, page_table, ring, piece_rows, sizes, ready):
    tok_slice, tok_quarter, groups = sizes
    requests = lengths.shape[0]
    tenant_count = tenant_lengths.shape[0]
    pages = page_table.shape[1]
    piece_pages = piece_rows // PAGE

    def spots_of(part, page_row, group_index, ring_index, plane_index):
        j, d, k, r, suffix, real, page_at, within = (part[i : i + 1, :] for i in range(8))
        in_plane = lax.bitwise_xor(plane_index, d)
        k = jnp.where(suffix == 2, jnp.where(in_plane < plane_index, 0, 1), k)
        from_ring = ring_index - k
        from_ring = jnp.where(from_ring < 0, from_ring + ring, from_ring)
        of_group = lax.bitwise_xor(group_index, j)
        owner = (of_group * ring + from_ring) * PLANE + in_plane
        index = owner * piece_pages + page_at
        count = part.shape[1]
        page = lax.broadcasted_iota(jnp.int32, (pages, count), 0)
        hit = jnp.where(page == index, 1.0, 0.0).astype(jnp.bfloat16)
        found = dot_f(page_row, hit)[:1].astype(jnp.int32)
        logical = jnp.where(real > 0, found * PAGE + within, -1)
        token = (from_ring * PLANE + in_plane) * tok_slice + of_group * tok_quarter + r
        return jnp.where(suffix > 0, token + LATER, logical)

    def kernel(lengths_ref, tenants_ref, tenant_lengths_ref, page_ref, table_ref, *refs):
        info_ref, order_ref, *spot_refs = refs
        group_index = jnp.full((1, 1), lax.axis_index("group"), jnp.int32)
        tensor_index = lax.axis_index("tensor")
        ring_index = jnp.full((1, 1), lax.div(tensor_index, PLANE), jnp.int32)
        plane_index = jnp.full((1, 1), lax.rem(tensor_index, PLANE), jnp.int32)
        page_row = page_ref[...].astype(jnp.float32).astype(jnp.bfloat16)
        page_row = jnp.broadcast_to(page_row, (16, pages))
        at = 0
        for count, spot_ref in zip(counts, spot_refs):
            part = table_ref[:, at : at + count]
            spot_ref[...] = spots_of(part, page_row, group_index, ring_index, plane_index)
            at += count
        row = lax.broadcasted_iota(jnp.int32, (tok_slice, 1), 0)
        share = jnp.zeros((tok_slice, 1), jnp.int32)
        for j in range(1, groups):
            share = share + jnp.where(row >= j * tok_quarter, 1, 0)
        local = (row - share * tok_quarter) * groups + lax.bitwise_xor(group_index, share)
        column = lax.broadcasted_iota(jnp.int32, (tok_slice, tok_slice), 1)
        order_ref[...] = jnp.where(column == local, 1.0, 0.0).astype(jnp.bfloat16)
        position = local + tensor_index * tok_slice
        low = jnp.zeros((tok_slice, 1), jnp.int32)
        high = jnp.zeros((tok_slice, 1), jnp.int32)
        start = jnp.zeros((tok_slice, 1), jnp.int32)
        begin = 0
        for i in range(requests):
            end = begin + lengths_ref[i]
            inside = (position >= begin) & (position < end)
            tenant = tenants_ref[i]
            first = 0
            tenant_low = 0
            tenant_high = 0
            for t in range(tenant_count):
                last = first + tenant_lengths_ref[t]
                tenant_low = jnp.where(tenant == t, first, tenant_low)
                tenant_high = jnp.where(tenant == t, last, tenant_high)
                first = last
            start = jnp.where(inside, begin, start)
            low = jnp.where(inside, tenant_low, low)
            high = jnp.where(inside, tenant_high, high)
            begin = end
        for i, value in enumerate((low, high, start + LATER, position + LATER)):
            info_ref[:, i : i + 1] = value

    shapes = [
        jax.ShapeDtypeStruct((tok_slice, 4), jnp.int32),
        jax.ShapeDtypeStruct((tok_slice, tok_slice), jnp.bfloat16),
    ] + [jax.ShapeDtypeStruct((1, count), jnp.int32) for count in counts]
    scalar = pl.BlockSpec(memory_space=pltpu.SMEM)
    arrays = [page_table, table]
    return pl.pallas_call(
        after(kernel, len(ready)),
        in_specs=unread(ready) + [scalar, scalar, scalar] + resident(arrays),
        out_specs=resident(shapes),
        out_shape=shapes,
        compiler_params=pltpu.CompilerParams(vmem_limit_bytes=20 * 1024 * 1024),
        cost_estimate=pl.CostEstimate(
            flops=4_000_000_000, bytes_accessed=1_000_000, transcendentals=0
        ),
        name="make_plan",
    )(*ready, lengths, tenants, tenant_lengths, *arrays)


def place_keys(key_refs, spot_ref, token_ref, keys, bias):
    at = 0
    for ref in key_refs:
        rows = ref.shape[0]
        keys[at : at + rows, :] = ref[...]
        at += rows
    columns = token_ref[...]
    spots = spot_ref[...]
    low, high, start, here = (columns[:, i : i + 1] for i in range(4))
    seen = ((spots >= low) & (spots < high)) | ((spots >= start) & (spots <= here))
    bias[...] = jnp.where(seen, 0.0, VERY_NEGATIVE)


SCORE_FACTOR = math.log2(math.e) / math.sqrt(NOPE + ROPE)


def score_rows(queries, keys, bias, pair):
    scores = dot_t(queries, keys[...])
    rows, count = scores.shape
    return (scores.reshape(pair, rows // pair, count) + bias[...][None]).reshape(rows, count)


def near_kernel(block_count, pair, token_ref, spot_ref, order_ref, query_ref, key_up_ref, *refs):
    key_refs = refs[:block_count]
    wide_ref, best_ref, sum_ref, acc_ref, flag_ref, keys, bias = refs[block_count:]
    flag_ref[...] = jnp.zeros_like(flag_ref)
    tokens = query_ref.shape[0]
    place_keys(key_refs, spot_ref, token_ref, keys, bias)
    queries = dot_f(order_ref[...], query_ref[...]).astype(jnp.bfloat16)
    size = NOPE + ROPE
    empty = jnp.zeros((tokens, WIDE - LAT - ROPE), jnp.bfloat16)
    for first in range(0, key_up_ref.shape[0], pair):
        wide = []
        for h in range(first, first + pair):
            part = queries[:, h * size : (h + 1) * size]
            content = dot_f(part[:, :NOPE], key_up_ref[h]).astype(jnp.bfloat16)
            wide.append(jnp.concatenate([content, part[:, NOPE:], empty], axis=1))
        wide = jnp.concatenate(wide, axis=0)
        here = pl.ds(first * tokens, pair * tokens)
        wide_ref[here, :] = wide
        masked = score_rows(wide, keys, bias, pair)
        best = jnp.max(masked, axis=-1, keepdims=True)
        weights = jnp.exp2((masked - best) * SCORE_FACTOR)
        best_ref[here, :] = best
        sum_ref[here, :] = jnp.sum(weights, axis=-1, keepdims=True)
        acc_ref[here, :] = dot_f(weights.astype(jnp.bfloat16), keys[:, :LAT])


def attend_call(kernel, name, inputs, outputs, scratch, work, limit=24):
    shapes = [jax.ShapeDtypeStruct(shape, dtype) for shape, dtype in outputs]
    return pl.pallas_call(
        kernel,
        in_specs=resident(inputs),
        out_specs=resident(shapes),
        out_shape=shapes,
        scratch_shapes=scratch,
        compiler_params=pltpu.CompilerParams(vmem_limit_bytes=limit * 1024 * 1024),
        cost_estimate=pl.CostEstimate(
            flops=work, bytes_accessed=8_000_000, transcendentals=work // 2176
        ),
        name=name,
    )(*inputs)


def key_scratch(tokens, blocks):
    count = sum(block.shape[0] for block in blocks)
    return [pltpu.VMEM((count, WIDE), jnp.bfloat16), pltpu.VMEM((tokens, count), jnp.float32)]


def attend_near(tokens_info, spots, order, queries, key_up, blocks):
    tokens = queries.shape[0]
    heads = key_up.shape[0]
    rows = heads * tokens
    outputs = [
        ((rows, WIDE), jnp.bfloat16),
        ((rows, 1), jnp.float32),
        ((rows, 1), jnp.float32),
        ((rows, LAT), jnp.float32),
        ((8, 128), jnp.float32),
    ]
    return attend_call(
        functools.partial(near_kernel, len(blocks), min(4, heads)),
        "attend_near",
        [tokens_info, spots, order, queries, key_up, *blocks],
        outputs,
        key_scratch(tokens, blocks),
        2 * rows * spots.shape[1] * (LAT + ROPE + LAT),
    )


def add_keys(here, wide_ref, best_ref, sum_ref, acc_ref, keys, bias, pair):
    masked = score_rows(wide_ref[here, :], keys, bias, pair)
    before = best_ref[here, :]
    best = jnp.maximum(before, jnp.max(masked, axis=-1, keepdims=True))
    factor = jnp.exp2((before - best) * SCORE_FACTOR)
    weights = jnp.exp2((masked - best) * SCORE_FACTOR)
    weight_sum = sum_ref[here, :] * factor + jnp.sum(weights, axis=-1, keepdims=True)
    attended = acc_ref[here, :] * factor + dot_f(weights.astype(jnp.bfloat16), keys[:, :LAT])
    return best, weight_sum, attended


def mid_kernel(block_count, pair, token_ref, spot_ref, wide_ref, best_ref, sum_ref, acc_ref, *refs):
    key_refs = refs[:block_count]
    new_best_ref, new_sum_ref, new_acc_ref, flag_ref, keys, bias = refs[block_count:]
    flag_ref[...] = jnp.zeros_like(flag_ref)
    place_keys(key_refs, spot_ref, token_ref, keys, bias)
    rows = pair * token_ref.shape[0]
    for first in range(0, wide_ref.shape[0], rows):
        here = pl.ds(first, rows)
        new_best_ref[here, :], new_sum_ref[here, :], new_acc_ref[here, :] = add_keys(
            here, wide_ref, best_ref, sum_ref, acc_ref, keys, bias, pair
        )


def attend_mid(tokens_info, spots, near, blocks):
    tokens = tokens_info.shape[0]
    rows = near[0].shape[0]
    outputs = [
        ((rows, 1), jnp.float32),
        ((rows, 1), jnp.float32),
        ((rows, LAT), jnp.float32),
        ((8, 128), jnp.float32),
    ]
    return attend_call(
        functools.partial(mid_kernel, len(blocks), min(4, rows // tokens)),
        "attend_mid",
        [tokens_info, spots, *near, *blocks],
        outputs,
        key_scratch(tokens, blocks),
        2 * rows * spots.shape[1] * (LAT + ROPE + LAT),
    )


def far_kernel(
    block_count,
    pair,
    token_ref,
    spot_ref,
    wide_ref,
    best_ref,
    sum_ref,
    acc_ref,
    value_up_ref,
    output_ref,
    *refs,
):
    key_refs = refs[:block_count]
    own_ref, other_ref, keys, bias = refs[block_count:]
    tokens = token_ref.shape[0]
    rows = pair * tokens
    place_keys(key_refs, spot_ref, token_ref, keys, bias)
    heads = []
    for first in range(0, wide_ref.shape[0], rows):
        _, weight_sum, attended = add_keys(
            pl.ds(first, rows), wide_ref, best_ref, sum_ref, acc_ref, keys, bias, pair
        )
        attended = (attended / weight_sum).astype(jnp.bfloat16)
        for h in range(pair):
            part = attended[h * tokens : (h + 1) * tokens]
            value = value_up_ref[first // tokens + h]
            heads.append(dot_f(part, value).astype(jnp.bfloat16))
    total = dot_f(jnp.concatenate(heads, axis=1), output_ref[...])
    mine = own_ref.shape[0]
    own_ref[...] = total[:mine]
    other_ref[...] = total[mine:].astype(jnp.bfloat16)


def attend_far(tokens_info, spots, near, value_up, output_weight, blocks, tok_quarter):
    tokens = tokens_info.shape[0]
    heads = value_up.shape[0]
    width = output_weight.shape[1]
    outputs = [
        ((tok_quarter, width), jnp.float32),
        ((tokens - tok_quarter, width), jnp.bfloat16),
    ]
    return attend_call(
        functools.partial(far_kernel, len(blocks), min(4, heads)),
        "attend_far",
        [tokens_info, spots, *near, value_up, output_weight, *blocks],
        outputs,
        key_scratch(tokens, blocks),
        2 * heads * tokens * spots.shape[1] * (LAT + ROPE + LAT),
    )


def pick_rows(turn, ring, top, block, routes_ref, router_ref, scaled_ref, outs):
    tokens = block.shape[0]
    capacity = outs[0].shape[0]
    tensor_index = lax.axis_index("tensor")
    here = lax.div(tensor_index, PLANE)
    plane_index = lax.rem(tensor_index, PLANE)
    order = ring_order(ring)
    place = sum(jnp.where(here == z, i, 0) for i, z in enumerate(order))
    place = lax.rem(place - turn + ring, ring)
    source = sum(jnp.where(place == i, z, 0) for i, z in enumerate(order))
    routes = routes_ref[lax.rem(here - source + ring, ring)].astype(jnp.float32)
    routes = routes[:, ROPE : ROPE + tokens]
    targets = [
        (here * PLANE + lax.bitwise_xor(plane_index, d)).astype(jnp.float32)
        for d in range(PLANE)
    ]
    hits = [
        jnp.sum(jnp.where(routes[:top] == target, 1.0, 0.0), axis=0, keepdims=True)
        for target in targets
    ]
    before = lax.broadcasted_iota(jnp.int32, (tokens, tokens), 0)
    after_it = lax.broadcasted_iota(jnp.int32, (tokens, tokens), 1)
    earlier = jnp.where(before < after_it, 1.0, 0.0).astype(jnp.bfloat16)
    ranks = dot_f(jnp.concatenate(hits, axis=0).astype(jnp.bfloat16), earlier)
    count = router_ref.shape[0]
    expert = lax.broadcasted_iota(jnp.int32, (count, tokens), 0).astype(jnp.float32)
    named = jnp.zeros((count, tokens), jnp.float32)
    for i in range(top):
        named = named + jnp.where(expert == routes[i : i + 1], 1.0, 0.0)
    picked = jax.nn.sigmoid(dot_t(router_ref[...], block)) * named
    gates = picked / jnp.sum(picked, axis=0, keepdims=True) * ROUTE_SCALING
    slot = lax.broadcasted_iota(jnp.int32, (capacity, tokens), 0).astype(jnp.float32)
    for d, out in enumerate(outs):
        taken = jnp.where(slot == ranks[d : d + 1], hits[d], 0.0)
        out[...] = dot_f(taken.astype(jnp.bfloat16), block).astype(jnp.bfloat16)
        gate = jnp.sum(jnp.where(expert == targets[d], gates, 0.0), axis=0, keepdims=True)
        scaled_ref[d * capacity : (d + 1) * capacity, :] = (taken * gate).astype(jnp.bfloat16)


def pick_outputs(block, capacity):
    tokens, width = block.shape
    pieces = [((capacity, width), jnp.bfloat16)] * PLANE
    return [((PLANE * capacity, tokens), jnp.bfloat16)] + pieces


def settle(hidden, own, others, gain, routes, router, sizes):
    ring, top, capacity = sizes

    def kernel(*refs):
        hidden_ref, own_ref = refs[:2]
        other_refs = refs[2 : 2 + len(others)]
        gain_ref, routes_ref, router_ref = refs[2 + len(others) : 5 + len(others)]
        residual_ref, normed_ref, scaled_ref, *outs = refs[5 + len(others) :]
        total = own_ref[...]
        for ref in other_refs:
            total = total + ref[...].astype(jnp.float32)
        residual = (hidden_ref[...].astype(jnp.float32) + total).astype(jnp.bfloat16)
        residual_ref[...] = residual
        normed = norm_rows(residual, gain_ref[...])
        normed_ref[...] = normed
        pick_rows(0, ring, top, normed, routes_ref, router_ref, scaled_ref, outs)

    outputs = [(hidden.shape, jnp.bfloat16)] * 2 + pick_outputs(hidden, capacity)
    inputs = [hidden, own, *others, gain, routes, router]
    residual, normed, scaled, *pieces = call(kernel, "settle", inputs, outputs, 10_000_000_000)
    return residual, normed, scaled, pieces


def choose(step, block, routes, router, sizes, ready):
    ring, top, capacity = sizes
    width = block.shape[1]

    def kernel(block_ref, routes_ref, router_ref, scaled_ref, *outs):
        pick_rows(step, ring, top, block_ref[...], routes_ref, router_ref, scaled_ref, outs)

    outputs = [((PLANE * capacity, block.shape[0]), jnp.bfloat16)]
    outputs += [((capacity, width), jnp.bfloat16)] * PLANE
    inputs = [block, routes, router]
    scaled, *pieces = call(kernel, "choose", inputs, outputs, 70_000_000, ready=ready)
    return scaled, pieces


def join_arrived(arrived, capacity, ready):
    def kernel(*refs):
        joined_ref = refs[PLANE]
        for d, ref in enumerate(refs[:PLANE]):
            joined_ref[d * capacity : (d + 1) * capacity, :] = ref[:capacity, :]

    outputs = [((PLANE * capacity, arrived[0].shape[1]), jnp.bfloat16)]
    return call(kernel, "join_arrived", arrived, outputs, 0, ready=ready)[0]


def blend(own, others, pieces, ready):
    capacity = own.shape[0] // PLANE
    first = pieces[0].shape[0] if pieces else 0
    inputs = [own, *others, *pieces]

    def kernel(*refs):
        outs = refs[len(inputs) :]
        total = refs[0][...]
        for ref in refs[1 : 1 + len(others)]:
            total = total + ref[...].astype(jnp.float32)
        total = total.astype(jnp.bfloat16)
        for d, out in enumerate(outs):
            if pieces:
                out[:first, :] = refs[1 + len(others) + d][...]
            out[first:, :] = total[d * capacity : (d + 1) * capacity]

    outputs = [((first + capacity, own.shape[1]), jnp.bfloat16)] * PLANE
    return call(kernel, "blend", inputs, outputs, 1_000_000, ready=ready)


def expert_apply(pieces, kept, gate_part, up_part, down_part):
    total = sum(piece.shape[0] for piece in pieces)
    units, width = gate_part.shape

    def kernel(*refs):
        row_refs = refs[: len(pieces)]
        gate_ref, up_ref, down_ref, own_ref, other_ref, flag_ref = refs[len(pieces) :]
        flag_ref[...] = jnp.zeros_like(flag_ref)
        rows = jnp.concatenate([ref[...] for ref in row_refs], axis=0)
        gate_vals = dot_t(rows, gate_ref[...])
        up_vals = dot_t(rows, up_ref[...])
        hidden = (jax.nn.silu(gate_vals) * up_vals).astype(jnp.bfloat16)
        partial = dot_f(hidden, down_ref[...])
        own_ref[...] = partial[:kept]
        other_ref[...] = partial[kept:].astype(jnp.bfloat16)

    outputs = [
        ((kept, width), jnp.float32),
        ((total - kept, width), jnp.bfloat16),
        ((8, 128), jnp.float32),
    ]
    inputs = [*pieces, gate_part, up_part, down_part]
    return call(kernel, "experts", inputs, outputs, 6 * total * width * units, limit=20)


def scatter_sum(scaled_ref, piece_refs, running_ref):
    size = scaled_ref.shape[0] // PLANE
    parts = [ref[ref.shape[0] - size :, :] for ref in piece_refs]
    returned = jnp.concatenate(parts, axis=0)
    total = lax.dot_general(
        scaled_ref[...], returned, (((0,), (0,)), ((), ())), preferred_element_type=jnp.float32
    )
    if running_ref is not None:
        total = total + running_ref[...].astype(jnp.float32)
    return total


def collect(scaled, pieces, running):
    extra = [] if running is None else [running]

    def kernel(scaled_ref, *refs):
        running_ref = refs[len(pieces)] if extra else None
        total = scatter_sum(scaled_ref, refs[: len(pieces)], running_ref)
        refs[-1][...] = total.astype(jnp.bfloat16)

    shape = (scaled.shape[1], pieces[0].shape[1])
    inputs = [scaled, *pieces, *extra]
    return call(kernel, "collect", inputs, [(shape, jnp.bfloat16)], 35_000_000)[0]


def conclude(scaled, pieces, running, residual, gain):
    extra = [] if running is None else [running]

    def kernel(residual_ref, gain_ref, scaled_ref, *refs):
        running_ref = refs[len(pieces)] if extra else None
        total = scatter_sum(scaled_ref, refs[: len(pieces)], running_ref)
        layer = (residual_ref[...].astype(jnp.float32) + total).astype(jnp.bfloat16)
        refs[-2][...] = layer
        refs[-1][...] = norm_rows(layer, gain_ref[...])

    inputs = [residual, gain, scaled, *pieces, *extra]
    return call(kernel, "conclude", inputs, [(residual.shape, jnp.bfloat16)] * 2, 35_000_000)


def project(shares, order, query_weight, latent_rows, layer_rows):
    def kernel(order_ref, query_ref, latent_ref, layer_ref, *refs):
        share_refs = refs[: len(shares)]
        queries_ref, latents_ref, copy_ref = refs[len(shares) :]
        copy_ref[...] = layer_ref[...]
        rows = jnp.concatenate([ref[...] for ref in share_refs], axis=0)
        rows = lax.dot_general(
            order_ref[...], rows, (((0,), (0,)), ((), ())), preferred_element_type=jnp.float32
        ).astype(jnp.bfloat16)
        latents_ref[...] = dot_t(latent_ref[...], rows).astype(jnp.bfloat16)
        queries_ref[...] = dot_f(rows, query_ref[...]).astype(jnp.bfloat16)

    tokens = order.shape[0]
    outputs = [
        ((tokens, query_weight.shape[1]), jnp.bfloat16),
        ((latent_rows.shape[0], tokens), jnp.bfloat16),
        (layer_rows.shape, jnp.bfloat16),
    ]
    inputs = [order, query_weight, latent_rows, layer_rows, *shares]
    return call(kernel, "project", inputs, outputs, 1_000_000_000, limit=16)


def per_device(
    hidden_in,
    queries,
    suffix_latent,
    prefix_latent,
    key_up,
    value_up,
    output_weight,
    norm_gain,
    router,
    expert_gate,
    expert_up,
    expert_down,
    next_gain,
    next_query_weight,
    next_latent_weight,
    suffix_lengths,
    request_tenant,
    tenant_lengths,
    page_table,
    routes,
):
    tok_slice = hidden_in.shape[0]
    groups = lax.axis_size("group")
    ring = lax.axis_size("tensor") // PLANE
    tok_quarter = tok_slice // groups
    expert_count = router.shape[1]
    top_count = routes.shape[2]
    capacity = max(2, 4 * tok_quarter * top_count // (3 * expert_count))
    capacity = -(-capacity // 16) * 16

    real_rows = prefix_latent.shape[0]
    piece_rows = -(-real_rows // 16) * 16
    piece = prefix_latent
    if piece_rows != real_rows:
        piece = jnp.pad(piece, ((0, piece_rows - real_rows), (0, 0)))
    routes_columns = jnp.transpose(routes, (2, 0, 1))
    full, lite = join_share(piece, suffix_latent.T, routes_columns, tok_quarter)
    along = [send_round(full, PLANE)] + [send_round(lite, PLANE * k) for k in range(2, ring)]
    near_segments = []
    far_segments = []
    for k in range(ring):
        near_segments.append((k, piece_rows, real_rows, 0))
        far_segments.append((k, piece_rows, real_rows, 0))
        if k < 2:
            near_segments.append((k, tok_quarter, 0, 1))
    far_segments.append((0, tok_quarter, 0, 2))
    prefix_rows = ring * piece_rows
    first_rows = (prefix_rows - tok_quarter) // 2
    diagonal = segment_rows(3, far_segments)
    sides = (
        segment_rows(0, near_segments),
        segment_rows(1, far_segments) + segment_rows(2, far_segments),
        diagonal[:first_rows] + diagonal[prefix_rows:] + diagonal[first_rows:prefix_rows],
    )
    tables = [key_table(groups, side) for side in sides]
    tokens_info, permutation, near_spots, mid_spots, far_spots = make_plan(
        jnp.asarray(np.concatenate(tables, axis=1)),
        [part.shape[1] for part in tables],
        suffix_lengths,
        request_tenant,
        tenant_lengths,
        page_table[None, :],
        ring,
        real_rows,
        (tok_slice, tok_quarter, groups),
        [full],
    )

    column, plane, routes_ring = join_column(
        [full, *along], piece_rows, tok_quarter, [near_spots]
    )
    plane = [send_plane(part, d + 1) for d, part in enumerate(plane)]
    near_blocks = [send_group(column, j) if j else column for j in range(groups)]

    *near, near_flag = attend_near(
        tokens_info, near_spots, permutation, queries, key_up, near_blocks
    )
    beside = pass_on(plane, [near_flag])
    first, second = halves(beside[1], beside[0], first_rows, prefix_rows)
    across = [send_plane(first, 1), send_plane(second, 2)]
    mid_blocks = [send_group(block, j) if j else block for j in range(groups) for block in beside]
    *mid, mid_flag = attend_mid(tokens_info, mid_spots, near, mid_blocks)
    near = [near[0], *mid]
    across = pass_on(across, [mid_flag])
    far_blocks = [send_group(block, j) if j else block for j in range(groups) for block in across]
    attend_own, attend_other = attend_far(
        tokens_info, far_spots, near, value_up, output_weight, far_blocks, tok_quarter
    )

    hidden_own = dot_f(permutation[:tok_quarter], hidden_in).astype(jnp.bfloat16)
    others = [
        send_group(attend_other[(j - 1) * tok_quarter : j * tok_quarter], j)
        for j in range(1, groups)
    ]
    sizes = (ring, top_count, capacity)
    experts_columns = router.T
    residual, block, scaled, pieces = settle(
        hidden_own,
        attend_own,
        others,
        norm_gain[None, :],
        routes_ring,
        experts_columns,
        sizes,
    )

    kept = PLANE * capacity
    gate_part = jnp.transpose(expert_gate, (0, 2, 1))[0]
    up_part = jnp.transpose(expert_up, (0, 2, 1))[0]
    down_part = expert_down[0]
    scales = [scaled]
    results = []
    running = None
    payload = pieces
    for step in range(1, ring + 4):
        if step <= ring - 1:
            block = send_ring(block, ring)
        arrived = send_pieces(payload)
        if 4 <= step:
            k = step - 3
            if k < ring:
                landed = running
                total = collect(scales[k], arrived, running)
                running = send_ring(total, ring)
            else:
                break
        payload = []
        back = step - 2 if step - 2 < ring else 0
        if step >= 3:
            own, other, _ = results[back]
            if back in (1, ring - 1):
                along_z = [block] if step <= ring - 1 else [landed] if step > 4 else []
                other = pass_on([other], arrived[1:] + along_z)[0]
            others = [
                send_group(other[(j - 1) * kept : j * kept], j) for j in range(1, groups)
            ]
        if step <= ring:
            ready = [results[step - 2][2]] if step >= 2 else []
            if step <= ring - 1:
                scaled, payload = choose(
                    step, block, routes_ring, experts_columns, sizes, ready
                )
                scales.append(scaled)
                ready = [scaled]
            joined = join_arrived(arrived, capacity, ready)
            rows = [send_group(joined, j) if j else joined for j in range(groups)]
            results.append(expert_apply(rows, kept, gate_part, up_part, down_part))
        if step >= 3:
            payload = blend(own, others, payload, [] if back else [total])
    layer_rows, normed_next = conclude(
        scales[0], arrived, running, residual, next_gain[None, :]
    )

    shares = [send_group(normed_next, j) if j else normed_next for j in range(groups)]
    next_queries, next_latent, layer_rows = project(
        shares, permutation, next_query_weight, next_latent_weight.T, layer_rows
    )
    return (layer_rows[:, None, :], next_queries, next_latent.T)


def solution(mesh):
    return jax.shard_map(
        per_device,
        mesh=mesh,
        in_specs=(
            P("tensor", None),
            P("tensor", "group"),
            P("tensor", None),
            P(("group", "tensor"), None),
            P("group", None, None),
            P("group", None, None),
            P("group", None),
            P(),
            P(),
            P("tensor", None, "group"),
            P("tensor", None, "group"),
            P("tensor", "group", None),
            P(),
            P(None, "group"),
            P(None, "group"),
            P(),
            P(),
            P(),
            P(),
            P(None, "tensor", None),
        ),
        out_specs=(P("tensor", "group", None), P("tensor", "group"), P("tensor", "group")),
        check_vma=False,
    )
```

```python
import functools
import math

import jax
import jax.numpy as jnp
import numpy as np
from jax import lax
from jax.experimental import pallas as pl
from jax.experimental.pallas import tpu as pltpu
from jax.sharding import PartitionSpec as P

NOPE = 128
ROPE = 64
LAT = 512
PAGE = 8
PLANE = 4
ROUTE_ROWS = 16
WIDE = 640

VERY_NEGATIVE = -1e30
ROUTE_SCALING = 2.446
NORM_EPSILON = 1e-06


def ring_order(count):
    odd = list(range(1, count, 2))
    even = list(range(2, count, 2))
    return [0] + odd + even[::-1]


def send_ring(block, count, steps=1):
    order = ring_order(count)
    after = {order[i]: order[(i + steps) % count] for i in range(count)}
    route = [
        (z * PLANE + p, after[z] * PLANE + p) for z in range(count) for p in range(PLANE)
    ]
    return lax.ppermute(block, "tensor", route)


def send_round(block, distance):
    count = lax.axis_size("tensor")
    return lax.ppermute(block, "tensor", [(i, (i + distance) % count) for i in range(count)])


def send_plane(block, distance):
    devices = range(lax.axis_size("tensor"))
    return lax.ppermute(block, "tensor", [(i, i ^ distance) for i in devices])


def send_pieces(pieces):
    sent = {d: send_plane(pieces[d], d) for d in reversed(range(1, PLANE))}
    return [pieces[0]] + [sent[d] for d in range(1, PLANE)]


def send_group(block, distance):
    devices = range(lax.axis_size("group"))
    return lax.ppermute(block, "group", [(i, i ^ distance) for i in devices])


def norm_rows(row_block, gain_vector):
    values = row_block.astype(jnp.float32)
    mean_square = jnp.mean(values * values, axis=-1, keepdims=True)
    return (
        values * lax.rsqrt(mean_square + NORM_EPSILON) * gain_vector.astype(jnp.float32)
    ).astype(jnp.bfloat16)


def dot_t(left, right):
    return lax.dot_general(
        left, right, (((1,), (1,)), ((), ())), preferred_element_type=jnp.float32
    )


def dot_f(left, right):
    return jnp.dot(left, right, preferred_element_type=jnp.float32)


def whole(array):
    return pl.BlockSpec(array.shape, lambda *i: (0,) * len(array.shape))


def after(kernel, count):
    def inner(*refs):
        kernel(*refs[count:])

    return inner


def resident(arrays):
    return [pl.BlockSpec(memory_space=pltpu.VMEM) for _ in arrays]


def unread(arrays):
    return [pl.BlockSpec(memory_space=pl.ANY) for _ in arrays]


def call(kernel, name, inputs, outputs, flops, limit=12, ready=(), streamed=False):
    shapes = [jax.ShapeDtypeStruct(shape, dtype) for shape, dtype in outputs]
    moved = sum(a.size * a.dtype.itemsize for a in list(inputs) + shapes)
    if streamed:
        places = {
            "grid": (1,),
            "in_specs": unread(ready) + [whole(a) for a in inputs],
            "out_specs": [whole(shape) for shape in shapes],
        }
    else:
        places = {
            "in_specs": unread(ready) + resident(inputs),
            "out_specs": resident(shapes),
        }
    return pl.pallas_call(
        after(kernel, len(ready)),
        **places,
        out_shape=shapes,
        compiler_params=pltpu.CompilerParams(vmem_limit_bytes=limit * 1024 * 1024),
        cost_estimate=pl.CostEstimate(flops=flops, bytes_accessed=moved, transcendentals=0),
        name=name,
    )(*ready, *inputs)


def join_share(piece, suffix_columns, routes_columns, tok_quarter):
    rows = piece.shape[0]
    tokens = suffix_columns.shape[1]
    top, groups, _ = routes_columns.shape

    def kernel(piece_ref, suffix_ref, routes_ref, full_ref, lite_ref):
        group_index = lax.axis_index("group")
        shape = (tok_quarter, tokens)
        row = lax.broadcasted_iota(jnp.int32, shape, 0)
        token = lax.broadcasted_iota(jnp.int32, shape, 1)
        select = jnp.where(token == group_index * tok_quarter + row, 1.0, 0.0)
        share = dot_t(select.astype(jnp.bfloat16), suffix_ref[...]).astype(jnp.bfloat16)
        named = jnp.zeros((top, tok_quarter), jnp.float32)
        for j in range(groups):
            part = routes_ref[:, j, :].astype(jnp.float32)
            named = jnp.where(group_index == j, part, named)
        named = jnp.concatenate([named, jnp.zeros((rows - top, tok_quarter), jnp.float32)], axis=0)
        spare = WIDE - LAT - ROPE - tok_quarter
        if spare:
            named = jnp.concatenate([named, jnp.zeros((rows, spare), jnp.float32)], axis=1)
        named = named.astype(jnp.bfloat16)
        piece = piece_ref[...]
        last = jnp.concatenate([piece[:, LAT:], named], axis=1)
        for ref in (full_ref, lite_ref):
            ref[:rows, :LAT] = piece[:, :LAT]
            ref[:rows, LAT:] = last
        empty = jnp.zeros((tok_quarter, WIDE - LAT - ROPE), jnp.bfloat16)
        full_ref[rows:, :LAT] = share[:, :LAT]
        full_ref[rows:, LAT:] = jnp.concatenate([share[:, LAT:], empty], axis=1)

    outputs = [((size, WIDE), piece.dtype) for size in (rows + tok_quarter, rows)]
    inputs = [piece, suffix_columns, routes_columns]
    return call(kernel, "join_share", inputs, outputs, 10_000_000, limit=58, streamed=True)


def join_column(blocks, rows, share, ready):
    count = len(blocks)

    def kernel(*refs):
        block_refs = refs[:count]
        near_ref, *far_refs, routes_ref = refs[count:]
        plane_index = lax.rem(lax.axis_index("tensor"), PLANE)
        at = 0
        for i, ref in enumerate(block_refs):
            near_ref[at : at + ref.shape[0], :] = ref[...]
            at += ref.shape[0]
            routes_ref[i] = ref[:ROUTE_ROWS, LAT:]
        here = block_refs[0][rows:, :].astype(jnp.float32)
        before = block_refs[1][rows:, :].astype(jnp.float32)
        for d, far_ref in enumerate(far_refs):
            for i, ref in enumerate(block_refs):
                far_ref[i * rows : (i + 1) * rows, :] = ref[:rows, :]
            later = plane_index < lax.bitwise_xor(plane_index, d + 1)
            part = jnp.where(later, here, before).astype(jnp.bfloat16)
            far_ref[far_ref.shape[0] - share :, :] = part

    dtype = blocks[0].dtype
    outputs = [((count * rows + 2 * share, WIDE), dtype)]
    outputs += [((count * rows + share, WIDE), dtype)] * (PLANE - 2)
    outputs.append(((count, ROUTE_ROWS, WIDE - LAT), dtype))
    near, *far, routes = call(kernel, "join_column", blocks, outputs, 0, ready=ready)
    return near, far, routes


def halves(by_y, by_x, first, prefix):
    share = by_y.shape[0] - prefix

    def kernel(by_y_ref, by_x_ref, first_ref, second_ref):
        first_ref[:first, :] = by_y_ref[:first, :]
        first_ref[first:, :] = by_y_ref[prefix:, :]
        second_ref[...] = by_x_ref[first:prefix, :]

    outputs = [((first + share, WIDE), by_y.dtype), ((prefix - first, WIDE), by_y.dtype)]
    return call(kernel, "halves", [by_y, by_x], outputs, 0)


def pass_on(blocks, ready):
    first = len(ready)

    def kernel(*refs):
        pass

    return pl.pallas_call(
        kernel,
        in_specs=unread(ready) + unread(blocks),
        out_specs=unread(blocks),
        out_shape=[jax.ShapeDtypeStruct(block.shape, block.dtype) for block in blocks],
        input_output_aliases={first + i: i for i in range(len(blocks))},
        compiler_params=pltpu.CompilerParams(vmem_limit_bytes=1024 * 1024),
        name="pass_on",
    )(*ready, *blocks)


LATER = 1 << 20


def segment_rows(d, segments):
    return [(d, k, r, s, r < real) for k, count, real, s in segments for r in range(count)]


def key_table(groups, side):
    rows = [(j, *row) for j in range(groups) for row in side]
    table = np.zeros((8, len(rows)), np.int32)
    table[:6] = np.array(rows, np.int32).T
    table[6] = table[3] // PAGE
    table[7] = table[3] % PAGE
    return table


def make_plan(table, counts, lengths, tenants, tenant_lengths, page_table, ring, piece_rows, sizes, ready):
    tok_slice, tok_quarter, groups = sizes
    requests = lengths.shape[0]
    tenant_count = tenant_lengths.shape[0]
    pages = page_table.shape[1]
    piece_pages = piece_rows // PAGE

    def spots_of(part, page_row, group_index, ring_index, plane_index):
        j, d, k, r, suffix, real, page_at, within = (part[i : i + 1, :] for i in range(8))
        in_plane = lax.bitwise_xor(plane_index, d)
        k = jnp.where(suffix == 2, jnp.where(in_plane < plane_index, 0, 1), k)
        from_ring = ring_index - k
        from_ring = jnp.where(from_ring < 0, from_ring + ring, from_ring)
        of_group = lax.bitwise_xor(group_index, j)
        owner = (of_group * ring + from_ring) * PLANE + in_plane
        index = owner * piece_pages + page_at
        count = part.shape[1]
        page = lax.broadcasted_iota(jnp.int32, (pages, count), 0)
        hit = jnp.where(page == index, 1.0, 0.0).astype(jnp.bfloat16)
        found = dot_f(page_row, hit)[:1].astype(jnp.int32)
        logical = jnp.where(real > 0, found * PAGE + within, -1)
        token = (from_ring * PLANE + in_plane) * tok_slice + of_group * tok_quarter + r
        return jnp.where(suffix > 0, token + LATER, logical)

    def kernel(lengths_ref, tenants_ref, tenant_lengths_ref, page_ref, table_ref, *refs):
        info_ref, order_ref, *spot_refs = refs
        group_index = jnp.full((1, 1), lax.axis_index("group"), jnp.int32)
        tensor_index = lax.axis_index("tensor")
        ring_index = jnp.full((1, 1), lax.div(tensor_index, PLANE), jnp.int32)
        plane_index = jnp.full((1, 1), lax.rem(tensor_index, PLANE), jnp.int32)
        page_row = page_ref[...].astype(jnp.float32).astype(jnp.bfloat16)
        page_row = jnp.broadcast_to(page_row, (16, pages))
        at = 0
        for count, spot_ref in zip(counts, spot_refs):
            part = table_ref[:, at : at + count]
            spot_ref[...] = spots_of(part, page_row, group_index, ring_index, plane_index)
            at += count
        row = lax.broadcasted_iota(jnp.int32, (tok_slice, 1), 0)
        share = jnp.zeros((tok_slice, 1), jnp.int32)
        for j in range(1, groups):
            share = share + jnp.where(row >= j * tok_quarter, 1, 0)
        local = (row - share * tok_quarter) * groups + lax.bitwise_xor(group_index, share)
        column = lax.broadcasted_iota(jnp.int32, (tok_slice, tok_slice), 1)
        order_ref[...] = jnp.where(column == local, 1.0, 0.0).astype(jnp.bfloat16)
        position = local + tensor_index * tok_slice
        low = jnp.zeros((tok_slice, 1), jnp.int32)
        high = jnp.zeros((tok_slice, 1), jnp.int32)
        start = jnp.zeros((tok_slice, 1), jnp.int32)
        begin = 0
        for i in range(requests):
            end = begin + lengths_ref[i]
            inside = (position >= begin) & (position < end)
            tenant = tenants_ref[i]
            first = 0
            tenant_low = 0
            tenant_high = 0
            for t in range(tenant_count):
                last = first + tenant_lengths_ref[t]
                tenant_low = jnp.where(tenant == t, first, tenant_low)
                tenant_high = jnp.where(tenant == t, last, tenant_high)
                first = last
            start = jnp.where(inside, begin, start)
            low = jnp.where(inside, tenant_low, low)
            high = jnp.where(inside, tenant_high, high)
            begin = end
        for i, value in enumerate((low, high, start + LATER, position + LATER)):
            info_ref[:, i : i + 1] = value

    shapes = [
        jax.ShapeDtypeStruct((tok_slice, 4), jnp.int32),
        jax.ShapeDtypeStruct((tok_slice, tok_slice), jnp.bfloat16),
    ] + [jax.ShapeDtypeStruct((1, count), jnp.int32) for count in counts]
    scalar = pl.BlockSpec(memory_space=pltpu.SMEM)
    arrays = [page_table, table]
    return pl.pallas_call(
        after(kernel, len(ready)),
        in_specs=unread(ready) + [scalar, scalar, scalar] + resident(arrays),
        out_specs=resident(shapes),
        out_shape=shapes,
        compiler_params=pltpu.CompilerParams(vmem_limit_bytes=20 * 1024 * 1024),
        cost_estimate=pl.CostEstimate(
            flops=4_000_000_000, bytes_accessed=1_000_000, transcendentals=0
        ),
        name="make_plan",
    )(*ready, lengths, tenants, tenant_lengths, *arrays)


def place_keys(key_refs, spot_ref, token_ref, keys, bias):
    at = 0
    for ref in key_refs:
        rows = ref.shape[0]
        keys[at : at + rows, :] = ref[...]
        at += rows
    columns = token_ref[...]
    spots = spot_ref[...]
    low, high, start, here = (columns[:, i : i + 1] for i in range(4))
    seen = ((spots >= low) & (spots < high)) | ((spots >= start) & (spots <= here))
    bias[...] = jnp.where(seen, 0.0, VERY_NEGATIVE)


SCORE_FACTOR = math.log2(math.e) / math.sqrt(NOPE + ROPE)


def score_rows(queries, keys, bias, pair):
    scores = dot_t(queries, keys[...])
    rows, count = scores.shape
    return (scores.reshape(pair, rows // pair, count) + bias[...][None]).reshape(rows, count)


def near_kernel(block_count, pair, token_ref, spot_ref, order_ref, query_ref, key_up_ref, *refs):
    key_refs = refs[:block_count]
    wide_ref, best_ref, sum_ref, acc_ref, flag_ref, keys, bias = refs[block_count:]
    flag_ref[...] = jnp.zeros_like(flag_ref)
    tokens = query_ref.shape[0]
    place_keys(key_refs, spot_ref, token_ref, keys, bias)
    queries = dot_f(order_ref[...], query_ref[...]).astype(jnp.bfloat16)
    size = NOPE + ROPE
    empty = jnp.zeros((tokens, WIDE - LAT - ROPE), jnp.bfloat16)
    for first in range(0, key_up_ref.shape[0], pair):
        wide = []
        for h in range(first, first + pair):
            part = queries[:, h * size : (h + 1) * size]
            content = dot_f(part[:, :NOPE], key_up_ref[h]).astype(jnp.bfloat16)
            wide.append(jnp.concatenate([content, part[:, NOPE:], empty], axis=1))
        wide = jnp.concatenate(wide, axis=0)
        here = pl.ds(first * tokens, pair * tokens)
        wide_ref[here, :] = wide
        masked = score_rows(wide, keys, bias, pair)
        best = jnp.max(masked, axis=-1, keepdims=True)
        weights = jnp.exp2((masked - best) * SCORE_FACTOR)
        best_ref[here, :] = best
        sum_ref[here, :] = jnp.sum(weights, axis=-1, keepdims=True)
        acc_ref[here, :] = dot_f(weights.astype(jnp.bfloat16), keys[:, :LAT])


def attend_call(kernel, name, inputs, outputs, scratch, work, limit=24):
    shapes = [jax.ShapeDtypeStruct(shape, dtype) for shape, dtype in outputs]
    return pl.pallas_call(
        kernel,
        in_specs=resident(inputs),
        out_specs=resident(shapes),
        out_shape=shapes,
        scratch_shapes=scratch,
        compiler_params=pltpu.CompilerParams(vmem_limit_bytes=limit * 1024 * 1024),
        cost_estimate=pl.CostEstimate(
            flops=work, bytes_accessed=8_000_000, transcendentals=work // 2176
        ),
        name=name,
    )(*inputs)


def key_scratch(tokens, blocks):
    count = sum(block.shape[0] for block in blocks)
    return [pltpu.VMEM((count, WIDE), jnp.bfloat16), pltpu.VMEM((tokens, count), jnp.float32)]


def attend_near(tokens_info, spots, order, queries, key_up, blocks):
    tokens = queries.shape[0]
    heads = key_up.shape[0]
    rows = heads * tokens
    outputs = [
        ((rows, WIDE), jnp.bfloat16),
        ((rows, 1), jnp.float32),
        ((rows, 1), jnp.float32),
        ((rows, LAT), jnp.float32),
        ((8, 128), jnp.float32),
    ]
    return attend_call(
        functools.partial(near_kernel, len(blocks), min(8, heads)),
        "attend_near",
        [tokens_info, spots, order, queries, key_up, *blocks],
        outputs,
        key_scratch(tokens, blocks),
        2 * rows * spots.shape[1] * (LAT + ROPE + LAT),
    )


def add_keys(here, wide_ref, best_ref, sum_ref, acc_ref, keys, bias, pair):
    masked = score_rows(wide_ref[here, :], keys, bias, pair)
    before = best_ref[here, :]
    best = jnp.maximum(before, jnp.max(masked, axis=-1, keepdims=True))
    factor = jnp.exp2((before - best) * SCORE_FACTOR)
    weights = jnp.exp2((masked - best) * SCORE_FACTOR)
    weight_sum = sum_ref[here, :] * factor + jnp.sum(weights, axis=-1, keepdims=True)
    attended = acc_ref[here, :] * factor + dot_f(weights.astype(jnp.bfloat16), keys[:, :LAT])
    return best, weight_sum, attended


def mid_kernel(block_count, pair, token_ref, spot_ref, wide_ref, best_ref, sum_ref, acc_ref, *refs):
    key_refs = refs[:block_count]
    new_best_ref, new_sum_ref, new_acc_ref, flag_ref, keys, bias = refs[block_count:]
    flag_ref[...] = jnp.zeros_like(flag_ref)
    place_keys(key_refs, spot_ref, token_ref, keys, bias)
    rows = pair * token_ref.shape[0]
    for first in range(0, wide_ref.shape[0], rows):
        here = pl.ds(first, rows)
        new_best_ref[here, :], new_sum_ref[here, :], new_acc_ref[here, :] = add_keys(
            here, wide_ref, best_ref, sum_ref, acc_ref, keys, bias, pair
        )


def attend_mid(tokens_info, spots, near, blocks):
    tokens = tokens_info.shape[0]
    rows = near[0].shape[0]
    outputs = [
        ((rows, 1), jnp.float32),
        ((rows, 1), jnp.float32),
        ((rows, LAT), jnp.float32),
        ((8, 128), jnp.float32),
    ]
    return attend_call(
        functools.partial(mid_kernel, len(blocks), min(8, rows // tokens)),
        "attend_mid",
        [tokens_info, spots, *near, *blocks],
        outputs,
        key_scratch(tokens, blocks),
        2 * rows * spots.shape[1] * (LAT + ROPE + LAT),
    )


def far_kernel(
    block_count,
    pair,
    token_ref,
    spot_ref,
    wide_ref,
    best_ref,
    sum_ref,
    acc_ref,
    value_up_ref,
    output_ref,
    *refs,
):
    key_refs = refs[:block_count]
    own_ref, other_ref, keys, bias = refs[block_count:]
    tokens = token_ref.shape[0]
    rows = pair * tokens
    place_keys(key_refs, spot_ref, token_ref, keys, bias)
    heads = []
    for first in range(0, wide_ref.shape[0], rows):
        _, weight_sum, attended = add_keys(
            pl.ds(first, rows), wide_ref, best_ref, sum_ref, acc_ref, keys, bias, pair
        )
        attended = (attended / weight_sum).astype(jnp.bfloat16)
        for h in range(pair):
            part = attended[h * tokens : (h + 1) * tokens]
            value = value_up_ref[first // tokens + h]
            heads.append(dot_f(part, value).astype(jnp.bfloat16))
    total = dot_f(jnp.concatenate(heads, axis=1), output_ref[...])
    mine = own_ref.shape[0]
    own_ref[...] = total[:mine]
    other_ref[...] = total[mine:].astype(jnp.bfloat16)


def attend_far(tokens_info, spots, near, value_up, output_weight, blocks, tok_quarter):
    tokens = tokens_info.shape[0]
    heads = value_up.shape[0]
    width = output_weight.shape[1]
    outputs = [
        ((tok_quarter, width), jnp.float32),
        ((tokens - tok_quarter, width), jnp.bfloat16),
    ]
    return attend_call(
        functools.partial(far_kernel, len(blocks), min(4, heads)),
        "attend_far",
        [tokens_info, spots, *near, value_up, output_weight, *blocks],
        outputs,
        key_scratch(tokens, blocks),
        2 * heads * tokens * spots.shape[1] * (LAT + ROPE + LAT),
    )


def pick_rows(turn, ring, top, block, routes_ref, router_ref, scaled_ref, outs):
    tokens = block.shape[0]
    capacity = outs[0].shape[0]
    tensor_index = lax.axis_index("tensor")
    here = lax.div(tensor_index, PLANE)
    plane_index = lax.rem(tensor_index, PLANE)
    order = ring_order(ring)
    place = sum(jnp.where(here == z, i, 0) for i, z in enumerate(order))
    place = lax.rem(place - turn + ring, ring)
    source = sum(jnp.where(place == i, z, 0) for i, z in enumerate(order))
    routes = routes_ref[lax.rem(here - source + ring, ring)].astype(jnp.float32)
    routes = routes[:, ROPE : ROPE + tokens]
    targets = [
        (here * PLANE + lax.bitwise_xor(plane_index, d)).astype(jnp.float32)
        for d in range(PLANE)
    ]
    hits = [
        jnp.sum(jnp.where(routes[:top] == target, 1.0, 0.0), axis=0, keepdims=True)
        for target in targets
    ]
    before = lax.broadcasted_iota(jnp.int32, (tokens, tokens), 0)
    after_it = lax.broadcasted_iota(jnp.int32, (tokens, tokens), 1)
    earlier = jnp.where(before < after_it, 1.0, 0.0).astype(jnp.bfloat16)
    ranks = dot_f(jnp.concatenate(hits, axis=0).astype(jnp.bfloat16), earlier)
    count = router_ref.shape[0]
    expert = lax.broadcasted_iota(jnp.int32, (count, tokens), 0).astype(jnp.float32)
    named = jnp.zeros((count, tokens), jnp.float32)
    for i in range(top):
        named = named + jnp.where(expert == routes[i : i + 1], 1.0, 0.0)
    picked = jax.nn.sigmoid(dot_t(router_ref[...], block)) * named
    gates = picked / jnp.sum(picked, axis=0, keepdims=True) * ROUTE_SCALING
    slot = lax.broadcasted_iota(jnp.int32, (capacity, tokens), 0).astype(jnp.float32)
    for d, out in enumerate(outs):
        taken = jnp.where(slot == ranks[d : d + 1], hits[d], 0.0)
        out[...] = dot_f(taken.astype(jnp.bfloat16), block).astype(jnp.bfloat16)
        gate = jnp.sum(jnp.where(expert == targets[d], gates, 0.0), axis=0, keepdims=True)
        scaled_ref[d * capacity : (d + 1) * capacity, :] = (taken * gate).astype(jnp.bfloat16)


def pick_outputs(block, capacity):
    tokens, width = block.shape
    pieces = [((capacity, width), jnp.bfloat16)] * PLANE
    return [((PLANE * capacity, tokens), jnp.bfloat16)] + pieces


def settle(hidden, own, others, gain, routes, router, sizes):
    ring, top, capacity = sizes

    def kernel(*refs):
        hidden_ref, own_ref = refs[:2]
        other_refs = refs[2 : 2 + len(others)]
        gain_ref, routes_ref, router_ref = refs[2 + len(others) : 5 + len(others)]
        residual_ref, normed_ref, scaled_ref, *outs = refs[5 + len(others) :]
        total = own_ref[...]
        for ref in other_refs:
            total = total + ref[...].astype(jnp.float32)
        residual = (hidden_ref[...].astype(jnp.float32) + total).astype(jnp.bfloat16)
        residual_ref[...] = residual
        normed = norm_rows(residual, gain_ref[...])
        normed_ref[...] = normed
        pick_rows(0, ring, top, normed, routes_ref, router_ref, scaled_ref, outs)

    outputs = [(hidden.shape, jnp.bfloat16)] * 2 + pick_outputs(hidden, capacity)
    inputs = [hidden, own, *others, gain, routes, router]
    residual, normed, scaled, *pieces = call(kernel, "settle", inputs, outputs, 10_000_000_000)
    return residual, normed, scaled, pieces


def choose(step, block, routes, router, sizes, ready):
    ring, top, capacity = sizes
    width = block.shape[1]

    def kernel(block_ref, routes_ref, router_ref, scaled_ref, *outs):
        pick_rows(step, ring, top, block_ref[...], routes_ref, router_ref, scaled_ref, outs)

    outputs = [((PLANE * capacity, block.shape[0]), jnp.bfloat16)]
    outputs += [((capacity, width), jnp.bfloat16)] * PLANE
    inputs = [block, routes, router]
    scaled, *pieces = call(kernel, "choose", inputs, outputs, 70_000_000, ready=ready)
    return scaled, pieces


def join_arrived(arrived, capacity, ready):
    def kernel(*refs):
        joined_ref = refs[PLANE]
        for d, ref in enumerate(refs[:PLANE]):
            joined_ref[d * capacity : (d + 1) * capacity, :] = ref[:capacity, :]

    outputs = [((PLANE * capacity, arrived[0].shape[1]), jnp.bfloat16)]
    return call(kernel, "join_arrived", arrived, outputs, 0, ready=ready)[0]


def blend(own, others, pieces, ready):
    capacity = own.shape[0] // PLANE
    first = pieces[0].shape[0] if pieces else 0
    inputs = [own, *others, *pieces]

    def kernel(*refs):
        outs = refs[len(inputs) :]
        total = refs[0][...]
        for ref in refs[1 : 1 + len(others)]:
            total = total + ref[...].astype(jnp.float32)
        total = total.astype(jnp.bfloat16)
        for d, out in enumerate(outs):
            if pieces:
                out[:first, :] = refs[1 + len(others) + d][...]
            out[first:, :] = total[d * capacity : (d + 1) * capacity]

    outputs = [((first + capacity, own.shape[1]), jnp.bfloat16)] * PLANE
    return call(kernel, "blend", inputs, outputs, 1_000_000, ready=ready)


def expert_apply(pieces, kept, gate_part, up_part, down_part):
    total = sum(piece.shape[0] for piece in pieces)
    units, width = gate_part.shape

    def kernel(*refs):
        row_refs = refs[: len(pieces)]
        gate_ref, up_ref, down_ref, own_ref, other_ref, flag_ref = refs[len(pieces) :]
        flag_ref[...] = jnp.zeros_like(flag_ref)
        rows = jnp.concatenate([ref[...] for ref in row_refs], axis=0)
        gate_vals = dot_t(rows, gate_ref[...])
        up_vals = dot_t(rows, up_ref[...])
        hidden = (jax.nn.silu(gate_vals) * up_vals).astype(jnp.bfloat16)
        partial = dot_f(hidden, down_ref[...])
        own_ref[...] = partial[:kept]
        other_ref[...] = partial[kept:].astype(jnp.bfloat16)

    outputs = [
        ((kept, width), jnp.float32),
        ((total - kept, width), jnp.bfloat16),
        ((8, 128), jnp.float32),
    ]
    inputs = [*pieces, gate_part, up_part, down_part]
    return call(kernel, "experts", inputs, outputs, 6 * total * width * units, limit=20)


def scatter_sum(scaled_ref, piece_refs, running_ref):
    size = scaled_ref.shape[0] // PLANE
    parts = [ref[ref.shape[0] - size :, :] for ref in piece_refs]
    returned = jnp.concatenate(parts, axis=0)
    total = lax.dot_general(
        scaled_ref[...], returned, (((0,), (0,)), ((), ())), preferred_element_type=jnp.float32
    )
    if running_ref is not None:
        total = total + running_ref[...].astype(jnp.float32)
    return total


def collect(scaled, pieces, running):
    extra = [] if running is None else [running]

    def kernel(scaled_ref, *refs):
        running_ref = refs[len(pieces)] if extra else None
        total = scatter_sum(scaled_ref, refs[: len(pieces)], running_ref)
        refs[-1][...] = total.astype(jnp.bfloat16)

    shape = (scaled.shape[1], pieces[0].shape[1])
    inputs = [scaled, *pieces, *extra]
    return call(kernel, "collect", inputs, [(shape, jnp.bfloat16)], 35_000_000)[0]


def conclude(scaled, pieces, running, residual, gain):
    extra = [] if running is None else [running]

    def kernel(residual_ref, gain_ref, scaled_ref, *refs):
        running_ref = refs[len(pieces)] if extra else None
        total = scatter_sum(scaled_ref, refs[: len(pieces)], running_ref)
        layer = (residual_ref[...].astype(jnp.float32) + total).astype(jnp.bfloat16)
        refs[-2][...] = layer
        refs[-1][...] = norm_rows(layer, gain_ref[...])

    inputs = [residual, gain, scaled, *pieces, *extra]
    return call(kernel, "conclude", inputs, [(residual.shape, jnp.bfloat16)] * 2, 35_000_000)


def project(shares, order, query_weight, latent_rows, layer_rows):
    def kernel(order_ref, query_ref, latent_ref, layer_ref, *refs):
        share_refs = refs[: len(shares)]
        queries_ref, latents_ref, copy_ref = refs[len(shares) :]
        copy_ref[...] = layer_ref[...]
        rows = jnp.concatenate([ref[...] for ref in share_refs], axis=0)
        rows = lax.dot_general(
            order_ref[...], rows, (((0,), (0,)), ((), ())), preferred_element_type=jnp.float32
        ).astype(jnp.bfloat16)
        latents_ref[...] = dot_t(latent_ref[...], rows).astype(jnp.bfloat16)
        queries_ref[...] = dot_f(rows, query_ref[...]).astype(jnp.bfloat16)

    tokens = order.shape[0]
    outputs = [
        ((tokens, query_weight.shape[1]), jnp.bfloat16),
        ((latent_rows.shape[0], tokens), jnp.bfloat16),
        (layer_rows.shape, jnp.bfloat16),
    ]
    inputs = [order, query_weight, latent_rows, layer_rows, *shares]
    return call(kernel, "project", inputs, outputs, 1_000_000_000, limit=16)


def per_device(
    hidden_in,
    queries,
    suffix_latent,
    prefix_latent,
    key_up,
    value_up,
    output_weight,
    norm_gain,
    router,
    expert_gate,
    expert_up,
    expert_down,
    next_gain,
    next_query_weight,
    next_latent_weight,
    suffix_lengths,
    request_tenant,
    tenant_lengths,
    page_table,
    routes,
):
    tok_slice = hidden_in.shape[0]
    groups = lax.axis_size("group")
    ring = lax.axis_size("tensor") // PLANE
    tok_quarter = tok_slice // groups
    expert_count = router.shape[1]
    top_count = routes.shape[2]
    capacity = max(2, 4 * tok_quarter * top_count // (3 * expert_count))
    capacity = -(-capacity // 16) * 16

    real_rows = prefix_latent.shape[0]
    piece_rows = -(-real_rows // 16) * 16
    piece = prefix_latent
    if piece_rows != real_rows:
        piece = jnp.pad(piece, ((0, piece_rows - real_rows), (0, 0)))
    routes_columns = jnp.transpose(routes, (2, 0, 1))
    full, lite = join_share(piece, suffix_latent.T, routes_columns, tok_quarter)
    along = [send_round(full, PLANE)] + [send_round(lite, PLANE * k) for k in range(2, ring)]
    near_segments = []
    far_segments = []
    for k in range(ring):
        near_segments.append((k, piece_rows, real_rows, 0))
        far_segments.append((k, piece_rows, real_rows, 0))
        if k < 2:
            near_segments.append((k, tok_quarter, 0, 1))
    far_segments.append((0, tok_quarter, 0, 2))
    prefix_rows = ring * piece_rows
    first_rows = (prefix_rows - tok_quarter) // 2
    diagonal = segment_rows(3, far_segments)
    sides = (
        segment_rows(0, near_segments),
        segment_rows(1, far_segments) + segment_rows(2, far_segments),
        diagonal[:first_rows] + diagonal[prefix_rows:] + diagonal[first_rows:prefix_rows],
    )
    tables = [key_table(groups, side) for side in sides]
    tokens_info, permutation, near_spots, mid_spots, far_spots = make_plan(
        jnp.asarray(np.concatenate(tables, axis=1)),
        [part.shape[1] for part in tables],
        suffix_lengths,
        request_tenant,
        tenant_lengths,
        page_table[None, :],
        ring,
        real_rows,
        (tok_slice, tok_quarter, groups),
        [full],
    )

    column, plane, routes_ring = join_column(
        [full, *along], piece_rows, tok_quarter, [near_spots]
    )
    plane = [send_plane(part, d + 1) for d, part in enumerate(plane)]
    near_blocks = [send_group(column, j) if j else column for j in range(groups)]

    *near, near_flag = attend_near(
        tokens_info, near_spots, permutation, queries, key_up, near_blocks
    )
    beside = pass_on(plane, [near_flag])
    first, second = halves(beside[1], beside[0], first_rows, prefix_rows)
    across = [send_plane(first, 1), send_plane(second, 2)]
    mid_blocks = [send_group(block, j) if j else block for j in range(groups) for block in beside]
    *mid, mid_flag = attend_mid(tokens_info, mid_spots, near, mid_blocks)
    near = [near[0], *mid]
    across = pass_on(across, [mid_flag])
    far_blocks = [send_group(block, j) if j else block for j in range(groups) for block in across]
    attend_own, attend_other = attend_far(
        tokens_info, far_spots, near, value_up, output_weight, far_blocks, tok_quarter
    )

    hidden_own = dot_f(permutation[:tok_quarter], hidden_in).astype(jnp.bfloat16)
    others = [
        send_group(attend_other[(j - 1) * tok_quarter : j * tok_quarter], j)
        for j in range(1, groups)
    ]
    sizes = (ring, top_count, capacity)
    experts_columns = router.T
    residual, block, scaled, pieces = settle(
        hidden_own,
        attend_own,
        others,
        norm_gain[None, :],
        routes_ring,
        experts_columns,
        sizes,
    )

    kept = PLANE * capacity
    gate_part = jnp.transpose(expert_gate, (0, 2, 1))[0]
    up_part = jnp.transpose(expert_up, (0, 2, 1))[0]
    down_part = expert_down[0]
    scales = [scaled]
    results = []
    running = None
    payload = pieces
    for step in range(1, ring + 4):
        if step <= ring - 1:
            block = send_ring(block, ring)
        arrived = send_pieces(payload)
        if 4 <= step:
            k = step - 3
            if k < ring:
                landed = running
                total = collect(scales[k], arrived, running)
                running = send_ring(total, ring)
            else:
                break
        payload = []
        back = step - 2 if step - 2 < ring else 0
        if step >= 3:
            own, other, _ = results[back]
            if back in (1, ring - 1):
                along_z = [block] if step <= ring - 1 else [landed] if step > 4 else []
                other = pass_on([other], arrived[1:] + along_z)[0]
            others = [
                send_group(other[(j - 1) * kept : j * kept], j) for j in range(1, groups)
            ]
        if step <= ring:
            ready = [results[step - 2][2]] if step >= 2 else []
            if step <= ring - 1:
                scaled, payload = choose(
                    step, block, routes_ring, experts_columns, sizes, ready
                )
                scales.append(scaled)
                ready = [scaled]
            joined = join_arrived(arrived, capacity, ready)
            rows = [send_group(joined, j) if j else joined for j in range(groups)]
            results.append(expert_apply(rows, kept, gate_part, up_part, down_part))
        if step >= 3:
            payload = blend(own, others, payload, [] if back else [total])
    layer_rows, normed_next = conclude(
        scales[0], arrived, running, residual, next_gain[None, :]
    )

    shares = [send_group(normed_next, j) if j else normed_next for j in range(groups)]
    next_queries, next_latent, layer_rows = project(
        shares, permutation, next_query_weight, next_latent_weight.T, layer_rows
    )
    return (layer_rows[:, None, :], next_queries, next_latent.T)


def solution(mesh):
    return jax.shard_map(
        per_device,
        mesh=mesh,
        in_specs=(
            P("tensor", None),
            P("tensor", "group"),
            P("tensor", None),
            P(("group", "tensor"), None),
            P("group", None, None),
            P("group", None, None),
            P("group", None),
            P(),
            P(),
            P("tensor", None, "group"),
            P("tensor", None, "group"),
            P("tensor", "group", None),
            P(),
            P(None, "group"),
            P(None, "group"),
            P(),
            P(),
            P(),
            P(),
            P(None, "tensor", None),
        ),
        out_specs=(P("tensor", "group", None), P("tensor", "group"), P("tensor", "group")),
        check_vma=False,
    )
```
